32 devices in a mesh: rows: 16 (over z, y, x), branch: 2 (over core).
Axes of the slice: x: 2, y: 2, z: 4, core: 2. Of those that a mesh axis runs over, the one named last changes fastest.
Arguments:
- node_feats: bfloat16 [65536, 256], P('rows')
- edge_feats: bfloat16 [131072, 256], P('rows')
- cotangent: bfloat16 [65536, 256], P(('rows', 'branch')), may hold values from -6 to 6
- graph_ids: int32 [65536], P('rows'), may hold values from 0 to 16383, as said below
- node_mask: int32 [65536], P('rows'), may hold values from 0 to 1, as said below
- edge_src: int32 [131072], P('rows'), may hold values from 0 to 126, as said below
- edge_dst: int32 [131072], P('rows'), may hold values from 0 to 126, as said below
- edge_mask: int32 [131072], P('rows'), may hold values from 0 to 1, as said below
- weights: float32 [13, 65536], P(None, ('rows', 'branch'))
- weight_moment1: float32 [13, 65536], P(None, ('rows', 'branch')), may hold values from -0.0017089844 to 0.0017089844
- weight_moment2: float32 [13, 65536], P(None, ('rows', 'branch')), may hold values from 1.168836e-09 to 4.675344e-09
- vectors: float32 [14, 256], replicated
- vector_moment1: float32 [14, 256], replicated, may hold values from -0.0048828125 to 0.0048828125
- vector_moment2: float32 [14, 256], replicated, may hold values from 1.0519524e-08 to 4.2078096e-08
Outputs:
- layer_out: bfloat16 [65536, 256], P(('rows', 'branch'))
- node_grad: float32 [65536, 256], P(('rows', 'branch'))
- edge_grad: float32 [131072, 256], P(('rows', 'branch'))
- new_weights: float32 [13, 65536], P(None, ('rows', 'branch'))
- new_moment1: float32 [13, 65536], P(None, ('rows', 'branch'))
- new_moment2: float32 [13, 65536], P(None, ('rows', 'branch'))
- new_vectors: float32 [14, 256], replicated
- new_vector_moment1: float32 [14, 256], replicated
- new_vector_moment2: float32 [14, 256], replicated
- grad_norm: float32 [], replicated
The draws below stay inside these ranges and needn't reach their ends.
Inputs may be any that keep to these rules, and one draw needn't show every extreme that they name: `graph_ids`: graph ids of block b lie in 32 * b to 32 * b + 25 for used nodes; unused nodes of block b carry 32 * b + 31; a block's used nodes come first, molecules are consecutive runs of 1 to 50 nodes. `node_mask`: each block's used slots come first; from 40 to 127 used slots a block, the last block holding 128 - 1. `edge_src`: edges join used nodes of one molecule; unused edge slots hold 0. `edge_dst`: the target lies in the source's molecule. `edge_mask`: at most twice the block's used nodes, and at most 256, edge slots of a block are used, all among the first slots.
All inputs are finite; a program needn't handle non-finite values.
Results may differ from the reference program's by a relative error of at most 0.011.
Values may be sent and summed in bfloat16 or wider, within the bound.
No kernel may reach another device: no remote copies, remote signals or barrier semaphores. Data moves between devices by JAX's collectives and lax.ppermute only.
A program may use at most 192 MiB of HBM per device.

```python
import math
import jax
import jax.numpy as jnp
from jax import lax

H = 256
HEADS = 8
HD = 32
BLOCK = 128
EB = 256
MATS = 13
VECS = 14
STEP = 7
BLOCKS = 512
NODES = 65536
EDGES = 131072


def packing(key):
    block_ids = jnp.arange(BLOCKS, dtype=jnp.int32)
    jitter = jax.random.randint(jax.random.fold_in(key, 11), (BLOCKS,), 0, 9)
    live_count = jnp.minimum(BLOCK - 1, 40 + 88 * block_ids // max(BLOCKS - 1, 1) + jitter)
    mol_sizes = jax.random.randint(jax.random.fold_in(key, 12), (BLOCKS, 26), 5, 51)
    mol_ends = jnp.cumsum(mol_sizes, axis=1).astype(jnp.int32)
    positions = jnp.arange(BLOCK, dtype=jnp.int32)
    local_ids = jnp.sum((mol_ends[:, None, :] <= positions[None, :, None]).astype(jnp.int32), axis=2)
    is_live = positions[None, :] < live_count[:, None]
    mol_starts = jnp.concatenate([jnp.zeros((BLOCKS, 1), jnp.int32), mol_ends], axis=1)
    mol_first = jnp.take_along_axis(mol_starts, local_ids, axis=1)
    mol_last = jnp.minimum(jnp.take_along_axis(mol_starts, local_ids + 1, axis=1), live_count[:, None]) - 1
    graph_rows = jnp.where(is_live, block_ids[:, None] * 32 + local_ids, block_ids[:, None] * 32 + 31)
    slot_ids = jnp.arange(EB, dtype=jnp.int32)
    used_count = jnp.minimum(EB, 2 * live_count)
    spare_src = jax.random.randint(jax.random.fold_in(key, 13), (BLOCKS, EB), 0, BLOCK) % live_count[:, None]
    source = jnp.where(slot_ids[None, :] < live_count[:, None], slot_ids[None, :], spare_src)
    magnitude = jax.random.randint(jax.random.fold_in(key, 14), (BLOCKS, EB), 1, 3)
    direction = 2 * jax.random.randint(jax.random.fold_in(key, 15), (BLOCKS, EB), 0, 2) - 1
    offset_step = magnitude * direction
    last_node = (live_count - 1)[:, None]
    last_first = jnp.take_along_axis(mol_first, last_node, axis=1)
    forced = slot_ids[None, :] == live_count[:, None]
    source = jnp.where(forced, last_first, source)
    lower = jnp.take_along_axis(mol_first, source, axis=1)
    upper = jnp.take_along_axis(mol_last, source, axis=1)
    target = source + offset_step
    target = jnp.where((target < lower) | (target > upper), source - offset_step, target)
    target = jnp.clip(target, lower, upper)
    target = jnp.where(forced, last_node, target)
    slot_used = slot_ids[None, :] < used_count[:, None]
    kept_edge = jax.random.randint(jax.random.fold_in(key, 16), (BLOCKS, EB), 0, 10) > 0
    edge_on = (slot_used & kept_edge).astype(jnp.int32)
    source = jnp.where(slot_used, source, 0)
    target = jnp.where(slot_used, target, 0)
    return (graph_rows, is_live.astype(jnp.int32), source, target, edge_on)


def rising(count):
    return 0.6 + 1.2 * jnp.arange(count, dtype=jnp.float32) / max(count - 1, 1)


def draw_graph_ids(key, part):
    graph_rows, live_rows, source, target, edge_on = packing(key)
    return graph_rows.reshape(NODES).astype(jnp.int32)


def draw_node_mask(key, part):
    graph_rows, live_rows, source, target, edge_on = packing(key)
    return live_rows.reshape(NODES).astype(jnp.int32)


def draw_edge_src(key, part):
    graph_rows, live_rows, source, target, edge_on = packing(key)
    return source.reshape(EDGES).astype(jnp.int32)


def draw_edge_dst(key, part):
    graph_rows, live_rows, source, target, edge_on = packing(key)
    return target.reshape(EDGES).astype(jnp.int32)


def draw_edge_mask(key, part):
    graph_rows, live_rows, source, target, edge_on = packing(key)
    return edge_on.reshape(EDGES).astype(jnp.int32)


def draw_node_feats(key, part):
    key = jax.random.fold_in(key, 21)
    normal = jnp.clip(jax.random.normal(key, (NODES, H), jnp.float32), -5.0, 5.0)
    return (normal * rising(H)).astype(jnp.bfloat16)


def draw_edge_feats(key, part):
    key = jax.random.fold_in(key, 22)
    normal = jnp.clip(jax.random.normal(key, (EDGES, H), jnp.float32), -5.0, 5.0)
    return (normal * rising(H)).astype(jnp.bfloat16)


def draw_weights(key, part):
    key = jax.random.fold_in(key, 23)
    scales = jnp.array([0.7, 1.0, 1.0, 1.0, 1.0, 1.0, 1.0, 1.0, 3.0, 1.0, 1.0, 0.7, 0.7], jnp.float32)
    normal = jnp.clip(jax.random.normal(key, (MATS, H * H), jnp.float32), -5.0, 5.0)
    return normal * scales[:, None] * H ** (-0.5)


def draw_vectors(key, part):
    key = jax.random.fold_in(key, 24)
    kinds = jnp.array([0, 0, 0, 0, 0, 1, 0, 1, 0, 0, 0, 0, 1, 0], jnp.int32)[:, None]
    normal = jnp.clip(jax.random.normal(key, (VECS, H), jnp.float32), -4.0, 4.0)
    spread = jax.random.uniform(jax.random.fold_in(key, 5), (VECS, H), jnp.float32, 0.8, 1.2)
    return jnp.where(kinds == 1, rising(H)[None, :] * spread, 0.3 * normal)


def levels(own_key, extent, cuts, smallest, high):
    loudness = 1.0
    for position, shards_of in cuts:
        steps = jax.random.uniform(jax.random.fold_in(jax.random.fold_in(own_key, 6), position), (shards_of,), jnp.float32, smallest / len(cuts), high / len(cuts))
        loudness = loudness * jnp.repeat(jnp.exp(steps), extent[position] // shards_of).reshape((-1,) + (1,) * (len(extent) - 1 - position))
    return loudness


def centred(rng, extent, deviation, most, split=(), kind=jnp.bfloat16):
    entries = jax.random.normal(rng, extent, jnp.float32) * deviation
    if len(split) > 0:
        entries = levels(rng, extent, split, -0.22, 0.18) * entries
    return jnp.clip(entries, min=-most, max=most).astype(kind)


def setup_inputs(seed: int = 0) -> dict:
    arg_keys = jax.random.split(jax.random.key(seed), 15)
    node_feats = draw_node_feats(jax.random.fold_in(arg_keys[14], 71), 0)
    edge_feats = draw_edge_feats(jax.random.fold_in(arg_keys[14], 71), 0)
    cotangent = centred(arg_keys[2], (NODES, H), 1.0, 6.0, ((0, 32),))
    graph_ids = draw_graph_ids(jax.random.fold_in(arg_keys[14], 71), 0)
    node_mask = draw_node_mask(jax.random.fold_in(arg_keys[14], 71), 0)
    edge_src = draw_edge_src(jax.random.fold_in(arg_keys[14], 71), 0)
    edge_dst = draw_edge_dst(jax.random.fold_in(arg_keys[14], 71), 0)
    edge_mask = draw_edge_mask(jax.random.fold_in(arg_keys[14], 71), 0)
    weights = draw_weights(jax.random.fold_in(arg_keys[14], 71), 0)
    weight_moment1 = centred(arg_keys[9], (MATS, H * H), (0.11 / (MATS * H * H + VECS * H) ** 0.5), 0.0017089844, ((1, 32),), jnp.float32)
    weight_moment2 = jnp.clip(jnp.exp(math.log(4.675344111859658e-09) - 1.3862944 * jax.random.uniform(arg_keys[10], (MATS, H * H), jnp.float32) ** levels(arg_keys[10], (MATS, H * H), ((1, 32),), -0.2, 0.2)), 1.1688360279649146e-09, 4.675344111859658e-09)
    vectors = draw_vectors(jax.random.fold_in(arg_keys[14], 71), 0)
    vector_moment1 = centred(arg_keys[12], (VECS, H), (0.33 / (MATS * H * H + VECS * H) ** 0.5), 0.0048828125, (), jnp.float32)
    vector_moment2 = jnp.clip(jnp.exp(jax.random.uniform(arg_keys[13], (VECS, H), jnp.float32, math.log(1.0519523918617324e-08), math.log(4.2078095674469296e-08))), 1.0519523918617324e-08, 4.2078095674469296e-08)
    return dict(node_feats=node_feats, edge_feats=edge_feats, cotangent=cotangent, graph_ids=graph_ids, node_mask=node_mask, edge_src=edge_src, edge_dst=edge_dst, edge_mask=edge_mask, weights=weights, weight_moment1=weight_moment1, weight_moment2=weight_moment2, vectors=vectors, vector_moment1=vector_moment1, vector_moment2=vector_moment2)


@jax.custom_vjp
def low(v):
    return lax.optimization_barrier(v.astype(jnp.bfloat16)).astype(jnp.float32)

@jax.custom_vjp
def low_back(v):
    return v

def low_keep(v):
    return (low(v), None)

def low_pass(kept, grad):
    return (grad,)

def back_keep(v):
    return (v, None)

def back_low(kept, grad):
    return (low(grad),)
low.defvjp(low_keep, low_pass)
low_back.defvjp(back_keep, back_low)
eps_norm = 1e-05
clip_limit = 1.0
beta_one = 0.9
beta_two = 0.999
rate_mats = 0.1
rate_vecs = 0.8
decay_mats = 0.01
adam_eps = 1e-08
hidden_floor = -1000000000.0

def product(first_arg, second_arg):
    return jnp.dot(first_arg, second_arg, precision=lax.Precision.HIGHEST, preferred_element_type=jnp.float32)

def batch_norm(values, live_rows, gain, shift):
    live_count = jnp.sum(live_rows)
    mean_row = lax.optimization_barrier(jnp.sum(values * live_rows[:, None], axis=0)) / live_count
    second = lax.optimization_barrier(jnp.sum(values * values * live_rows[:, None], axis=0)) / live_count
    return gain * (values - mean_row) * lax.rsqrt(second - mean_row * mean_row + eps_norm) + shift

def gated_graph(node_in, edge_in, source, target, edge_live, matrices, vectors):
    node_count = node_in.shape[0]
    a_part = low_back(product(node_in, matrices[0])) + vectors[0]
    b_part = low_back(low(product(node_in, matrices[1])))
    d_part = low_back(low(product(node_in, matrices[3])))
    e_part = low_back(low(product(node_in, matrices[4])))
    gate_pre = low_back(product(edge_in, matrices[2]) + d_part[target] + e_part[source]) + vectors[1]
    opened = jax.nn.sigmoid(gate_pre) * edge_live[:, None]
    b_source = low_back(b_part[source])
    numerator = low_back(jax.ops.segment_sum(low(opened * b_source), target, num_segments=node_count))
    denominator = low_back(jax.ops.segment_sum(low(opened), target, num_segments=node_count))
    return node_in + jax.nn.silu(a_part + numerator / (denominator + 1.0))

def graph_attention(node_in, id_rows, matrices, vectors):
    node_count = node_in.shape[0]
    blocks = node_count // BLOCK
    queries = low_back(low(product(node_in, matrices[5]) + vectors[2])).reshape(blocks, BLOCK, HEADS, HD)
    keyed = low_back(low(product(node_in, matrices[6]))).reshape(blocks, BLOCK, HEADS, HD)
    valued = low_back(low(product(node_in, matrices[7]) + vectors[3])).reshape(blocks, BLOCK, HEADS, HD)
    raw_scores = jnp.einsum('bqhd,bkhd->bhqk', queries, keyed, precision=lax.Precision.HIGHEST)
    scores = low_back(raw_scores) * HD ** (-0.5)
    block_ids = id_rows.reshape(blocks, BLOCK)
    same_graph = block_ids[:, :, None] == block_ids[:, None, :]
    scores = jnp.where(same_graph[:, None], scores, hidden_floor)
    row_max = lax.optimization_barrier(jnp.max(scores, axis=-1, keepdims=True))
    expd = jnp.exp(scores - row_max)
    attn_probs = expd / lax.optimization_barrier(jnp.sum(expd, axis=-1, keepdims=True))
    attended = jnp.einsum('bhqk,bkhd->bqhd', low(attn_probs), valued, precision=lax.Precision.HIGHEST)
    attended = low_back(low(attended.reshape(node_count, H)))
    return node_in + low_back(product(attended, matrices[8])) + vectors[4]

def feed_forward(summed, matrices, vectors):
    w_inner = jnp.concatenate([matrices[9], matrices[10]], axis=1)
    w_outer = jnp.concatenate([matrices[11], matrices[12]], axis=0)
    b_inner = jnp.concatenate([vectors[9], vectors[10]])
    hidden = low_back(product(low(summed), w_inner) + b_inner)
    branch_term = low_back(product(low(jax.nn.silu(hidden)), w_outer))
    return summed + branch_term + vectors[11]

def layer(node_feats, edge_feats, weights, vectors, graph_ids, node_mask, edge_src, edge_dst, edge_mask):
    matrices = low(weights).reshape(MATS, H, H)
    group_blocks = math.gcd(BLOCKS, 16)
    groups = BLOCKS // group_blocks
    group_nodes = group_blocks * BLOCK
    group_edges = group_blocks * EB
    live_rows = node_mask.astype(jnp.float32)
    offsets = (jnp.arange(group_edges, dtype=jnp.int32) // EB * BLOCK).astype(jnp.int32)
    sources = (edge_src.reshape(groups, group_edges) + offsets).astype(jnp.int32)
    targets = (edge_dst.reshape(groups, group_edges) + offsets).astype(jnp.int32)
    edge_live = edge_mask.astype(jnp.float32).reshape(groups, group_edges)
    node_groups = node_feats.reshape(groups, group_nodes, H)
    edge_groups = edge_feats.reshape(groups, group_edges, H)

    def graph_part(pieces):
        return gated_graph(pieces[0], pieces[1], pieces[2], pieces[3], pieces[4], matrices, vectors)

    def attention_part(pieces):
        return graph_attention(pieces[0], pieces[1], matrices, vectors)

    def mlp_part(rows_in):
        return feed_forward(rows_in, matrices, vectors)
    local_out = lax.map(jax.checkpoint(graph_part), (node_groups, edge_groups, sources, targets, edge_live)).reshape(NODES, H)
    global_out = lax.map(jax.checkpoint(attention_part), (node_groups, graph_ids.reshape(groups, group_nodes))).reshape(NODES, H)
    local_norm = batch_norm(local_out, live_rows, vectors[5], vectors[6])
    global_norm = batch_norm(global_out, live_rows, vectors[7], vectors[8])
    summed = low_back(low(local_norm) + low(global_norm))
    mixed = lax.map(jax.checkpoint(mlp_part), summed.reshape(groups, group_nodes, H)).reshape(NODES, H)
    return batch_norm(mixed, live_rows, vectors[12], vectors[13]) * live_rows[:, None]

def adamw(params, gradient, moment_one, moment_two, rate, decay):
    first = beta_one * moment_one + (1.0 - beta_one) * gradient
    second = beta_two * moment_two + (1.0 - beta_two) * gradient * gradient
    first_hat = first / (1.0 - beta_one ** STEP)
    second_hat = second / (1.0 - beta_two ** STEP)
    updated = params - rate * (first_hat / (jnp.sqrt(second_hat) + adam_eps) + decay * params)
    return (updated, first, second)

def reference(node_feats, edge_feats, cotangent, graph_ids, node_mask, edge_src, edge_dst, edge_mask, weights, weight_moment1, weight_moment2, vectors, vector_moment1, vector_moment2):

    def bound(node_in, edge_in, weight_in, vector_in):
        return layer(node_in, edge_in, weight_in, vector_in, graph_ids, node_mask, edge_src, edge_dst, edge_mask)
    result, pullback = jax.vjp(bound, node_feats.astype(jnp.float32), edge_feats.astype(jnp.float32), weights, vectors)
    node_grad, edge_grad, weight_grad, vector_grad = pullback(cotangent.astype(jnp.float32))
    grad_norm = jnp.sqrt(jnp.sum(weight_grad * weight_grad) + jnp.sum(vector_grad * vector_grad))
    factor = jnp.minimum(1.0, clip_limit / (grad_norm + 1e-06))
    new_weights, first_w, second_w = adamw(weights, factor * weight_grad, weight_moment1, weight_moment2, rate_mats, decay_mats)
    new_vectors, first_v, second_v = adamw(vectors, factor * vector_grad, vector_moment1, vector_moment2, rate_vecs, 0.0)
    return (result.astype(jnp.bfloat16), node_grad, edge_grad, new_weights, first_w, second_w, new_vectors, first_v, second_v, grad_norm)
```

```python
import math

import jax
import jax.numpy as jnp
from jax import lax
from jax.sharding import PartitionSpec as P

HEADS = 8
BLOCK = 128
EB = 256
MATS = 13
STEP = 7


eps_norm = 1e-05
clip_limit = 1.0
beta_one = 0.9
beta_two = 0.999
rate_mats = 0.1
rate_vecs = 0.8
decay_mats = 0.01
adam_eps = 1e-08
hidden_floor = -1000000000.0


def matmul(first_arg, second_arg):
    return jnp.dot(first_arg, second_arg, preferred_element_type=jnp.float32)


def matmul_back(first_arg, second_arg):
    return lax.dot_general(
        first_arg, second_arg, (((1,), (1,)), ((), ())), preferred_element_type=jnp.float32
    )


def weight_term(inputs, gradient):
    return lax.dot_general(
        inputs, gradient, (((0,), (0,)), ((), ())), preferred_element_type=jnp.float32
    )


def to_low(values):
    return values.astype(jnp.bfloat16)


def swish_slope(values):
    sig_value = jax.nn.sigmoid(values)
    return sig_value * (1.0 + values * (1.0 - sig_value))


def pick_rows(node_table, onehot):
    return jnp.einsum("bep,bph->beh", onehot, node_table, preferred_element_type=jnp.float32)


def spread_rows(onehot, values):
    return jnp.einsum("bep,beh->bph", onehot, values, preferred_element_type=jnp.float32)


def group_count(blocks):
    return math.gcd(blocks, 4)


def lse_shape(blocks):
    group_size = group_count(blocks)
    return (blocks // group_size, group_size, HEADS, BLOCK)


def split_heads(values, group_size):
    row_total, feature_dim = values.shape
    return values.reshape(
        row_total // (group_size * BLOCK), group_size, BLOCK, HEADS, feature_dim // HEADS
    )


def masked_scores(queries, keyed, id_group, score_scale):
    raw_scores = jnp.einsum("gqhd,gkhd->ghqk", queries, keyed, preferred_element_type=jnp.float32)
    same_graph = id_group[:, :, None] == id_group[:, None, :]
    return jnp.where(same_graph[:, None], raw_scores * score_scale, hidden_floor)


def graph_front(node_low, edge_low, src_hot, dst_hot, edge_live, matrices, vectors):
    blocks, slot_count, places = src_hot.shape
    feature_dim = node_low.shape[1]
    a_part = matmul(node_low, matrices[0]) + vectors[0]
    b_part = to_low(matmul(node_low, matrices[1])).reshape(blocks, places, feature_dim)
    d_part = to_low(matmul(node_low, matrices[3])).reshape(blocks, places, feature_dim)
    e_part = to_low(matmul(node_low, matrices[4])).reshape(blocks, places, feature_dim)
    c_part = matmul(edge_low, matrices[2]).reshape(blocks, slot_count, feature_dim)
    gate_pre = c_part + pick_rows(d_part, dst_hot) + pick_rows(e_part, src_hot) + vectors[1]
    opened = jax.nn.sigmoid(gate_pre) * edge_live[:, :, None]
    b_source = pick_rows(b_part, src_hot)
    numerator = spread_rows(dst_hot, to_low(opened * b_source)).reshape(
        blocks * places, feature_dim
    )
    denominator = spread_rows(dst_hot, to_low(opened)).reshape(blocks * places, feature_dim)
    gated = a_part + numerator / (denominator + 1.0)
    return (gated, gate_pre, opened, b_source, numerator, denominator)


def graph_forward(operand):
    node_low, edge_low, src_hot, dst_hot, edge_live, id_rows, matrices, vectors = operand
    gated = graph_front(node_low, edge_low, src_hot, dst_hot, edge_live, matrices, vectors)[0]
    blocks = src_hot.shape[0]
    return (
        node_low.astype(jnp.float32) + jax.nn.silu(gated),
        jnp.zeros(lse_shape(blocks), jnp.float32),
    )


def attention_tables(node_low, matrices, vectors):
    queries = to_low(matmul(node_low, matrices[5]) + vectors[2])
    keyed = to_low(matmul(node_low, matrices[6]))
    valued = to_low(matmul(node_low, matrices[7]) + vectors[3])
    return (queries, keyed, valued)


def attention_forward(operand):
    node_low, edge_low, src_hot, dst_hot, edge_live, id_rows, matrices, vectors = operand
    row_count, feature_dim = node_low.shape
    blocks = row_count // BLOCK
    group_size = group_count(blocks)
    score_scale = (feature_dim // HEADS) ** (-0.5)
    queries, keyed, valued = attention_tables(node_low, matrices, vectors)
    id_groups = id_rows.reshape(blocks // group_size, group_size, BLOCK)

    def attend(pieces):
        scores = masked_scores(pieces[0], pieces[1], pieces[3], score_scale)
        row_max = jnp.max(scores, axis=-1, keepdims=True)
        log_total = row_max + jnp.log(jnp.sum(jnp.exp(scores - row_max), axis=-1, keepdims=True))
        attn_probs = to_low(jnp.exp(scores - log_total))
        attended = jnp.einsum(
            "ghqk,gkhd->gqhd", attn_probs, pieces[2], preferred_element_type=jnp.float32
        )
        return (to_low(attended), log_total[..., 0])

    attended, log_totals = lax.map(
        attend,
        (
            split_heads(queries, group_size),
            split_heads(keyed, group_size),
            split_heads(valued, group_size),
            id_groups,
        ),
    )
    attended_rows = attended.reshape(row_count, feature_dim)
    output = node_low.astype(jnp.float32) + matmul(attended_rows, matrices[8]) + vectors[4]
    return (output, log_totals)


def graph_back(operand):
    (
        grad_out,
        log_totals,
        node_low,
        edge_low,
        src_hot,
        dst_hot,
        edge_live,
        id_rows,
        matrices,
        vectors,
    ) = operand
    blocks, slot_count, places = src_hot.shape
    feature_dim = node_low.shape[1]
    gated, gate_pre, opened, b_source, numerator, denominator = graph_front(
        node_low, edge_low, src_hot, dst_hot, edge_live, matrices, vectors
    )
    d_gated = grad_out * swish_slope(gated)
    d_gated_low = to_low(d_gated)
    shifted = denominator + 1.0
    d_num = to_low(d_gated / shifted).reshape(blocks, places, feature_dim)
    d_den = to_low(-d_gated * numerator / (shifted * shifted)).reshape(blocks, places, feature_dim)
    d_message = pick_rows(d_num, dst_hot)
    d_open = d_message * b_source + pick_rows(d_den, dst_hot)
    d_source = to_low(d_message * opened)
    d_b_part = to_low(spread_rows(src_hot, d_source).reshape(blocks * places, feature_dim))
    sig_value = jax.nn.sigmoid(gate_pre)
    d_pre = d_open * edge_live[:, :, None] * sig_value * (1.0 - sig_value)
    d_pre_low = to_low(d_pre)
    d_d_part = to_low(spread_rows(dst_hot, d_pre_low).reshape(blocks * places, feature_dim))
    d_e_part = to_low(spread_rows(src_hot, d_pre_low).reshape(blocks * places, feature_dim))
    d_edges = d_pre_low.reshape(blocks * slot_count, feature_dim)
    node_grad = (
        grad_out + matmul_back(d_gated_low, matrices[0]) + matmul_back(d_b_part, matrices[1])
    )
    node_grad = node_grad + matmul_back(d_d_part, matrices[3]) + matmul_back(d_e_part, matrices[4])
    edge_grad = matmul_back(d_edges, matrices[2])
    own_grads = jnp.stack(
        [
            weight_term(node_low, d_gated_low),
            weight_term(node_low, d_b_part),
            weight_term(edge_low, d_edges),
            weight_term(node_low, d_d_part),
            weight_term(node_low, d_e_part),
        ]
    )
    mat_grads = jnp.concatenate(
        [own_grads, jnp.zeros((4, feature_dim, feature_dim), jnp.float32)], axis=0
    )
    zero_row = jnp.zeros((feature_dim,), jnp.float32)
    bias_grads = jnp.stack(
        [jnp.sum(d_gated, axis=0), jnp.sum(d_pre, axis=(0, 1)), zero_row, zero_row, zero_row]
    )
    return (node_grad, edge_grad, mat_grads, bias_grads)


def attention_back(operand):
    (
        grad_out,
        log_totals,
        node_low,
        edge_low,
        src_hot,
        dst_hot,
        edge_live,
        id_rows,
        matrices,
        vectors,
    ) = operand
    row_count, feature_dim = node_low.shape
    blocks = row_count // BLOCK
    group_size = group_count(blocks)
    score_scale = (feature_dim // HEADS) ** (-0.5)
    queries, keyed, valued = attention_tables(node_low, matrices, vectors)
    d_att_low = to_low(grad_out)
    d_attended = to_low(matmul_back(d_att_low, matrices[8]))
    id_groups = id_rows.reshape(blocks // group_size, group_size, BLOCK)

    def attend_back(pieces):
        q_group, k_group, v_group, id_group, lse_group, dmix_group = pieces
        scores = masked_scores(q_group, k_group, id_group, score_scale)
        attn_probs = jnp.exp(scores - lse_group[..., None])
        probs_low = to_low(attn_probs)
        attended = jnp.einsum(
            "ghqk,gkhd->gqhd", probs_low, v_group, preferred_element_type=jnp.float32
        )
        d_probs = jnp.einsum(
            "gqhd,gkhd->ghqk", dmix_group, v_group, preferred_element_type=jnp.float32
        )
        inner_sum = jnp.sum(attn_probs * d_probs, axis=-1, keepdims=True)
        d_scores = to_low(attn_probs * (d_probs - inner_sum) * score_scale)
        d_query = jnp.einsum(
            "ghqk,gkhd->gqhd", d_scores, k_group, preferred_element_type=jnp.float32
        )
        d_key = jnp.einsum("ghqk,gqhd->gkhd", d_scores, q_group, preferred_element_type=jnp.float32)
        d_value = jnp.einsum(
            "ghqk,gqhd->gkhd", probs_low, dmix_group, preferred_element_type=jnp.float32
        )
        return (to_low(attended), to_low(d_query), to_low(d_key), to_low(d_value))

    attended, d_query, d_key, d_value = lax.map(
        attend_back,
        (
            split_heads(queries, group_size),
            split_heads(keyed, group_size),
            split_heads(valued, group_size),
            id_groups,
            log_totals,
            split_heads(d_attended, group_size),
        ),
    )
    attended_rows = attended.reshape(row_count, feature_dim)
    d_q_low = d_query.reshape(row_count, feature_dim)
    d_k_low = d_key.reshape(row_count, feature_dim)
    d_v_low = d_value.reshape(row_count, feature_dim)
    node_grad = (
        grad_out
        + matmul_back(d_q_low, matrices[5])
        + matmul_back(d_k_low, matrices[6])
        + matmul_back(d_v_low, matrices[7])
    )
    edge_grad = jnp.zeros(edge_low.shape, jnp.float32)
    own_grads = jnp.stack(
        [
            weight_term(node_low, d_q_low),
            weight_term(node_low, d_k_low),
            weight_term(node_low, d_v_low),
            weight_term(attended_rows, d_att_low),
        ]
    )
    mat_grads = jnp.concatenate(
        [jnp.zeros((5, feature_dim, feature_dim), jnp.float32), own_grads], axis=0
    )
    zero_row = jnp.zeros((feature_dim,), jnp.float32)
    bias_grads = jnp.stack(
        [
            zero_row,
            zero_row,
            jnp.sum(d_q_low, axis=0, dtype=jnp.float32),
            jnp.sum(d_v_low, axis=0, dtype=jnp.float32),
            jnp.sum(grad_out, axis=0),
        ]
    )
    return (node_grad, edge_grad, mat_grads, bias_grads)


def adamw(params, gradient, moment_one, moment_two, rate, decay):
    first = beta_one * moment_one + (1.0 - beta_one) * gradient
    second = beta_two * moment_two + (1.0 - beta_two) * gradient * gradient
    first_hat = first / (1.0 - beta_one**STEP)
    second_hat = second / (1.0 - beta_two**STEP)
    updated = params - rate * (first_hat / (jnp.sqrt(second_hat) + adam_eps) + decay * params)
    return (updated, first, second)


axis_names = ("rows", "branch")


def swap_with(values, step, total):
    return lax.ppermute(values, axis_names, [(place, place ^ step) for place in range(total)])


def steps_of(total):
    return [1 << power for power in range(total.bit_length() - 1)]


def sum_small(values, total):
    for step in steps_of(total):
        values = values + swap_with(values, step, total)
    return values


def own_place():
    return lax.axis_index(axis_names)


def gather_matrices(shard, total):
    place = own_place()
    mats, width = shard.shape
    held = shard[None]
    for step in reversed(steps_of(total)):
        other = swap_with(held, step, total)
        upper = (place & step) != 0
        held = jnp.concatenate(
            [jnp.where(upper, other, held), jnp.where(upper, held, other)], axis=0
        )
    bits = total.bit_length() - 1
    held = held.reshape((2,) * bits + (mats, width))
    held = held.transpose((bits,) + tuple(reversed(range(bits))) + (bits + 1,))
    return held.reshape(mats, total * width)


def scatter_sum(grads, total):
    place = own_place()
    mats, width = grads.shape
    bits = total.bit_length() - 1
    held = grads.astype(jnp.bfloat16).reshape((mats,) + (2,) * bits + (width // total,))
    held = held.transpose(tuple(reversed(range(1, bits + 1))) + (0, bits + 1))
    for step in steps_of(total):
        mine = ((place & step) != 0).astype(jnp.int32)
        sent = lax.dynamic_index_in_dim(held, 1 - mine, 0, keepdims=False)
        kept = lax.dynamic_index_in_dim(held, mine, 0, keepdims=False)
        held = kept.astype(jnp.float32) + swap_with(sent, step, total).astype(jnp.float32)
        if step * 2 < total:
            held = held.astype(jnp.bfloat16)
    return held


def own_half(values, branch_index):
    half = values.shape[0] // 2
    return lax.dynamic_slice_in_dim(values, branch_index * half, half, 0)


def per_device(
    node_feats,
    edge_feats,
    cotangent,
    graph_ids,
    node_mask,
    edge_src,
    edge_dst,
    edge_mask,
    weights,
    weight_moment1,
    weight_moment2,
    vectors,
    vector_moment1,
    vector_moment2,
):
    total = lax.axis_size("rows") * lax.axis_size("branch")
    branch_index = lax.axis_index("branch")
    node_feats, edge_feats, graph_ids, node_mask, edge_src, edge_dst, edge_mask = [
        own_half(values, branch_index)
        for values in (
            node_feats, edge_feats, graph_ids, node_mask, edge_src, edge_dst, edge_mask
        )
    ]
    row_count, feature_dim = node_feats.shape
    blocks = row_count // BLOCK
    matrices = gather_matrices(weights.astype(jnp.bfloat16), total).reshape(
        MATS, feature_dim, feature_dim
    )
    live_rows = node_mask.astype(jnp.float32)[:, None]
    edge_live = edge_mask.astype(jnp.float32).reshape(blocks, EB)
    places = jnp.arange(BLOCK, dtype=jnp.int32)
    src_hot = (edge_src.reshape(blocks, EB)[:, :, None] == places).astype(jnp.bfloat16)
    dst_hot = (edge_dst.reshape(blocks, EB)[:, :, None] == places).astype(jnp.bfloat16)
    id_rows = graph_ids.reshape(blocks, BLOCK)
    operand = (node_feats, edge_feats, src_hot, dst_hot, edge_live, id_rows, matrices, vectors)
    local_in, _ = graph_forward(operand)
    global_in, log_totals = attention_forward(operand)
    count_row = jnp.broadcast_to(jnp.sum(live_rows), (feature_dim,))
    sums = sum_small(
        jnp.stack(
            [
                jnp.sum(live_rows * local_in, axis=0),
                jnp.sum(live_rows * local_in * local_in, axis=0),
                jnp.sum(live_rows * global_in, axis=0),
                jnp.sum(live_rows * global_in * global_in, axis=0),
                count_row,
            ]
        ),
        total,
    )
    live_count = sums[4, 0]

    def norm_of(values, first_sum, second_sum):
        mean = first_sum / live_count
        rstd = lax.rsqrt(second_sum / live_count - mean * mean + eps_norm)
        return ((values - mean) * rstd, rstd)

    local_hat, local_rstd = norm_of(local_in, sums[0], sums[1])
    global_hat, global_rstd = norm_of(global_in, sums[2], sums[3])
    summed = to_low(vectors[5] * local_hat + vectors[6]).astype(jnp.float32) + to_low(
        vectors[7] * global_hat + vectors[8]
    ).astype(jnp.float32)
    w_inner = jnp.concatenate([matrices[9], matrices[10]], axis=1)
    w_outer = jnp.concatenate([matrices[11], matrices[12]], axis=0)
    summed_low = to_low(summed)
    hidden = matmul(summed_low, w_inner) + jnp.concatenate([vectors[9], vectors[10]])
    hidden_low = to_low(jax.nn.silu(hidden))
    mixed_rows = summed + matmul(hidden_low, w_outer) + vectors[11]
    d_norm = live_rows * cotangent.astype(jnp.float32)
    out_sums = sum_small(
        jnp.stack(
            [
                jnp.sum(live_rows * mixed_rows, axis=0),
                jnp.sum(live_rows * mixed_rows * mixed_rows, axis=0),
                jnp.sum(d_norm, axis=0),
                jnp.sum(d_norm * mixed_rows, axis=0),
            ]
        ),
        total,
    )
    out_mean = out_sums[0] / live_count
    out_rstd = lax.rsqrt(out_sums[1] / live_count - out_mean * out_mean + eps_norm)
    out_hat = (mixed_rows - out_mean) * out_rstd
    layer_out = (live_rows * (vectors[12] * out_hat + vectors[13])).astype(jnp.bfloat16)
    dz_sum = out_sums[2]
    dz_hat = (out_sums[3] - out_mean * dz_sum) * out_rstd
    d_mixed = (
        vectors[12] * out_rstd * (d_norm - live_rows * (dz_sum + out_hat * dz_hat) / live_count)
    )
    d_mixed_low = to_low(d_mixed)
    d_hidden = to_low(matmul_back(d_mixed_low, w_outer) * swish_slope(hidden))
    d_summed = to_low(d_mixed + matmul_back(d_hidden, w_inner)).astype(jnp.float32)
    d_inner_bias = jnp.sum(d_hidden, axis=0, dtype=jnp.float32).reshape(2, feature_dim)
    back_sums = sum_small(
        jnp.stack(
            [
                jnp.sum(d_summed, axis=0),
                jnp.sum(d_summed * local_hat, axis=0),
                jnp.sum(d_summed * global_hat, axis=0),
                d_inner_bias[0],
                d_inner_bias[1],
                jnp.sum(d_mixed, axis=0),
            ]
        ),
        total,
    )
    inner_grad = weight_term(summed_low, d_hidden)
    outer_grad = weight_term(hidden_low, d_mixed_low)
    ffn_grads = jnp.stack(
        [
            inner_grad[:, :feature_dim],
            inner_grad[:, feature_dim:],
            outer_grad[:feature_dim],
            outer_grad[feature_dim:],
        ]
    )

    def norm_back(hat, rstd, gain, back_hat):
        return (
            gain
            * rstd
            * (d_summed - live_rows * (back_sums[0] + hat * back_hat) / live_count)
        )

    d_local = norm_back(local_hat, local_rstd, vectors[5], back_sums[1])
    d_global = norm_back(global_hat, global_rstd, vectors[7], back_sums[2])
    node_l, edge_grad, mats_l, bias_l = graph_back((d_local, log_totals) + operand)
    node_g, _, mats_g, bias_g = attention_back((d_global, log_totals) + operand)
    node_grad = node_l + node_g
    all_grads = jnp.concatenate([mats_l[:5], mats_g[5:], ffn_grads], axis=0).reshape(
        MATS, feature_dim * feature_dim
    )
    grad_shard = scatter_sum(all_grads, total)
    biases = bias_l + bias_g
    square_row = jnp.broadcast_to(jnp.sum(grad_shard * grad_shard), (1, feature_dim))
    tail_sums = sum_small(jnp.concatenate([biases, square_row], axis=0), total)
    vector_total = jnp.concatenate(
        [
            tail_sums[:5],
            back_sums[1:2],
            back_sums[0:1],
            back_sums[2:3],
            back_sums[0:1],
            back_sums[3:6],
            dz_hat[None],
            dz_sum[None],
        ],
        axis=0,
    )
    grad_norm = jnp.sqrt(tail_sums[5, 0] + jnp.sum(vector_total * vector_total))
    factor = jnp.minimum(1.0, clip_limit / (grad_norm + 1e-06))
    new_weights, first_w, second_w = adamw(
        weights, factor * grad_shard, weight_moment1, weight_moment2, rate_mats, decay_mats
    )
    new_vectors, first_v, second_v = adamw(
        vectors, factor * vector_total, vector_moment1, vector_moment2, rate_vecs, 0.0
    )
    return (
        layer_out,
        node_grad,
        edge_grad,
        new_weights,
        first_w,
        second_w,
        new_vectors,
        first_v,
        second_v,
        grad_norm,
    )


def solution(mesh):
    in_specs = (
        P("rows", None),
        P("rows", None),
        P(("rows", "branch"), None),
        P("rows"),
        P("rows"),
        P("rows"),
        P("rows"),
        P("rows"),
        P(None, ("rows", "branch")),
        P(None, ("rows", "branch")),
        P(None, ("rows", "branch")),
        P(),
        P(),
        P(),
    )
    out_specs = (
        P(("rows", "branch"), None),
        P(("rows", "branch"), None),
        P(("rows", "branch"), None),
        P(None, ("rows", "branch")),
        P(None, ("rows", "branch")),
        P(None, ("rows", "branch")),
        P(),
        P(),
        P(),
        P(),
    )
    return jax.shard_map(
        per_device, mesh=mesh, in_specs=in_specs, out_specs=out_specs, check_vma=False
    )
```

```python
import functools
import math

import jax
import jax.numpy as jnp
from jax import lax
from jax.experimental import pallas as pl
from jax.experimental.pallas import tpu as pltpu
from jax.sharding import PartitionSpec as P

HEADS = 8
BLOCK = 128
EB = 256
MATS = 13
STEP = 7
GROUP = 4

eps_norm = 1e-05
clip_limit = 1.0
beta_one = 0.9
beta_two = 0.999
rate_mats = 0.1
rate_vecs = 0.8
decay_mats = 0.01
adam_eps = 1e-08
hidden_floor = -1e30
axis_names = ("rows", "branch")
f32 = jnp.float32
bf16 = jnp.bfloat16


def mm(left, right):
    return jnp.dot(left, right, preferred_element_type=f32)


def mm_back(left, right):
    return lax.dot_general(left, right, (((1,), (1,)), ((), ())), preferred_element_type=f32)


def mm_rows(left, right):
    return lax.dot_general(left, right, (((0,), (0,)), ((), ())), preferred_element_type=f32)


def low(values):
    return values.astype(bf16)


def sig(values):
    return 0.5 * jnp.tanh(0.5 * values) + 0.5


def col_sum(values):
    return jnp.sum(values, axis=0, keepdims=True)


def live_of(info_ref, first_block, group, width):
    slot = lax.broadcasted_iota(jnp.int32, (BLOCK, width), 0)
    return jnp.concatenate(
        [
            jnp.where(slot < info_ref[1 + first_block + place], 1.0, 0.0)
            for place in range(group)
        ],
        axis=0,
    )


def add_rows(out_ref, rows):
    @pl.when(pl.program_id(0) == 0)
    def _():
        out_ref[...] = jnp.zeros_like(out_ref)

    for place, row in enumerate(rows):
        out_ref[place : place + 1, :] += row


def norm_terms(sums, first, count_row):
    mean = sums[first : first + 1] / count_row
    rstd = lax.rsqrt(sums[first + 1 : first + 2] / count_row - mean * mean + eps_norm)
    return (mean, rstd)


def prep_kernel(info_ref, src_ref, dst_ref, mask_ref, id_ref, hot_ref, turned_ref, bias_ref):
    for place in range(GROUP):
        row = pl.ds(place, 1)
        node = lax.broadcasted_iota(jnp.int32, (BLOCK, EB), 0)
        live = mask_ref[0, row, :] != 0
        dst_rows = jnp.where((node == dst_ref[0, row, :]) & live, 1.0, 0.0)
        src_rows = jnp.where((node == src_ref[0, row, :]) & live, 1.0, 0.0)
        turned = jnp.concatenate([dst_rows, src_rows], axis=0)
        turned_ref[place * EB : (place + 1) * EB, :] = low(turned)
        hot_ref[place * EB : (place + 1) * EB, :] = low(turned.T)
        ids = jnp.broadcast_to(id_ref[0, row, :].astype(f32), (BLOCK, BLOCK))
        bias_ref[place * BLOCK : (place + 1) * BLOCK, :] = jnp.where(
            ids == ids.T, 0.0, hidden_floor
        )


def local_kernel(
    info_ref, x_ref, e_ref, hot_ref, turned_ref, w_ref, vec_ref,
    out_ref, gated_ref, recip_ref, ratio_ref, open_ref, bsrc_ref, sums_ref,
):
    group = x_ref.shape[0] // BLOCK
    x = x_ref[...]
    a_part = mm(x, w_ref[0]) + vec_ref[0:1, :]
    b_part = low(mm(x, w_ref[1]))
    d_part = low(mm(x, w_ref[3]))
    e_part = low(mm(x, w_ref[4]))
    c_part = mm(e_ref[...], w_ref[2]) + vec_ref[1:2, :]
    nums = []
    dens = []
    for place in range(group):
        nodes = slice(place * BLOCK, (place + 1) * BLOCK)
        edges = slice(place * EB, (place + 1) * EB)
        hot = hot_ref[edges, :]
        gate = c_part[edges] + mm(hot, jnp.concatenate([d_part[nodes], e_part[nodes]], axis=0))
        opened = sig(gate)
        b_source = mm(hot[:, BLOCK:], b_part[nodes])
        open_ref[edges, :] = opened
        bsrc_ref[edges, :] = low(b_source)
        dst_turned = turned_ref[place * EB : place * EB + BLOCK, :]
        nums.append(mm(dst_turned, low(opened * b_source)))
        dens.append(mm(dst_turned, low(opened)))
    recip = 1.0 / (jnp.concatenate(dens, axis=0) + 1.0)
    ratio = jnp.concatenate(nums, axis=0) * recip
    gated = a_part + ratio
    out = x.astype(f32) + gated * sig(gated)
    gated_ref[...] = gated
    recip_ref[...] = recip
    ratio_ref[...] = ratio
    out_ref[...] = out
    live = live_of(info_ref, pl.program_id(0) * group, group, out.shape[1])
    kept = live * out
    add_rows(sums_ref, [col_sum(kept), col_sum(kept * out)])


def head_stack(values):
    head = lax.broadcasted_iota(jnp.int32, values.shape, 1) // (values.shape[1] // HEADS)
    wide = values.astype(f32)
    return jnp.concatenate(
        [low(jnp.where(head == place, wide, 0.0)) for place in range(HEADS)], axis=0
    )


def attend_kernel(
    info_ref, x_ref, bias_ref, w_ref, vec_ref,
    out_ref, q_ref, k_ref, v_ref, att_ref, prob_ref, sums_ref,
):
    group = x_ref.shape[0] // BLOCK
    x = x_ref[...]
    queries = low(mm(x, w_ref[5]) + vec_ref[2:3, :])
    keyed = low(mm(x, w_ref[6]))
    valued = low(mm(x, w_ref[7]) + vec_ref[3:4, :])
    q_ref[...] = queries
    k_ref[...] = keyed
    v_ref[...] = valued
    score_scale = (x.shape[1] // HEADS) ** (-0.5)
    for place in range(group):
        nodes = slice(place * BLOCK, (place + 1) * BLOCK)
        raw = mm_back(keyed[nodes], head_stack(queries[nodes]))
        bias = bias_ref[nodes, :]
        probs = []
        turned = []
        for head in range(HEADS):
            part = raw[:, head * BLOCK : (head + 1) * BLOCK] + bias
            part = jnp.exp((part - jnp.max(part, axis=0, keepdims=True)) * score_scale)
            part = part * (1.0 / jnp.sum(part, axis=0, keepdims=True))
            probs.append(low(part))
            turned.append(low(part.T))
        prob_ref[nodes, :] = jnp.concatenate(probs, axis=1)
        att_ref[nodes, :] = low(
            mm(jnp.concatenate(turned, axis=1), head_stack(valued[nodes]))
        )
    out = x.astype(f32) + mm(att_ref[...], w_ref[8]) + vec_ref[4:5, :]
    out_ref[...] = out
    live = live_of(info_ref, pl.program_id(0) * group, group, out.shape[1])
    kept = live * out
    add_rows(sums_ref, [col_sum(kept), col_sum(kept * out)])


def mix_kernel(
    info_ref, local_ref, global_ref, cot_ref, sums_ref, w_ref, vec_ref,
    low_ref, hidden_ref, mixed_ref, stat_ref,
):
    group = local_ref.shape[0] // BLOCK
    width = local_ref.shape[1]
    sums = sums_ref[...]
    count_row = sums[4:5]
    local_mean, local_rstd = norm_terms(sums, 0, count_row)
    global_mean, global_rstd = norm_terms(sums, 2, count_row)
    local_norm = (local_ref[...] - local_mean) * (vec_ref[5:6, :] * local_rstd) + vec_ref[6:7, :]
    global_norm = (global_ref[...] - global_mean) * (vec_ref[7:8, :] * global_rstd) + vec_ref[
        8:9, :
    ]
    summed = low(local_norm).astype(f32) + low(global_norm).astype(f32)
    summed_low = low(summed)
    low_ref[...] = summed_low
    mixed = summed + vec_ref[11:12, :]
    for half in range(2):
        hidden = mm(summed_low, w_ref[9 + half]) + vec_ref[9 + half : 10 + half, :]
        hidden_ref[:, half * width : (half + 1) * width] = hidden
        mixed = mixed + mm(low(hidden * sig(hidden)), w_ref[11 + half])
    mixed_ref[...] = mixed
    live = live_of(info_ref, pl.program_id(0) * group, group, width)
    kept = live * mixed
    d_norm = live * cot_ref[...].astype(f32)
    add_rows(
        stat_ref, [col_sum(kept), col_sum(kept * mixed), col_sum(d_norm), col_sum(d_norm * mixed)]
    )


def mix_back_kernel(
    info_ref, mixed_ref, hidden_ref, cot_ref, local_ref, global_ref, sums_ref, tops_ref, w_ref,
    vec_ref,
    layer_ref, dmix_ref, dhid_ref, hlow_ref, dsum_ref, stat_ref,
):
    group = mixed_ref.shape[0] // BLOCK
    width = mixed_ref.shape[1]
    sums = sums_ref[...]
    tops = tops_ref[...]
    count_row = sums[4:5]
    mean, rstd = norm_terms(tops, 0, count_row)
    live = live_of(info_ref, pl.program_id(0) * group, group, width)
    hat = (mixed_ref[...] - mean) * rstd
    layer_ref[...] = low(live * (vec_ref[12:13, :] * hat + vec_ref[13:14, :]))
    d_norm = live * cot_ref[...].astype(f32)
    dz_sum = tops[2:3]
    dz_hat = (tops[3:4] - mean * dz_sum) * rstd
    d_mixed = (vec_ref[12:13, :] * rstd) * (
        d_norm - live * (dz_sum / count_row + hat * (dz_hat / count_row))
    )
    d_mixed_low = low(d_mixed)
    dmix_ref[...] = d_mixed_low
    d_summed = d_mixed
    rows = []
    for half in range(2):
        cols = slice(half * width, (half + 1) * width)
        hidden = hidden_ref[:, cols]
        sig_value = sig(hidden)
        hlow_ref[:, cols] = low(hidden * sig_value)
        d_hidden = low(
            mm_back(d_mixed_low, w_ref[11 + half])
            * (sig_value * (1.0 + hidden * (1.0 - sig_value)))
        )
        dhid_ref[:, cols] = d_hidden
        rows.append(col_sum(d_hidden.astype(f32)))
        d_summed = d_summed + mm_back(d_hidden, w_ref[9 + half])
    d_low = low(d_summed)
    dsum_ref[...] = d_low
    d_sum = d_low.astype(f32)
    local_mean, local_rstd = norm_terms(sums, 0, count_row)
    global_mean, global_rstd = norm_terms(sums, 2, count_row)
    add_rows(
        stat_ref,
        [
            col_sum(d_sum),
            col_sum(d_sum * ((local_ref[...] - local_mean) * local_rstd)),
            col_sum(d_sum * ((global_ref[...] - global_mean) * global_rstd)),
            rows[0],
            rows[1],
            col_sum(d_mixed),
        ],
    )


def accumulate(acc_ref, terms):
    @pl.when(pl.program_id(0) == 0)
    def _():
        acc_ref[...] = jnp.zeros_like(acc_ref)

    for place, term in enumerate(terms):
        acc_ref[place] += term


def emit(acc_ref, out_ref):
    @pl.when(pl.program_id(0) == pl.num_programs(0) - 1)
    def _():
        out_ref[...] = low(acc_ref[...])


def mix_grad_kernel(slow_ref, dhid_ref, hlow_ref, dmix_ref, out_ref, acc_ref):
    width = slow_ref.shape[1]
    terms = []
    for half in range(2):
        terms.append(mm_rows(slow_ref[...], dhid_ref[:, half * width : (half + 1) * width]))
    for half in range(2):
        terms.append(mm_rows(hlow_ref[:, half * width : (half + 1) * width], dmix_ref[...]))
    accumulate(acc_ref, terms)
    emit(acc_ref, out_ref)


def norm_back(info_ref, dsum_ref, value_ref, sums, backs, first, gain_row, hat_row):
    group = value_ref.shape[0] // BLOCK
    count_row = sums[4:5]
    mean, rstd = norm_terms(sums, first, count_row)
    live = live_of(info_ref, pl.program_id(0) * group, group, value_ref.shape[1])
    hat = (value_ref[...] - mean) * rstd
    return (gain_row * rstd) * (
        dsum_ref[...].astype(f32)
        - live * (backs[0:1] / count_row + hat * (backs[hat_row : hat_row + 1] / count_row))
    )


def local_back_kernel(
    info_ref, dsum_ref, local_ref, gated_ref, recip_ref, ratio_ref, open_ref, bsrc_ref, hot_ref,
    turned_ref, x_ref, e_ref, sums_ref, backs_ref, vec_ref,
    dnode_ref, dedge_ref, stat_ref, out_ref, acc_ref,
):
    group = local_ref.shape[0] // BLOCK
    width = local_ref.shape[1]
    d_local = norm_back(
        info_ref, dsum_ref, local_ref, sums_ref[...], backs_ref[...], 0, vec_ref[5:6, :], 1
    )
    gated = gated_ref[...]
    sig_value = sig(gated)
    d_gated = d_local * (sig_value * (1.0 + gated * (1.0 - sig_value)))
    dnode_ref[:, :width] = low(d_gated)
    scaled = d_gated * recip_ref[...]
    d_num = low(scaled)
    d_den = low(-scaled * ratio_ref[...])
    pre_row = jnp.zeros((1, width), f32)
    for place in range(group):
        nodes = slice(place * BLOCK, (place + 1) * BLOCK)
        edges = slice(place * EB, (place + 1) * EB)
        hot_dst = hot_ref[edges, :BLOCK]
        d_message = mm(hot_dst, d_num[nodes])
        opened = open_ref[edges, :]
        d_open = d_message * bsrc_ref[edges, :].astype(f32) + mm(hot_dst, d_den[nodes])
        d_source = low(d_message * opened)
        d_pre = d_open * (opened * (1.0 - opened))
        d_pre_low = low(d_pre)
        pre_row = pre_row + col_sum(d_pre)
        dedge_ref[edges, :] = d_pre_low
        turned = turned_ref[edges, :]
        d_b = low(mm(turned[BLOCK:], d_source))
        d_both = low(mm(turned, d_pre_low))
        dnode_ref[nodes, width : 2 * width] = d_b
        dnode_ref[nodes, 2 * width : 3 * width] = d_both[:BLOCK]
        dnode_ref[nodes, 3 * width :] = d_both[BLOCK:]
    x = x_ref[...]
    add_rows(stat_ref, [col_sum(d_gated), pre_row])
    accumulate(
        acc_ref,
        [
            mm_rows(x, dnode_ref[:, :width]),
            mm_rows(x, dnode_ref[:, width : 2 * width]),
            mm_rows(e_ref[...], dedge_ref[...]),
            mm_rows(x, dnode_ref[:, 2 * width : 3 * width]),
            mm_rows(x, dnode_ref[:, 3 * width :]),
        ],
    )
    emit(acc_ref, out_ref)


def attend_back_kernel(
    info_ref, dsum_ref, global_ref, att_ref, q_ref, k_ref, v_ref, prob_ref, x_ref, sums_ref,
    backs_ref, w_ref, vec_ref,
    dqkv_ref, stat_ref, out_ref, acc_ref,
):
    group = global_ref.shape[0] // BLOCK
    width = global_ref.shape[1]
    score_scale = (width // HEADS) ** (-0.5)
    d_global = norm_back(
        info_ref, dsum_ref, global_ref, sums_ref[...], backs_ref[...], 2, vec_ref[7:8, :], 2
    )
    d_low = low(d_global)
    d_att = low(mm_back(d_low, w_ref[8]))
    for place in range(group):
        nodes = slice(place * BLOCK, (place + 1) * BLOCK)
        att_stack = head_stack(d_att[nodes])
        d_prob = mm_back(v_ref[nodes, :], att_stack)
        turned = []
        straight = []
        for head in range(HEADS):
            cols = slice(head * BLOCK, (head + 1) * BLOCK)
            prob = prob_ref[nodes, cols].astype(f32)
            part = d_prob[:, cols]
            inner = jnp.sum(prob * part, axis=0, keepdims=True)
            d_score = prob * (part - inner) * score_scale
            straight.append(low(d_score))
            turned.append(low(d_score.T))
        dqkv_ref[nodes, :width] = low(
            mm(jnp.concatenate(turned, axis=1), head_stack(k_ref[nodes, :]))
        )
        dqkv_ref[nodes, width : 2 * width] = low(
            mm(jnp.concatenate(straight, axis=1), head_stack(q_ref[nodes, :]))
        )
        dqkv_ref[nodes, 2 * width :] = low(mm(prob_ref[nodes, :], att_stack))
    x = x_ref[...]
    add_rows(
        stat_ref,
        [
            col_sum(dqkv_ref[:, :width].astype(f32)),
            col_sum(dqkv_ref[:, 2 * width :].astype(f32)),
            col_sum(d_global),
        ],
    )
    accumulate(
        acc_ref,
        [mm_rows(x, dqkv_ref[:, part * width : (part + 1) * width]) for part in range(3)]
        + [mm_rows(att_ref[...], d_low)],
    )
    emit(acc_ref, out_ref)


def input_grad_kernel(
    info_ref, dsum_ref, local_ref, global_ref, dnode_ref, dqkv_ref, dedge_ref, sums_ref,
    backs_ref, w_ref, vec_ref,
    node_ref, edge_ref,
):
    width = local_ref.shape[1]
    sums = sums_ref[...]
    backs = backs_ref[...]
    total = norm_back(info_ref, dsum_ref, local_ref, sums, backs, 0, vec_ref[5:6, :], 1)
    total = total + norm_back(info_ref, dsum_ref, global_ref, sums, backs, 2, vec_ref[7:8, :], 2)
    for place, mat in enumerate((0, 1, 3, 4)):
        total = total + mm_back(dnode_ref[:, place * width : (place + 1) * width], w_ref[mat])
    for place in range(3):
        total = total + mm_back(dqkv_ref[:, place * width : (place + 1) * width], w_ref[5 + place])
    node_ref[...] = total
    edge_ref[...] = mm_back(dedge_ref[...], w_ref[2])


def rows_spec(rows, width, offset=0):
    if offset:
        return pl.BlockSpec((rows, width), lambda step, info: (step + info[0], 0))
    return pl.BlockSpec((rows, width), lambda step, info: (step, 0))


def whole_spec(shape):
    zeros = (0,) * len(shape)
    return pl.BlockSpec(shape, lambda step, info: zeros)


def call(kernel, steps, info, inputs, outputs, scratch=(), cost=None):
    in_specs = []
    arrays = []
    for array, spec in inputs:
        arrays.append(array)
        in_specs.append(whole_spec(array.shape) if spec is None else spec)
    out_specs = []
    out_shapes = []
    for shape, dtype, spec in outputs:
        out_specs.append(whole_spec(shape) if spec is None else spec)
        out_shapes.append(jax.ShapeDtypeStruct(shape, dtype))
    return pl.pallas_call(
        kernel,
        grid_spec=pltpu.PrefetchScalarGridSpec(
            num_scalar_prefetch=1,
            grid=(steps,),
            in_specs=in_specs,
            out_specs=out_specs,
            scratch_shapes=list(scratch),
        ),
        out_shape=out_shapes,
        compiler_params=pltpu.CompilerParams(
            dimension_semantics=("arbitrary",), vmem_limit_bytes=48 * 1024 * 1024
        ),
        cost_estimate=cost,
    )(info, *arrays)


def swap_with(values, step, total):
    return lax.ppermute(values, axis_names, [(place, place ^ step) for place in range(total)])


def steps_of(total):
    return [1 << power for power in range(total.bit_length() - 1)]


def sum_small(values, total):
    for step in steps_of(total):
        values = values + swap_with(values, step, total)
    return values


def gather_matrices(shard, total):
    place = lax.axis_index(axis_names)
    mats, width = shard.shape
    held = shard[None]
    for step in reversed(steps_of(total)):
        other = swap_with(held, step, total)
        upper = (place & step) != 0
        held = jnp.concatenate(
            [jnp.where(upper, other, held), jnp.where(upper, held, other)], axis=0
        )
    bits = total.bit_length() - 1
    held = held.reshape((2,) * bits + (mats, width))
    held = held.transpose((bits,) + tuple(reversed(range(bits))) + (bits + 1,))
    return held.reshape(mats, total * width)


def scatter_sum(grads, total):
    place = lax.axis_index(axis_names)
    mats, width = grads.shape
    bits = total.bit_length() - 1
    held = grads.reshape((mats,) + (2,) * bits + (width // total,))
    held = held.transpose(tuple(reversed(range(1, bits + 1))) + (0, bits + 1))
    for step in steps_of(total):
        mine = ((place & step) != 0).astype(jnp.int32)
        sent = lax.dynamic_index_in_dim(held, 1 - mine, 0, keepdims=False)
        kept = lax.dynamic_index_in_dim(held, mine, 0, keepdims=False)
        held = kept.astype(f32) + swap_with(sent, step, total).astype(f32)
        if step * 2 < total:
            held = low(held)
    return held


def adamw(params, gradient, moment_one, moment_two, rate, decay):
    first = beta_one * moment_one + (1.0 - beta_one) * gradient
    second = beta_two * moment_two + (1.0 - beta_two) * gradient * gradient
    first_hat = first / (1.0 - beta_one**STEP)
    second_hat = second / (1.0 - beta_two**STEP)
    updated = params - rate * (first_hat / (jnp.sqrt(second_hat) + adam_eps) + decay * params)
    return (updated, first, second)


def own_half(values, branch_index):
    half = values.shape[0] // 2
    return lax.dynamic_slice_in_dim(values, branch_index * half, half, 0)


def per_device(
    node_feats,
    edge_feats,
    cotangent,
    graph_ids,
    node_mask,
    edge_src,
    edge_dst,
    edge_mask,
    weights,
    weight_moment1,
    weight_moment2,
    vectors,
    vector_moment1,
    vector_moment2,
):
    total = lax.axis_size("rows") * lax.axis_size("branch")
    branch_index = lax.axis_index("branch")
    width = node_feats.shape[1]
    rows = node_feats.shape[0] // 2
    edges = edge_feats.shape[0] // 2
    blocks = rows // BLOCK
    group = math.gcd(blocks, GROUP)
    steps = blocks // group
    tall = group * BLOCK
    tall_edges = group * EB
    w_bf = low(weights)
    matrices = gather_matrices(w_bf, total).reshape(MATS, width, width)
    counts = jnp.sum(own_half(node_mask, branch_index).reshape(blocks, BLOCK), axis=1)
    info = jnp.concatenate([(branch_index * steps)[None], counts]).astype(jnp.int32)

    def by_step(values, slots):
        return own_half(values, branch_index).reshape(steps, group, slots)

    def step_spec(slots):
        return pl.BlockSpec((1, group, slots), lambda step, info: (step, 0, 0))

    edge_spec = rows_spec(tall_edges, width)
    node_spec = rows_spec(tall, width)
    hot, turned, bias = call(
        prep_kernel,
        steps,
        info,
        [
            (by_step(edge_src, EB), step_spec(EB)),
            (by_step(edge_dst, EB), step_spec(EB)),
            (by_step(edge_mask, EB), step_spec(EB)),
            (by_step(graph_ids, BLOCK), step_spec(BLOCK)),
        ],
        [
            ((edges, EB), bf16, edge_spec),
            ((edges, EB), bf16, edge_spec),
            ((rows, BLOCK), f32, rows_spec(tall, BLOCK)),
        ],
    )
    x_in = (node_feats, rows_spec(tall, width, 1))
    e_in = (edge_feats, rows_spec(tall_edges, width, 1))
    mats_in = (matrices, None)
    vec_in = (vectors, None)
    node_f32 = ((rows, width), f32, node_spec)
    node_bf = ((rows, width), bf16, node_spec)
    sums_out = ((8, width), f32, None)
    local_out, gated, recip, ratio, opened, b_source, local_sums = call(
        local_kernel,
        steps,
        info,
        [x_in, e_in, (hot, edge_spec), (turned, edge_spec), mats_in, vec_in],
        [
            node_f32,
            node_f32,
            node_f32,
            node_f32,
            ((edges, width), f32, edge_spec),
            ((edges, width), bf16, edge_spec),
            sums_out,
        ],
    )
    prob_spec = rows_spec(tall, HEADS * BLOCK)
    global_out, queries, keyed, valued, attended, probs, global_sums = call(
        attend_kernel,
        steps,
        info,
        [x_in, (bias, rows_spec(tall, BLOCK)), mats_in, vec_in],
        [
            node_f32,
            node_bf,
            node_bf,
            node_bf,
            node_bf,
            ((rows, HEADS * BLOCK), bf16, prob_spec),
            sums_out,
        ],
    )
    count_row = jnp.full((1, width), jnp.sum(counts).astype(f32))
    sums = sum_small(
        jnp.concatenate(
            [local_sums[:2], global_sums[:2], count_row, jnp.zeros((3, width), f32)], axis=0
        ),
        total,
    )
    sums_in = (sums, None)
    cot_in = (cotangent, node_spec)
    wide_spec = rows_spec(tall, 2 * width)
    summed_low, hidden, mixed, top_part = call(
        mix_kernel,
        steps,
        info,
        [(local_out, node_spec), (global_out, node_spec), cot_in, sums_in, mats_in, vec_in],
        [node_bf, ((rows, 2 * width), f32, wide_spec), node_f32, sums_out],
    )
    tops = sum_small(top_part, total)
    layer_out, d_mixed, d_hidden, hidden_low, d_summed, back_part = call(
        mix_back_kernel,
        steps,
        info,
        [
            (mixed, node_spec),
            (hidden, wide_spec),
            cot_in,
            (local_out, node_spec),
            (global_out, node_spec),
            sums_in,
            (tops, None),
            mats_in,
            vec_in,
        ],
        [
            node_bf,
            node_bf,
            ((rows, 2 * width), bf16, wide_spec),
            ((rows, 2 * width), bf16, wide_spec),
            node_bf,
            sums_out,
        ],
    )
    backs = sum_small(back_part, total)

    def mat_out(number):
        return ((number, width, width), bf16, None)

    def mat_acc(number):
        return pltpu.VMEM((number, width, width), f32)

    mix_grads = call(
        lambda info_ref, *refs: mix_grad_kernel(*refs),
        steps,
        info,
        [
            (summed_low, node_spec),
            (d_hidden, wide_spec),
            (hidden_low, wide_spec),
            (d_mixed, node_spec),
        ],
        [mat_out(4)],
        [mat_acc(4)],
    )[0]
    backs_in = (backs, None)
    dsum_in = (d_summed, node_spec)
    dnode_spec = rows_spec(tall, 4 * width)
    d_node, d_edge, local_bias, local_grads = call(
        local_back_kernel,
        steps,
        info,
        [
            dsum_in,
            (local_out, node_spec),
            (gated, node_spec),
            (recip, node_spec),
            (ratio, node_spec),
            (opened, edge_spec),
            (b_source, edge_spec),
            (hot, edge_spec),
            (turned, edge_spec),
            x_in,
            e_in,
            sums_in,
            backs_in,
            vec_in,
        ],
        [
            ((rows, 4 * width), bf16, dnode_spec),
            ((edges, width), bf16, edge_spec),
            sums_out,
            mat_out(5),
        ],
        [mat_acc(5)],
    )
    dqkv_spec = rows_spec(tall, 3 * width)
    d_qkv, attend_bias, attend_grads = call(
        attend_back_kernel,
        steps,
        info,
        [
            dsum_in,
            (global_out, node_spec),
            (attended, node_spec),
            (queries, node_spec),
            (keyed, node_spec),
            (valued, node_spec),
            (probs, prob_spec),
            x_in,
            sums_in,
            backs_in,
            mats_in,
            vec_in,
        ],
        [((rows, 3 * width), bf16, dqkv_spec), sums_out, mat_out(4)],
        [mat_acc(4)],
    )
    all_grads = jnp.concatenate([local_grads, attend_grads, mix_grads], axis=0)
    grad_shard = scatter_sum(all_grads.reshape(MATS, width * width), total)
    node_grad, edge_grad = call(
        input_grad_kernel,
        steps,
        info,
        [
            dsum_in,
            (local_out, node_spec),
            (global_out, node_spec),
            (d_node, dnode_spec),
            (d_qkv, dqkv_spec),
            (d_edge, edge_spec),
            sums_in,
            backs_in,
            mats_in,
            vec_in,
        ],
        [node_f32, ((edges, width), f32, edge_spec)],
    )
    square_row = jnp.broadcast_to(jnp.sum(grad_shard * grad_shard), (1, width))
    tail = sum_small(
        jnp.concatenate(
            [local_bias[:2], attend_bias[:3], square_row, jnp.zeros((2, width), f32)], axis=0
        ),
        total,
    )
    top_mean = tops[0:1] / sums[4:5]
    top_rstd = lax.rsqrt(tops[1:2] / sums[4:5] - top_mean * top_mean + eps_norm)
    vector_total = jnp.concatenate(
        [
            tail[:5],
            backs[1:2],
            backs[0:1],
            backs[2:3],
            backs[0:1],
            backs[3:6],
            (tops[3:4] - top_mean * tops[2:3]) * top_rstd,
            tops[2:3],
        ],
        axis=0,
    )
    grad_norm = jnp.sqrt(tail[5, 0] + jnp.sum(vector_total * vector_total))
    factor = jnp.minimum(1.0, clip_limit / (grad_norm + 1e-06))
    new_weights, first_w, second_w = adamw(
        weights, factor * grad_shard, weight_moment1, weight_moment2, rate_mats, decay_mats
    )
    new_vectors, first_v, second_v = adamw(
        vectors, factor * vector_total, vector_moment1, vector_moment2, rate_vecs, 0.0
    )
    return (
        layer_out,
        node_grad,
        edge_grad,
        new_weights,
        first_w,
        second_w,
        new_vectors,
        first_v,
        second_v,
        grad_norm,
    )


def solution(mesh):
    in_specs = (
        P("rows", None),
        P("rows", None),
        P(("rows", "branch"), None),
        P("rows"),
        P("rows"),
        P("rows"),
        P("rows"),
        P("rows"),
        P(None, ("rows", "branch")),
        P(None, ("rows", "branch")),
        P(None, ("rows", "branch")),
        P(),
        P(),
        P(),
    )
    out_specs = (
        P(("rows", "branch"), None),
        P(("rows", "branch"), None),
        P(("rows", "branch"), None),
        P(None, ("rows", "branch")),
        P(None, ("rows", "branch")),
        P(None, ("rows", "branch")),
        P(),
        P(),
        P(),
        P(),
    )
    return jax.shard_map(
        per_device, mesh=mesh, in_specs=in_specs, out_specs=out_specs, check_vma=False
    )
```

```python
import functools
import math

import jax
import jax.numpy as jnp
from jax import lax
from jax.experimental import pallas as pl
from jax.experimental.pallas import tpu as pltpu
from jax.sharding import PartitionSpec as P

HEADS = 8
BLOCK = 128
EB = 256
MATS = 13
STEP = 7
GROUP = 4

eps_norm = 1e-05
clip_limit = 1.0
beta_one = 0.9
beta_two = 0.999
rate_mats = 0.1
rate_vecs = 0.8
decay_mats = 0.01
adam_eps = 1e-08
hidden_floor = -1e30
axis_names = ("rows", "branch")
f32 = jnp.float32
bf16 = jnp.bfloat16


def mm(left, right):
    return jnp.dot(left, right, preferred_element_type=f32)


def mm_back(left, right):
    return lax.dot_general(left, right, (((1,), (1,)), ((), ())), preferred_element_type=f32)


def mm_rows(left, right):
    return lax.dot_general(left, right, (((0,), (0,)), ((), ())), preferred_element_type=f32)


def low(values):
    return values.astype(bf16)


def sig(values):
    return 0.5 * jnp.tanh(0.5 * values) + 0.5


def col_sum(values):
    return jnp.sum(values, axis=0, keepdims=True)


def live_of(info_ref, first_block, group, width):
    slot = lax.broadcasted_iota(jnp.int32, (BLOCK, width), 0)
    return jnp.concatenate(
        [
            jnp.where(slot < info_ref[1 + first_block + place], 1.0, 0.0)
            for place in range(group)
        ],
        axis=0,
    )


def add_rows(out_ref, rows):
    @pl.when(pl.program_id(0) == 0)
    def _():
        out_ref[...] = jnp.zeros_like(out_ref)

    for place, row in enumerate(rows):
        out_ref[place : place + 1, :] += row


def norm_terms(sums, first, count_row):
    mean = sums[first : first + 1] / count_row
    rstd = lax.rsqrt(sums[first + 1 : first + 2] / count_row - mean * mean + eps_norm)
    return (mean, rstd)


def prep_kernel(info_ref, src_ref, dst_ref, mask_ref, id_ref, hot_ref, turned_ref, bias_ref):
    for place in range(GROUP):
        row = pl.ds(place, 1)
        node = lax.broadcasted_iota(jnp.int32, (BLOCK, EB), 0)
        live = mask_ref[0, row, :] != 0
        dst_rows = jnp.where((node == dst_ref[0, row, :]) & live, 1.0, 0.0)
        src_rows = jnp.where((node == src_ref[0, row, :]) & live, 1.0, 0.0)
        turned = jnp.concatenate([dst_rows, src_rows], axis=0)
        turned_ref[place * EB : (place + 1) * EB, :] = low(turned)
        hot_ref[place * EB : (place + 1) * EB, :] = low(turned.T)
        ids = jnp.broadcast_to(id_ref[0, row, :].astype(f32), (BLOCK, BLOCK))
        bias_ref[place * BLOCK : (place + 1) * BLOCK, :] = jnp.where(
            ids == ids.T, 0.0, hidden_floor
        )


def local_kernel(
    info_ref, x_ref, e_ref, hot_ref, turned_ref, w_ref, vec_ref,
    out_ref, slope_ref, recip_ref, fall_ref, open_ref, bend_ref, bsrc_ref, sums_ref,
):
    group = x_ref.shape[0] // BLOCK
    x = x_ref[...]
    a_part = mm(x, w_ref[0]) + vec_ref[0:1, :]
    b_part = low(mm(x, w_ref[1]))
    d_part = low(mm(x, w_ref[3]))
    e_part = low(mm(x, w_ref[4]))
    c_part = mm(e_ref[...], w_ref[2]) + vec_ref[1:2, :]
    nums = []
    dens = []
    for place in range(group):
        nodes = slice(place * BLOCK, (place + 1) * BLOCK)
        edges = slice(place * EB, (place + 1) * EB)
        hot = hot_ref[edges, :]
        gate = c_part[edges] + mm(hot, jnp.concatenate([d_part[nodes], e_part[nodes]], axis=0))
        opened = sig(gate)
        b_source = mm(hot[:, BLOCK:], b_part[nodes])
        open_ref[edges, :] = low(opened)
        bend_ref[edges, :] = low(opened * (1.0 - opened))
        bsrc_ref[edges, :] = low(b_source)
        dst_turned = turned_ref[place * EB : place * EB + BLOCK, :]
        nums.append(mm(dst_turned, low(opened * b_source)))
        dens.append(mm(dst_turned, low(opened)))
    recip = 1.0 / (jnp.concatenate(dens, axis=0) + 1.0)
    ratio = jnp.concatenate(nums, axis=0) * recip
    gated = a_part + ratio
    gated_sig = sig(gated)
    out = x.astype(f32) + gated * gated_sig
    slope_ref[...] = low(gated_sig * (1.0 + gated * (1.0 - gated_sig)))
    recip_ref[...] = low(recip)
    fall_ref[...] = low(ratio * recip)
    out_ref[...] = out
    live = live_of(info_ref, pl.program_id(0) * group, group, out.shape[1])
    kept = live * out
    add_rows(sums_ref, [col_sum(kept), col_sum(kept * out)])


def head_stack(values):
    head = lax.broadcasted_iota(jnp.int32, values.shape, 1) // (values.shape[1] // HEADS)
    wide = values.astype(f32)
    return jnp.concatenate(
        [low(jnp.where(head == place, wide, 0.0)) for place in range(HEADS)], axis=0
    )


def attend_kernel(
    info_ref, x_ref, bias_ref, w_ref, vec_ref,
    out_ref, q_ref, k_ref, v_ref, att_ref, prob_ref, sums_ref,
):
    group = x_ref.shape[0] // BLOCK
    x = x_ref[...]
    queries = low(mm(x, w_ref[5]) + vec_ref[2:3, :])
    keyed = low(mm(x, w_ref[6]))
    valued = low(mm(x, w_ref[7]) + vec_ref[3:4, :])
    q_ref[...] = queries
    k_ref[...] = keyed
    v_ref[...] = valued
    score_scale = (x.shape[1] // HEADS) ** (-0.5)
    for place in range(group):
        nodes = slice(place * BLOCK, (place + 1) * BLOCK)
        raw = mm_back(keyed[nodes], head_stack(queries[nodes]))
        bias = bias_ref[nodes, :]
        probs = []
        turned = []
        for head in range(HEADS):
            part = raw[:, head * BLOCK : (head + 1) * BLOCK] + bias
            part = jnp.exp((part - jnp.max(part, axis=0, keepdims=True)) * score_scale)
            part = part * (1.0 / jnp.sum(part, axis=0, keepdims=True))
            probs.append(low(part))
            turned.append(low(part).T)
        prob_ref[nodes, :] = jnp.concatenate(probs, axis=1)
        att_ref[nodes, :] = low(
            mm(jnp.concatenate(turned, axis=1), head_stack(valued[nodes]))
        )
    out = x.astype(f32) + mm(att_ref[...], w_ref[8]) + vec_ref[4:5, :]
    out_ref[...] = out
    live = live_of(info_ref, pl.program_id(0) * group, group, out.shape[1])
    kept = live * out
    add_rows(sums_ref, [col_sum(kept), col_sum(kept * out)])


def mix_kernel(
    info_ref, local_ref, global_ref, cot_ref, sums_ref, w_ref, vec_ref,
    low_ref, hlow_ref, slope_ref, lhat_ref, ghat_ref, mixed_ref, stat_ref,
):
    group = local_ref.shape[0] // BLOCK
    width = local_ref.shape[1]
    sums = sums_ref[...]
    count_row = sums[4:5]
    local_mean, local_rstd = norm_terms(sums, 0, count_row)
    global_mean, global_rstd = norm_terms(sums, 2, count_row)
    local_hat = (local_ref[...] - local_mean) * local_rstd
    global_hat = (global_ref[...] - global_mean) * global_rstd
    lhat_ref[...] = low(local_hat)
    ghat_ref[...] = low(global_hat)
    local_norm = local_hat * vec_ref[5:6, :] + vec_ref[6:7, :]
    global_norm = global_hat * vec_ref[7:8, :] + vec_ref[8:9, :]
    summed = low(local_norm).astype(f32) + low(global_norm).astype(f32)
    summed_low = low(summed)
    low_ref[...] = summed_low
    mixed = summed + vec_ref[11:12, :]
    for half in range(2):
        hidden = mm(summed_low, w_ref[9 + half]) + vec_ref[9 + half : 10 + half, :]
        sig_value = sig(hidden)
        hidden_low = low(hidden * sig_value)
        hlow_ref[:, half * width : (half + 1) * width] = hidden_low
        slope_ref[:, half * width : (half + 1) * width] = low(
            sig_value * (1.0 + hidden * (1.0 - sig_value))
        )
        mixed = mixed + mm(hidden_low, w_ref[11 + half])
    mixed_ref[...] = mixed
    live = live_of(info_ref, pl.program_id(0) * group, group, width)
    kept = live * mixed
    d_norm = live * cot_ref[...].astype(f32)
    add_rows(
        stat_ref, [col_sum(kept), col_sum(kept * mixed), col_sum(d_norm), col_sum(d_norm * mixed)]
    )


def mix_back_kernel(
    info_ref, mixed_ref, slope_ref, cot_ref, lhat_ref, ghat_ref, sums_ref, tops_ref, w_ref,
    vec_ref,
    layer_ref, dmix_ref, dhid_ref, dsum_ref, stat_ref,
):
    group = mixed_ref.shape[0] // BLOCK
    width = mixed_ref.shape[1]
    sums = sums_ref[...]
    tops = tops_ref[...]
    count_row = sums[4:5]
    mean, rstd = norm_terms(tops, 0, count_row)
    live = live_of(info_ref, pl.program_id(0) * group, group, width)
    hat = (mixed_ref[...] - mean) * rstd
    layer_ref[...] = low(live * (vec_ref[12:13, :] * hat + vec_ref[13:14, :]))
    d_norm = live * cot_ref[...].astype(f32)
    dz_sum = tops[2:3]
    dz_hat = (tops[3:4] - mean * dz_sum) * rstd
    d_mixed = (vec_ref[12:13, :] * rstd) * (
        d_norm - live * (dz_sum / count_row + hat * (dz_hat / count_row))
    )
    d_mixed_low = low(d_mixed)
    dmix_ref[...] = d_mixed_low
    d_summed = d_mixed
    rows = []
    for half in range(2):
        cols = slice(half * width, (half + 1) * width)
        d_hidden = low(mm_back(d_mixed_low, w_ref[11 + half]) * slope_ref[:, cols].astype(f32))
        dhid_ref[:, cols] = d_hidden
        rows.append(col_sum(d_hidden.astype(f32)))
        d_summed = d_summed + mm_back(d_hidden, w_ref[9 + half])
    d_low = low(d_summed)
    dsum_ref[...] = d_low
    d_sum = d_low.astype(f32)
    add_rows(
        stat_ref,
        [
            col_sum(d_sum),
            col_sum(d_sum * lhat_ref[...].astype(f32)),
            col_sum(d_sum * ghat_ref[...].astype(f32)),
            rows[0],
            rows[1],
            col_sum(d_mixed),
        ],
    )


def accumulate(acc_ref, terms):
    @pl.when(pl.program_id(0) == 0)
    def _():
        acc_ref[...] = jnp.zeros_like(acc_ref)

    for place, term in enumerate(terms):
        acc_ref[place] += term


def emit(acc_ref, out_ref):
    @pl.when(pl.program_id(0) == pl.num_programs(0) - 1)
    def _():
        out_ref[...] = acc_ref[...]


def inner_grad_kernel(info_ref, slow_ref, dhid_ref, out_ref, acc_ref):
    width = slow_ref.shape[1]
    accumulate(
        acc_ref,
        [
            mm_rows(slow_ref[...], dhid_ref[:, half * width : (half + 1) * width])
            for half in range(2)
        ],
    )
    emit(acc_ref, out_ref)


def outer_grad_kernel(info_ref, hlow_ref, dmix_ref, out_ref, acc_ref):
    width = dmix_ref.shape[1]
    accumulate(
        acc_ref,
        [
            mm_rows(hlow_ref[:, half * width : (half + 1) * width], dmix_ref[...])
            for half in range(2)
        ],
    )
    emit(acc_ref, out_ref)


def norm_back(info_ref, dsum_ref, hat_ref, sums, backs, first, gain_row, hat_row):
    group = hat_ref.shape[0] // BLOCK
    count_row = sums[4:5]
    rstd = norm_terms(sums, first, count_row)[1]
    live = live_of(info_ref, pl.program_id(0) * group, group, hat_ref.shape[1])
    hat = hat_ref[...].astype(f32)
    return (gain_row * rstd) * (
        dsum_ref[...].astype(f32)
        - live * (backs[0:1] / count_row + hat * (backs[hat_row : hat_row + 1] / count_row))
    )


def local_back_kernel(
    info_ref, dsum_ref, local_ref, slope_ref, recip_ref, fall_ref, open_ref, bend_ref, bsrc_ref,
    hot_ref, turned_ref, x_ref, e_ref, sums_ref, backs_ref, vec_ref,
    dnode_ref, dedge_ref, stat_ref, out_ref, acc_ref,
):
    group = local_ref.shape[0] // BLOCK
    width = local_ref.shape[1]
    d_local = norm_back(
        info_ref, dsum_ref, local_ref, sums_ref[...], backs_ref[...], 0, vec_ref[5:6, :], 1
    )
    d_gated = d_local * slope_ref[...].astype(f32)
    dnode_ref[:, :width] = low(d_gated)
    d_num = low(d_gated * recip_ref[...].astype(f32))
    d_den = low(-d_gated * fall_ref[...].astype(f32))
    pre_row = jnp.zeros((1, width), f32)
    for place in range(group):
        nodes = slice(place * BLOCK, (place + 1) * BLOCK)
        edges = slice(place * EB, (place + 1) * EB)
        hot_dst = hot_ref[edges, :BLOCK]
        d_message = mm(hot_dst, d_num[nodes])
        opened = open_ref[edges, :].astype(f32)
        d_open = d_message * bsrc_ref[edges, :].astype(f32) + mm(hot_dst, d_den[nodes])
        d_source = low(d_message * opened)
        d_pre = d_open * bend_ref[edges, :].astype(f32)
        d_pre_low = low(d_pre)
        pre_row = pre_row + col_sum(d_pre)
        dedge_ref[edges, :] = d_pre_low
        turned = turned_ref[edges, :]
        d_b = low(mm(turned[BLOCK:], d_source))
        d_both = low(mm(turned, d_pre_low))
        dnode_ref[nodes, width : 2 * width] = d_b
        dnode_ref[nodes, 2 * width : 3 * width] = d_both[:BLOCK]
        dnode_ref[nodes, 3 * width :] = d_both[BLOCK:]
    x = x_ref[...]
    add_rows(stat_ref, [col_sum(d_gated), pre_row])
    accumulate(
        acc_ref,
        [
            mm_rows(x, dnode_ref[:, :width]),
            mm_rows(x, dnode_ref[:, width : 2 * width]),
            mm_rows(e_ref[...], dedge_ref[...]),
            mm_rows(x, dnode_ref[:, 2 * width : 3 * width]),
            mm_rows(x, dnode_ref[:, 3 * width :]),
        ],
    )
    emit(acc_ref, out_ref)


def attend_back_kernel(
    info_ref, dsum_ref, global_ref, att_ref, q_ref, k_ref, v_ref, prob_ref, x_ref, sums_ref,
    backs_ref, w_ref, vec_ref, lgrad_ref, igrad_ref, ograd_ref,
    dqkv_ref, stat_ref, *out_and_acc,
):
    acc_ref = out_and_acc[-1]
    group = global_ref.shape[0] // BLOCK
    width = global_ref.shape[1]
    score_scale = (width // HEADS) ** (-0.5)
    d_global = norm_back(
        info_ref, dsum_ref, global_ref, sums_ref[...], backs_ref[...], 2, vec_ref[7:8, :], 2
    )
    d_low = low(d_global)
    d_att = low(mm_back(d_low, w_ref[8]))
    for place in range(group):
        nodes = slice(place * BLOCK, (place + 1) * BLOCK)
        att_stack = head_stack(d_att[nodes])
        d_prob = mm_back(v_ref[nodes, :], att_stack)
        turned = []
        straight = []
        for head in range(HEADS):
            cols = slice(head * BLOCK, (head + 1) * BLOCK)
            prob = prob_ref[nodes, cols].astype(f32)
            part = d_prob[:, cols]
            inner = jnp.sum(prob * part, axis=0, keepdims=True)
            d_score = prob * (part - inner) * score_scale
            straight.append(low(d_score))
            turned.append(low(d_score).T)
        dqkv_ref[nodes, :width] = low(
            mm(jnp.concatenate(turned, axis=1), head_stack(k_ref[nodes, :]))
        )
        dqkv_ref[nodes, width : 2 * width] = low(
            mm(jnp.concatenate(straight, axis=1), head_stack(q_ref[nodes, :]))
        )
        dqkv_ref[nodes, 2 * width :] = low(mm(prob_ref[nodes, :], att_stack))
    x = x_ref[...]
    add_rows(
        stat_ref,
        [
            col_sum(dqkv_ref[:, :width].astype(f32)),
            col_sum(dqkv_ref[:, 2 * width :].astype(f32)),
            col_sum(d_global),
        ],
    )
    accumulate(
        acc_ref,
        [mm_rows(x, dqkv_ref[:, part * width : (part + 1) * width]) for part in range(3)]
        + [mm_rows(att_ref[...], d_low)],
    )
    last = pl.num_programs(0) - 1

    @pl.when(pl.program_id(0) == last)
    def _():
        parts = [lgrad_ref.at[place] for place in range(5)]
        parts = parts + [acc_ref.at[place] for place in range(4)]
        parts = parts + [ref.at[place] for ref in (igrad_ref, ograd_ref) for place in range(2)]
        if len(out_and_acc) == 2:
            for place, part in enumerate(parts):
                out_and_acc[0][place] = low(part[...])
        else:
            pack(info_ref, parts, out_and_acc[0], out_and_acc[1])


def reach(order, index):
    found = 0
    for place, step in enumerate(order):
        if index >> (len(order) - 1 - place) & 1:
            found ^= step >> 1
    return found


def chip_orders(total):
    chips = steps_of(total)[1:]
    return (chips, chips[1:-1] + chips[:1] + chips[-1:])


def pack(info_ref, parts, keep_ref, send_ref):
    slots = keep_ref.shape[0]
    orders = chip_orders(2 * slots)
    core = info_ref[info_ref.shape[0] - 2]
    chip = info_ref[info_ref.shape[0] - 1]
    for slot in range(slots):
        near = [reach(order, slot) for order in orders]
        for out_ref, owner in ((keep_ref, core), (send_ref, 1 - core)):
            step = jnp.where(owner == 0, near[0], near[1])
            row = pl.multiple_of(16 * jnp.bitwise_xor(chip, step) + 8 * owner, 8)
            for first in range(0, len(parts), 2):
                pair = [part[pl.ds(row, 8), :] for part in parts[first : first + 2]]
                out_ref[slot, first * 8 : first * 8 + 8 * len(pair), :] = low(
                    jnp.concatenate(pair, axis=0)
                )


def assemble_kernel(info_ref, held_ref, other_ref, out_ref):
    slots, tall, _ = held_ref.shape
    orders = chip_orders(2 * slots)
    core = info_ref[info_ref.shape[0] - 2]
    chip = info_ref[info_ref.shape[0] - 1]

    def fill(even_ref, odd_ref):
        for far in range(slots):
            even, odd = [
                [slot for slot in range(slots) if reach(order, slot) == far][0] for order in orders
            ]
            row = pl.multiple_of(16 * jnp.bitwise_xor(chip, far), 16)
            for first in range(0, tall, 16):
                size = min(16, tall - first)
                upper = even_ref[even, first : first + size, :].astype(f32)
                lower = odd_ref[odd, first : first + size, :].astype(f32)
                for half in range(size // 8):
                    rows = slice(half * 8, half * 8 + 8)
                    out_ref[first // 8 + half, pl.ds(row, 16), :] = low(
                        jnp.concatenate([upper[rows], lower[rows]], axis=0)
                    )

    @pl.when(core == 0)
    def _():
        fill(held_ref, other_ref)

    @pl.when(core != 0)
    def _():
        fill(other_ref, held_ref)


def node_grad_kernel(
    info_ref, dsum_ref, lhat_ref, ghat_ref, dnode_ref, dqkv_ref, sums_ref, backs_ref, w_ref,
    vec_ref,
    node_ref,
):
    width = lhat_ref.shape[1]
    sums = sums_ref[...]
    backs = backs_ref[...]
    total = norm_back(info_ref, dsum_ref, lhat_ref, sums, backs, 0, vec_ref[5:6, :], 1)
    total = total + norm_back(info_ref, dsum_ref, ghat_ref, sums, backs, 2, vec_ref[7:8, :], 2)
    for place, mat in enumerate((0, 1, 3, 4)):
        total = total + mm_back(dnode_ref[:, place * width : (place + 1) * width], w_ref[mat])
    for place in range(3):
        total = total + mm_back(dqkv_ref[:, place * width : (place + 1) * width], w_ref[5 + place])
    node_ref[...] = total


def edge_grad_kernel(info_ref, dedge_ref, w_ref, edge_ref):
    edge_ref[...] = mm_back(dedge_ref[...], w_ref[2])


def rows_spec(rows, width, offset=0):
    if offset:
        return pl.BlockSpec((rows, width), lambda step, info: (step + info[0], 0))
    return pl.BlockSpec((rows, width), lambda step, info: (step, 0))


def whole_spec(shape):
    zeros = (0,) * len(shape)
    return pl.BlockSpec(shape, lambda step, info: zeros)


def call(kernel, steps, info, inputs, outputs, scratch=(), cost=None):
    in_specs = []
    arrays = []
    for array, spec in inputs:
        arrays.append(array)
        in_specs.append(whole_spec(array.shape) if spec is None else spec)
    out_specs = []
    out_shapes = []
    for shape, dtype, spec in outputs:
        out_specs.append(whole_spec(shape) if spec is None else spec)
        out_shapes.append(jax.ShapeDtypeStruct(shape, dtype))
    return pl.pallas_call(
        kernel,
        grid_spec=pltpu.PrefetchScalarGridSpec(
            num_scalar_prefetch=1,
            grid=(steps,),
            in_specs=in_specs,
            out_specs=out_specs,
            scratch_shapes=list(scratch),
        ),
        out_shape=out_shapes,
        compiler_params=pltpu.CompilerParams(
            dimension_semantics=("arbitrary",), vmem_limit_bytes=12 * 1024 * 1024
        ),
        cost_estimate=cost,
    )(info, *arrays)


def swap_with(values, step, total):
    return lax.ppermute(values, axis_names, [(place, place ^ step) for place in range(total)])


def steps_of(total):
    return [1 << power for power in range(total.bit_length() - 1)]


def beside(start, transfer, info, work):
    info = lax.optimization_barrier((info, start))[0]
    return lax.optimization_barrier((transfer, work(info)))


def sum_small(values, total, info=None, works=()):
    results = []
    works = list(works)
    for step in steps_of(total):
        other = swap_with(values, step, total)
        if works and step > 1:
            other, done = beside(values, other, info, works.pop(0))
            results.append(done)
        values = values + other
    return (values, results) if results else values


def swap_chips(values, number, total):
    orders = chip_orders(total)
    return lax.ppermute(
        values,
        axis_names,
        [(place, place ^ orders[place % 2][number]) for place in range(total)],
    )


def in_rows(total, width):
    return width * width // total == 8 * width


def gather_matrices(shard, info, total, width):
    mats = shard.shape[0]
    if not in_rows(total, width):
        gathered = lax.all_gather(shard, axis_names, axis=1, tiled=True)
        return gathered.reshape(mats, width, width)
    held = shard.reshape(1, mats * 8, width)
    for number in reversed(range(len(chip_orders(total)[0]))):
        held = jnp.concatenate([held, swap_chips(held, number, total)], axis=0)
    other = swap_with(held, 1, total)
    return call(
        assemble_kernel,
        1,
        info,
        [(held, None), (other, None)],
        [((mats, width, width), bf16, None)],
    )[0]


def scatter_plain(grads, total):
    place = lax.axis_index(axis_names)
    mats, width, _ = grads.shape
    bits = total.bit_length() - 1
    held = grads.reshape((mats,) + (2,) * bits + (width * width // total,))
    held = held.transpose(tuple(reversed(range(1, bits + 1))) + (0, bits + 1))
    for step in steps_of(total):
        mine = ((place & step) != 0).astype(jnp.int32)
        sent = lax.dynamic_index_in_dim(held, 1 - mine, 0, keepdims=False)
        kept = lax.dynamic_index_in_dim(held, mine, 0, keepdims=False)
        held = kept.astype(f32) + swap_with(sent, step, total).astype(f32)
        if step * 2 < total:
            held = low(held)
    return held


def scatter_packed(kept, sent, total, info, works):
    got = swap_with(sent, 1, total)
    results = []
    for number in range(len(chip_orders(total)[0])):
        half = kept.shape[0] // 2
        sent = low(kept[half:].astype(f32) + got[half:].astype(f32))
        kept = kept[:half].astype(f32) + got[:half].astype(f32)
        got = swap_chips(sent, number, total)
        if number < len(works):
            got, done = beside(sent, got, info, works[number])
            results.append(done)
    return ((kept + got.astype(f32)).reshape(-1, 8 * kept.shape[-1]), results)


def adamw(params, gradient, moment_one, moment_two, rate, decay):
    first = beta_one * moment_one + (1.0 - beta_one) * gradient
    second = beta_two * moment_two + (1.0 - beta_two) * gradient * gradient
    first_hat = first / (1.0 - beta_one**STEP)
    second_hat = second / (1.0 - beta_two**STEP)
    updated = params - rate * (first_hat / (jnp.sqrt(second_hat) + adam_eps) + decay * params)
    return (updated, first, second)


def own_half(values, branch_index):
    half = values.shape[0] // 2
    return lax.dynamic_slice_in_dim(values, branch_index * half, half, 0)


def per_device(
    node_feats,
    edge_feats,
    cotangent,
    graph_ids,
    node_mask,
    edge_src,
    edge_dst,
    edge_mask,
    weights,
    weight_moment1,
    weight_moment2,
    vectors,
    vector_moment1,
    vector_moment2,
):
    total = lax.axis_size("rows") * lax.axis_size("branch")
    branch_index = lax.axis_index("branch")
    width = node_feats.shape[1]
    rows = node_feats.shape[0] // 2
    edges = edge_feats.shape[0] // 2
    blocks = rows // BLOCK
    group = math.gcd(blocks, GROUP)
    steps = blocks // group
    tall = group * BLOCK
    tall_edges = group * EB
    w_bf = low(weights)
    counts = jnp.sum(own_half(node_mask, branch_index).reshape(blocks, BLOCK), axis=1)
    info = jnp.concatenate(
        [(branch_index * steps)[None], counts, branch_index[None], lax.axis_index("rows")[None]]
    ).astype(jnp.int32)
    matrices = gather_matrices(w_bf, info, total, width)

    def by_step(values, slots):
        return own_half(values, branch_index).reshape(steps, group, slots)

    def step_spec(slots):
        return pl.BlockSpec((1, group, slots), lambda step, info: (step, 0, 0))

    edge_spec = rows_spec(tall_edges, width)
    node_spec = rows_spec(tall, width)
    hot, turned, bias = call(
        prep_kernel,
        steps,
        info,
        [
            (by_step(edge_src, EB), step_spec(EB)),
            (by_step(edge_dst, EB), step_spec(EB)),
            (by_step(edge_mask, EB), step_spec(EB)),
            (by_step(graph_ids, BLOCK), step_spec(BLOCK)),
        ],
        [
            ((edges, EB), bf16, edge_spec),
            ((edges, EB), bf16, edge_spec),
            ((rows, BLOCK), f32, rows_spec(tall, BLOCK)),
        ],
    )
    x_in = (node_feats, rows_spec(tall, width, 1))
    e_in = (edge_feats, rows_spec(tall_edges, width, 1))
    mats_in = (matrices, None)
    vec_in = (vectors, None)
    node_f32 = ((rows, width), f32, node_spec)
    node_bf = ((rows, width), bf16, node_spec)
    sums_out = ((8, width), f32, None)
    local_out, gate_slope, recip, fall, opened, bend, b_source, local_sums = call(
        local_kernel,
        steps,
        info,
        [x_in, e_in, (hot, edge_spec), (turned, edge_spec), mats_in, vec_in],
        [
            node_f32,
            node_bf,
            node_bf,
            node_bf,
            ((edges, width), bf16, edge_spec),
            ((edges, width), bf16, edge_spec),
            ((edges, width), bf16, edge_spec),
            sums_out,
        ],
    )
    prob_spec = rows_spec(tall, HEADS * BLOCK)
    global_out, queries, keyed, valued, attended, probs, global_sums = call(
        attend_kernel,
        steps,
        info,
        [x_in, (bias, rows_spec(tall, BLOCK)), mats_in, vec_in],
        [
            node_f32,
            node_bf,
            node_bf,
            node_bf,
            node_bf,
            ((rows, HEADS * BLOCK), bf16, prob_spec),
            sums_out,
        ],
    )
    count_row = jnp.full((1, width), jnp.sum(counts).astype(f32))
    sums = sum_small(
        jnp.concatenate(
            [local_sums[:2], global_sums[:2], count_row, jnp.zeros((3, width), f32)], axis=0
        ),
        total,
    )
    sums_in = (sums, None)
    cot_in = (cotangent, node_spec)
    wide_spec = rows_spec(tall, 2 * width)
    summed_low, hidden_low, hidden_slope, local_hat, global_hat, mixed, top_part = call(
        mix_kernel,
        steps,
        info,
        [(local_out, node_spec), (global_out, node_spec), cot_in, sums_in, mats_in, vec_in],
        [
            node_bf,
            ((rows, 2 * width), bf16, wide_spec),
            ((rows, 2 * width), bf16, wide_spec),
            node_bf,
            node_bf,
            node_f32,
            sums_out,
        ],
    )
    tops = sum_small(top_part, total)
    layer_out, d_mixed, d_hidden, d_summed, back_part = call(
        mix_back_kernel,
        steps,
        info,
        [
            (mixed, node_spec),
            (hidden_slope, wide_spec),
            cot_in,
            (local_hat, node_spec),
            (global_hat, node_spec),
            sums_in,
            (tops, None),
            mats_in,
            vec_in,
        ],
        [
            node_bf,
            node_bf,
            ((rows, 2 * width), bf16, wide_spec),
            node_bf,
            sums_out,
        ],
    )

    def mat_out(number):
        return ((number, width, width), f32, None)

    def mat_acc(number):
        return pltpu.VMEM((number, width, width), f32)

    def inner_work(info):
        return call(
            inner_grad_kernel,
            steps,
            info,
            [(summed_low, node_spec), (d_hidden, wide_spec)],
            [mat_out(2)],
            [mat_acc(2)],
        )[0]

    def outer_work(info):
        return call(
            outer_grad_kernel,
            steps,
            info,
            [(hidden_low, wide_spec), (d_mixed, node_spec)],
            [mat_out(2)],
            [mat_acc(2)],
        )[0]

    backs, (inner_grads, outer_grads) = sum_small(back_part, total, info, [inner_work, outer_work])
    backs_in = (backs, None)
    dsum_in = (d_summed, node_spec)
    dnode_spec = rows_spec(tall, 4 * width)
    d_node, d_edge, local_bias, local_grads = call(
        local_back_kernel,
        steps,
        info,
        [
            dsum_in,
            (local_hat, node_spec),
            (gate_slope, node_spec),
            (recip, node_spec),
            (fall, node_spec),
            (opened, edge_spec),
            (bend, edge_spec),
            (b_source, edge_spec),
            (hot, edge_spec),
            (turned, edge_spec),
            x_in,
            e_in,
            sums_in,
            backs_in,
            vec_in,
        ],
        [
            ((rows, 4 * width), bf16, dnode_spec),
            ((edges, width), bf16, edge_spec),
            sums_out,
            mat_out(5),
        ],
        [mat_acc(5)],
    )
    dqkv_spec = rows_spec(tall, 3 * width)
    slots = total // 2
    packed = in_rows(total, width)
    grad_outs = [((MATS, width, width), bf16, None)]
    if packed:
        grad_outs = [((slots, MATS * 8, width), bf16, None)] * 2
    d_qkv, attend_bias, *grads = call(
        attend_back_kernel,
        steps,
        info,
        [
            dsum_in,
            (global_hat, node_spec),
            (attended, node_spec),
            (queries, node_spec),
            (keyed, node_spec),
            (valued, node_spec),
            (probs, prob_spec),
            x_in,
            sums_in,
            backs_in,
            mats_in,
            vec_in,
            (local_grads, None),
            (inner_grads, None),
            (outer_grads, None),
        ],
        [((rows, 3 * width), bf16, dqkv_spec), sums_out] + grad_outs,
        [mat_acc(4)],
    )
    def node_work(info):
        return call(
            node_grad_kernel,
            steps,
            info,
            [
                dsum_in,
                (local_hat, node_spec),
                (global_hat, node_spec),
                (d_node, dnode_spec),
                (d_qkv, dqkv_spec),
                sums_in,
                backs_in,
                mats_in,
                vec_in,
            ],
            [node_f32],
        )[0]

    def edge_work(info):
        return call(
            edge_grad_kernel,
            steps,
            info,
            [(d_edge, edge_spec), mats_in],
            [((edges, width), f32, edge_spec)],
        )[0]

    if packed:
        grad_shard, (node_grad, edge_grad) = scatter_packed(
            *grads, total, info, [node_work, edge_work]
        )
    else:
        grad_shard = scatter_plain(grads[0], total)
        node_grad, edge_grad = node_work(info), edge_work(info)
    square_row = jnp.broadcast_to(jnp.sum(grad_shard * grad_shard), (1, width))
    tail = sum_small(
        jnp.concatenate(
            [local_bias[:2], attend_bias[:3], square_row, jnp.zeros((2, width), f32)], axis=0
        ),
        total,
    )
    top_mean = tops[0:1] / sums[4:5]
    top_rstd = lax.rsqrt(tops[1:2] / sums[4:5] - top_mean * top_mean + eps_norm)
    vector_total = jnp.concatenate(
        [
            tail[:5],
            backs[1:2],
            backs[0:1],
            backs[2:3],
            backs[0:1],
            backs[3:6],
            (tops[3:4] - top_mean * tops[2:3]) * top_rstd,
            tops[2:3],
        ],
        axis=0,
    )
    grad_norm = jnp.sqrt(tail[5, 0] + jnp.sum(vector_total * vector_total))
    factor = jnp.minimum(1.0, clip_limit / (grad_norm + 1e-06))
    new_weights, first_w, second_w = adamw(
        weights, factor * grad_shard, weight_moment1, weight_moment2, rate_mats, decay_mats
    )
    new_vectors, first_v, second_v = adamw(
        vectors, factor * vector_total, vector_moment1, vector_moment2, rate_vecs, 0.0
    )
    return (
        layer_out,
        node_grad,
        edge_grad,
        new_weights,
        first_w,
        second_w,
        new_vectors,
        first_v,
        second_v,
        grad_norm,
    )


def solution(mesh):
    in_specs = (
        P("rows", None),
        P("rows", None),
        P(("rows", "branch"), None),
        P("rows"),
        P("rows"),
        P("rows"),
        P("rows"),
        P("rows"),
        P(None, ("rows", "branch")),
        P(None, ("rows", "branch")),
        P(None, ("rows", "branch")),
        P(),
        P(),
        P(),
    )
    out_specs = (
        P(("rows", "branch"), None),
        P(("rows", "branch"), None),
        P(("rows", "branch"), None),
        P(None, ("rows", "branch")),
        P(None, ("rows", "branch")),
        P(None, ("rows", "branch")),
        P(),
        P(),
        P(),
        P(),
    )
    return jax.shard_map(
        per_device, mesh=mesh, in_specs=in_specs, out_specs=out_specs, check_vma=False
    )
```

```python
import functools
import math

import jax
import jax.numpy as jnp
from jax import lax
from jax.experimental import pallas as pl
from jax.experimental.pallas import tpu as pltpu
from jax.sharding import PartitionSpec as P

HEADS = 8
BLOCK = 128
EB = 256
MATS = 13
STEP = 7
GROUP = 8

eps_norm = 1e-05
clip_limit = 1.0
beta_one = 0.9
beta_two = 0.999
rate_mats = 0.1
rate_vecs = 0.8
decay_mats = 0.01
adam_eps = 1e-08
hidden_floor = -1e30
axis_names = ("rows", "branch")
f32 = jnp.float32
bf16 = jnp.bfloat16


def mm(left, right):
    return jnp.dot(left, right, preferred_element_type=f32)


def mm_back(left, right):
    return lax.dot_general(left, right, (((1,), (1,)), ((), ())), preferred_element_type=f32)


def mm_rows(left, right):
    return lax.dot_general(left, right, (((0,), (0,)), ((), ())), preferred_element_type=f32)


def low(values):
    return values.astype(bf16)


def sig(values):
    return 0.5 * jnp.tanh(0.5 * values) + 0.5


def col_sum(values):
    return jnp.sum(values, axis=0, keepdims=True)


def live_of(info_ref, first_block, group, width):
    slot = lax.broadcasted_iota(jnp.int32, (BLOCK, width), 0)
    return jnp.concatenate(
        [
            jnp.where(slot < info_ref[1 + first_block + place], 1.0, 0.0)
            for place in range(group)
        ],
        axis=0,
    )


def nodes_of(place):
    return slice(place * BLOCK, (place + 1) * BLOCK)


def edges_of(place):
    return slice(place * EB, (place + 1) * EB)


def add_rows(out_ref, rows):
    @pl.when(pl.program_id(0) == 0)
    def _():
        out_ref[...] = jnp.zeros_like(out_ref)

    for place, row in enumerate(rows):
        out_ref[place : place + 1, :] += row


def norm_terms(sums, first, count_row):
    mean = sums[first : first + 1] / count_row
    rstd = lax.rsqrt(sums[first + 1 : first + 2] / count_row - mean * mean + eps_norm)
    return (mean, rstd)


def prep_kernel(info_ref, src_ref, dst_ref, mask_ref, id_ref, hot_ref, turned_ref, bias_ref):
    for place in range(GROUP):
        row = pl.ds(place, 1)
        node = lax.broadcasted_iota(jnp.int32, (BLOCK, EB), 0)
        live = mask_ref[0, row, :] != 0
        dst_rows = jnp.where((node == dst_ref[0, row, :]) & live, 1.0, 0.0)
        src_rows = jnp.where((node == src_ref[0, row, :]) & live, 1.0, 0.0)
        turned = jnp.concatenate([dst_rows, src_rows], axis=0)
        turned_ref[place * EB : (place + 1) * EB, :] = low(turned)
        hot_ref[place * EB : (place + 1) * EB, :] = low(turned.T)
        ids = jnp.broadcast_to(id_ref[0, row, :].astype(f32), (BLOCK, BLOCK))
        bias_ref[place * BLOCK : (place + 1) * BLOCK, :] = jnp.where(
            ids == ids.T, 0.0, hidden_floor
        )


def local_kernel(
    info_ref, x_ref, e_ref, hot_ref, turned_ref, w_ref, vec_ref,
    out_ref, slope_ref, recip_ref, fall_ref, open_ref, bend_ref, bsrc_ref, sums_ref,
):
    group = x_ref.shape[0] // BLOCK
    x = x_ref[...]
    a_part = mm(x, w_ref[0]) + vec_ref[0:1, :]
    b_part = low(mm(x, w_ref[1]))
    d_part = low(mm(x, w_ref[3]))
    e_part = low(mm(x, w_ref[4]))
    c_part = mm(e_ref[...], w_ref[2]) + vec_ref[1:2, :]
    gates = []
    picks = []
    for place in range(group):
        nodes = nodes_of(place)
        hot = hot_ref[edges_of(place), :]
        gates.append(mm(hot, jnp.concatenate([d_part[nodes], e_part[nodes]], axis=0)))
        picks.append(mm(hot[:, BLOCK:], b_part[nodes]))
    sums = []
    for place in range(group):
        edges = edges_of(place)
        opened = sig(c_part[edges] + gates[place])
        b_source = picks[place]
        opened_low = low(opened)
        open_ref[edges, :] = opened_low
        bend_ref[edges, :] = low(opened * (1.0 - opened))
        bsrc_ref[edges, :] = low(b_source)
        dst_turned = turned_ref[place * EB : place * EB + BLOCK, :]
        sums.append(
            mm(dst_turned, jnp.concatenate([low(opened * b_source), opened_low], axis=1))
        )
    both = jnp.concatenate(sums, axis=0)
    width = x.shape[1]
    recip = 1.0 / (both[:, width:] + 1.0)
    ratio = both[:, :width] * recip
    gated = a_part + ratio
    gated_sig = sig(gated)
    out = x.astype(f32) + gated * gated_sig
    slope_ref[...] = low(gated_sig * (1.0 + gated * (1.0 - gated_sig)))
    recip_ref[...] = low(recip)
    fall_ref[...] = low(ratio * recip)
    out_ref[...] = out
    live = live_of(info_ref, pl.program_id(0) * group, group, out.shape[1])
    kept = live * out
    add_rows(sums_ref, [col_sum(kept), col_sum(kept * out)])


def head_masks(width):
    head = lax.broadcasted_iota(jnp.int32, (16, width), 1) // (width // HEADS)
    return [low(jnp.where(head == place, 1.0, 0.0))[:1] for place in range(HEADS)]


def head_stack(values, masks):
    return jnp.concatenate([values * mask for mask in masks], axis=0)


def tall_masks(width):
    head = lax.broadcasted_iota(jnp.int32, (width, BLOCK), 0) // (width // HEADS)
    return [low(jnp.where(head == place, 1.0, 0.0)) for place in range(HEADS)]


def side_stack(turned, masks):
    return jnp.concatenate([turned * mask for mask in masks], axis=1)


def attend_kernel(
    info_ref, x_ref, bias_ref, w_ref, vec_ref,
    out_ref, q_ref, k_ref, v_ref, att_ref, prob_ref, sums_ref,
):
    group = x_ref.shape[0] // BLOCK
    x = x_ref[...]
    queries = low(mm(x, w_ref[5]) + vec_ref[2:3, :])
    keyed = low(mm(x, w_ref[6]))
    valued = low(mm(x, w_ref[7]) + vec_ref[3:4, :])
    q_ref[...] = queries
    k_ref[...] = keyed
    v_ref[...] = valued
    score_scale = (x.shape[1] // HEADS) ** (-0.5) * math.log2(math.e)
    masks = head_masks(x.shape[1])
    tall = tall_masks(x.shape[1])
    queries_turned = queries.T
    raws = [
        mm(keyed[nodes_of(place)], side_stack(queries_turned[:, nodes_of(place)], tall))
        for place in range(group)
    ]
    turns = []
    for place in range(group):
        nodes = nodes_of(place)
        bias = bias_ref[nodes, :]
        turned = []
        for head in range(HEADS):
            cols = nodes_of(head)
            part = raws[place][:, cols] + bias
            part = jnp.exp2((part - jnp.max(part, axis=0, keepdims=True)) * score_scale)
            part = low(part * (1.0 / jnp.sum(part, axis=0, keepdims=True)))
            prob_ref[nodes, cols] = part
            turned.append(part.T)
        turns.append(jnp.concatenate(turned, axis=1))
    for place in range(group):
        nodes = nodes_of(place)
        att_ref[nodes, :] = low(mm(turns[place], head_stack(valued[nodes], masks)))
    out = x.astype(f32) + mm(att_ref[...], w_ref[8]) + vec_ref[4:5, :]
    out_ref[...] = out
    live = live_of(info_ref, pl.program_id(0) * group, group, out.shape[1])
    kept = live * out
    add_rows(sums_ref, [col_sum(kept), col_sum(kept * out)])


def mix_kernel(
    info_ref, local_ref, global_ref, cot_ref, sums_ref, w_ref, vec_ref,
    low_ref, hlow_ref, slope_ref, lhat_ref, ghat_ref, mixed_ref, stat_ref,
):
    group = local_ref.shape[0] // BLOCK
    width = local_ref.shape[1]
    sums = sums_ref[...]
    count_row = sums[4:5]
    local_mean, local_rstd = norm_terms(sums, 0, count_row)
    global_mean, global_rstd = norm_terms(sums, 2, count_row)
    local_hat = (local_ref[...] - local_mean) * local_rstd
    global_hat = (global_ref[...] - global_mean) * global_rstd
    lhat_ref[...] = low(local_hat)
    ghat_ref[...] = low(global_hat)
    local_norm = local_hat * vec_ref[5:6, :] + vec_ref[6:7, :]
    global_norm = global_hat * vec_ref[7:8, :] + vec_ref[8:9, :]
    summed = low(local_norm).astype(f32) + low(global_norm).astype(f32)
    summed_low = low(summed)
    low_ref[...] = summed_low
    mixed = summed + vec_ref[11:12, :]
    for half in range(2):
        hidden = mm(summed_low, w_ref[9 + half]) + vec_ref[9 + half : 10 + half, :]
        sig_value = sig(hidden)
        hidden_low = low(hidden * sig_value)
        hlow_ref[:, half * width : (half + 1) * width] = hidden_low
        slope_ref[:, half * width : (half + 1) * width] = low(
            sig_value * (1.0 + hidden * (1.0 - sig_value))
        )
        mixed = mixed + mm(hidden_low, w_ref[11 + half])
    mixed_ref[...] = mixed
    live = live_of(info_ref, pl.program_id(0) * group, group, width)
    kept = live * mixed
    d_norm = live * cot_ref[...].astype(f32)
    add_rows(
        stat_ref, [col_sum(kept), col_sum(kept * mixed), col_sum(d_norm), col_sum(d_norm * mixed)]
    )


def mix_back_kernel(
    info_ref, mixed_ref, slope_ref, cot_ref, lhat_ref, ghat_ref, sums_ref, tops_ref, w_ref,
    vec_ref,
    dmix_ref, dhid_ref, dsum_ref, stat_ref,
):
    group = mixed_ref.shape[0] // BLOCK
    width = mixed_ref.shape[1]
    sums = sums_ref[...]
    tops = tops_ref[...]
    count_row = sums[4:5]
    mean, rstd = norm_terms(tops, 0, count_row)
    live = live_of(info_ref, pl.program_id(0) * group, group, width)
    hat = (mixed_ref[...] - mean) * rstd
    d_norm = live * cot_ref[...].astype(f32)
    dz_sum = tops[2:3]
    dz_hat = (tops[3:4] - mean * dz_sum) * rstd
    d_mixed = (vec_ref[12:13, :] * rstd) * (
        d_norm - live * (dz_sum / count_row + hat * (dz_hat / count_row))
    )
    d_mixed_low = low(d_mixed)
    dmix_ref[...] = d_mixed_low
    d_summed = d_mixed
    for half in range(2):
        cols = slice(half * width, (half + 1) * width)
        d_hidden = low(mm_back(d_mixed_low, w_ref[11 + half]) * slope_ref[:, cols].astype(f32))
        dhid_ref[:, cols] = d_hidden
        d_summed = d_summed + mm_back(d_hidden, w_ref[9 + half])
    d_low = low(d_summed)
    dsum_ref[...] = d_low
    d_sum = d_low.astype(f32)
    add_rows(
        stat_ref,
        [
            col_sum(d_sum),
            col_sum(d_sum * lhat_ref[...].astype(f32)),
            col_sum(d_sum * ghat_ref[...].astype(f32)),
            col_sum(d_mixed),
        ],
    )


def accumulate(acc_ref, term):
    @pl.when(pl.program_id(0) == 0)
    def _():
        acc_ref[...] = jnp.zeros_like(acc_ref)

    acc_ref[...] += term


def layer_kernel(info_ref, mixed_ref, sums_ref, tops_ref, vec_ref, layer_ref):
    group = mixed_ref.shape[0] // BLOCK
    mean, rstd = norm_terms(tops_ref[...], 0, sums_ref[4:5, :])
    live = live_of(info_ref, pl.program_id(0) * group, group, mixed_ref.shape[1])
    hat = (mixed_ref[...] - mean) * rstd
    layer_ref[...] = low(live * (vec_ref[12:13, :] * hat + vec_ref[13:14, :]))


def ones_sum(ref, cols):
    return mm(jnp.ones((8, ref.shape[0]), bf16), ref[:, cols])


def inner_grad_kernel(info_ref, slow_ref, dhid_ref, out_ref, bias_ref):
    accumulate(out_ref, mm_rows(slow_ref[...], dhid_ref[...]))
    accumulate(bias_ref, ones_sum(dhid_ref, slice(None)))


def outer_grad_kernel(info_ref, hlow_ref, dmix_ref, out_ref):
    accumulate(out_ref, mm_rows(hlow_ref[...], dmix_ref[...]))


def norm_back(info_ref, dsum_ref, hat_ref, sums, backs, first, gain_row, hat_row):
    group = hat_ref.shape[0] // BLOCK
    count_row = sums[4:5]
    rstd = norm_terms(sums, first, count_row)[1]
    live = live_of(info_ref, pl.program_id(0) * group, group, hat_ref.shape[1])
    hat = hat_ref[...].astype(f32)
    return (gain_row * rstd) * (
        dsum_ref[...].astype(f32)
        - live * (backs[0:1] / count_row + hat * (backs[hat_row : hat_row + 1] / count_row))
    )


def local_back_kernel(
    info_ref, dsum_ref, local_ref, slope_ref, recip_ref, fall_ref, open_ref, bend_ref, bsrc_ref,
    hot_ref, turned_ref, sums_ref, backs_ref, vec_ref,
    dnode_ref, dedge_ref, stat_ref,
):
    group = local_ref.shape[0] // BLOCK
    width = local_ref.shape[1]
    d_local = norm_back(
        info_ref, dsum_ref, local_ref, sums_ref[...], backs_ref[...], 0, vec_ref[5:6, :], 1
    )
    d_gated = d_local * slope_ref[...].astype(f32)
    dnode_ref[:, :width] = low(d_gated)
    d_num = low(d_gated * recip_ref[...].astype(f32))
    d_den = low(-d_gated * fall_ref[...].astype(f32))
    pre_row = jnp.zeros((1, width), f32)
    picks = [
        mm(
            hot_ref[edges_of(place), :BLOCK],
            jnp.concatenate([d_num[nodes_of(place)], d_den[nodes_of(place)]], axis=1),
        )
        for place in range(group)
    ]
    sources = []
    for place in range(group):
        edges = edges_of(place)
        d_message = picks[place][:, :width]
        d_open = d_message * bsrc_ref[edges, :].astype(f32) + picks[place][:, width:]
        sources.append(low(d_message * open_ref[edges, :].astype(f32)))
        d_pre = d_open * bend_ref[edges, :].astype(f32)
        pre_row = pre_row + col_sum(d_pre)
        dedge_ref[edges, :] = low(d_pre)
    for place in range(group):
        nodes = nodes_of(place)
        turned = turned_ref[edges_of(place), :]
        d_both = low(mm(turned, dedge_ref[edges_of(place), :]))
        dnode_ref[nodes, width : 2 * width] = low(mm(turned[BLOCK:], sources[place]))
        dnode_ref[nodes, 2 * width : 3 * width] = d_both[:BLOCK]
        dnode_ref[nodes, 3 * width :] = d_both[BLOCK:]
    add_rows(stat_ref, [col_sum(d_gated), pre_row])


def attend_back_kernel(
    info_ref, dsum_ref, global_ref, q_ref, k_ref, v_ref, prob_ref, sums_ref,
    backs_ref, w_ref, vec_ref,
    dqkv_ref, dlow_ref, stat_ref,
):
    group = global_ref.shape[0] // BLOCK
    width = global_ref.shape[1]
    score_scale = (width // HEADS) ** (-0.5)
    d_global = norm_back(
        info_ref, dsum_ref, global_ref, sums_ref[...], backs_ref[...], 2, vec_ref[7:8, :], 2
    )
    d_low = low(d_global)
    dlow_ref[...] = d_low
    d_att = low(mm_back(d_low, w_ref[8]))
    masks = head_masks(width)
    tall = tall_masks(width)
    turned_att = low(mm_back(w_ref[8], d_low))
    d_probs = [
        mm(v_ref[nodes_of(place), :], side_stack(turned_att[:, nodes_of(place)], tall))
        for place in range(group)
    ]
    straights = []
    turns = []
    for place in range(group):
        nodes = nodes_of(place)
        straight = []
        turned = []
        for head in range(HEADS):
            cols = nodes_of(head)
            prob = prob_ref[nodes, cols].astype(f32)
            part = d_probs[place][:, cols]
            inner = jnp.sum(prob * part, axis=0, keepdims=True)
            d_score = low(prob * ((part - inner) * score_scale))
            straight.append(d_score)
            turned.append(d_score.T)
        straights.append(jnp.concatenate(straight, axis=1))
        turns.append(jnp.concatenate(turned, axis=1))
    for place in range(group):
        nodes = nodes_of(place)
        dqkv_ref[nodes, :width] = low(mm(turns[place], head_stack(k_ref[nodes, :], masks)))
        dqkv_ref[nodes, width : 2 * width] = low(
            mm(straights[place], head_stack(q_ref[nodes, :], masks))
        )
        dqkv_ref[nodes, 2 * width :] = low(
            mm(prob_ref[nodes, :], head_stack(d_att[nodes], masks))
        )
    add_rows(
        stat_ref,
        [
            col_sum(d_global),
        ],
    )


def branch_grad_kernel(
    info_ref, x_ref, e_ref, att_ref, dnode_ref, dedge_ref, dqkv_ref, dlow_ref, igrad_ref, ograd_ref,
    *outs,
):
    outs, bias_ref, (node_ref, wide_ref, edge_ref, acc_ref) = outs[:-5], outs[-5], outs[-4:]
    width = x_ref.shape[1]
    for place in (0, 2):
        bias_ref[:, place // 2 * width : (place // 2 + 1) * width] = ones_sum(
            dqkv_ref, slice(place * width, (place + 1) * width)
        )
    x = x_ref[...]
    node_ref[...] = mm_rows(x, dnode_ref[...])
    wide_ref[...] = mm_rows(x, dqkv_ref[...])
    edge_ref[...] = mm_rows(e_ref[...], dedge_ref[...])
    acc_ref[...] = mm_rows(att_ref[...], dlow_ref[...])
    cols = [slice(place * width, (place + 1) * width) for place in range(4)]
    parts = [node_ref.at[:, cols[0]], node_ref.at[:, cols[1]], edge_ref]
    parts = parts + [node_ref.at[:, cols[2]], node_ref.at[:, cols[3]]]
    parts = parts + [wide_ref.at[:, cols[place]] for place in range(3)] + [acc_ref]
    parts = parts + [igrad_ref.at[:, cols[place]] for place in range(2)]
    parts = parts + [ograd_ref.at[cols[place], :] for place in range(2)]
    if len(outs) == 1:
        for place, part in enumerate(parts):
            outs[0][place] = low(part[...])
    else:
        pack(info_ref, parts, outs[0], outs[1])


def reach(order, index):
    found = 0
    for place, step in enumerate(order):
        if index >> (len(order) - 1 - place) & 1:
            found ^= step >> 1
    return found


def chip_orders(total):
    chips = steps_of(total)[1:]
    return (chips, chips[1:-1] + chips[:1] + chips[-1:])


def pack(info_ref, parts, keep_ref, send_ref):
    slots = keep_ref.shape[0]
    orders = chip_orders(2 * slots)
    core = info_ref[info_ref.shape[0] - 2]
    chip = info_ref[info_ref.shape[0] - 1]
    for slot in range(slots):
        near = [reach(order, slot) for order in orders]
        for out_ref, owner in ((keep_ref, core), (send_ref, 1 - core)):
            step = jnp.where(owner == 0, near[0], near[1])
            row = pl.multiple_of(16 * jnp.bitwise_xor(chip, step) + 8 * owner, 8)
            for first in range(0, len(parts), 2):
                pair = [part[pl.ds(row, 8), :] for part in parts[first : first + 2]]
                out_ref[slot, first * 8 : first * 8 + 8 * len(pair), :] = low(
                    jnp.concatenate(pair, axis=0)
                )


def assemble_kernel(info_ref, held_ref, other_ref, out_ref):
    slots, tall, _ = held_ref.shape
    orders = chip_orders(2 * slots)
    core = info_ref[info_ref.shape[0] - 2]
    chip = info_ref[info_ref.shape[0] - 1]

    def fill(even_ref, odd_ref):
        for far in range(slots):
            even, odd = [
                [slot for slot in range(slots) if reach(order, slot) == far][0] for order in orders
            ]
            row = pl.multiple_of(16 * jnp.bitwise_xor(chip, far), 16)
            for first in range(0, tall, 16):
                size = min(16, tall - first)
                upper = even_ref[even, first : first + size, :].astype(f32)
                lower = odd_ref[odd, first : first + size, :].astype(f32)
                for half in range(size // 8):
                    rows = slice(half * 8, half * 8 + 8)
                    out_ref[first // 8 + half, pl.ds(row, 16), :] = low(
                        jnp.concatenate([upper[rows], lower[rows]], axis=0)
                    )

    @pl.when(core == 0)
    def _():
        fill(held_ref, other_ref)

    @pl.when(core != 0)
    def _():
        fill(other_ref, held_ref)


def node_grad_kernel(
    info_ref, dsum_ref, lhat_ref, ghat_ref, dnode_ref, dqkv_ref, sums_ref, backs_ref, w_ref,
    vec_ref,
    node_ref,
):
    width = lhat_ref.shape[1]
    sums = sums_ref[...]
    backs = backs_ref[...]
    total = norm_back(info_ref, dsum_ref, lhat_ref, sums, backs, 0, vec_ref[5:6, :], 1)
    total = total + norm_back(info_ref, dsum_ref, ghat_ref, sums, backs, 2, vec_ref[7:8, :], 2)
    for place, mat in enumerate((0, 1, 3, 4)):
        total = total + mm_back(dnode_ref[:, place * width : (place + 1) * width], w_ref[mat])
    for place in range(3):
        total = total + mm_back(dqkv_ref[:, place * width : (place + 1) * width], w_ref[5 + place])
    node_ref[...] = total


def edge_grad_kernel(info_ref, dedge_ref, w_ref, edge_ref):
    edge_ref[...] = mm_back(dedge_ref[...], w_ref[2])


def square_kernel(
    info_ref, kept_ref, got_ref, local_ref, attend_ref, inner_ref, wide_ref, grad_ref, tail_ref
):
    width = tail_ref.shape[1]
    grad = kept_ref[...].astype(f32) + got_ref[...].astype(f32)
    half = grad.shape[1] // 2
    grad_ref[0] = grad[:, :half]
    grad_ref[1] = grad[:, half:]
    squares = grad * grad
    square = jnp.sum(jnp.sum(squares, axis=0, keepdims=True), axis=1, keepdims=True)
    tail_ref[0:2, :] = local_ref[0:2, :]
    tail_ref[2:3, :] = wide_ref[0:1, :width]
    tail_ref[3:4, :] = wide_ref[0:1, width:]
    tail_ref[4:5, :] = attend_ref[0:1, :]
    tail_ref[5:6, :] = inner_ref[0:1, :width]
    tail_ref[6:7, :] = inner_ref[0:1, width:]
    tail_ref[7:8, :] = jnp.broadcast_to(square, (1, width))


def update_kernel(
    info_ref, grad_ref, tail_ref, sums_ref, tops_ref, backs_ref, w_ref, w1_ref, w2_ref, v_ref,
    v1_ref, v2_ref,
    new_w_ref, new_w1_ref, new_w2_ref, new_v_ref, new_v1_ref, new_v2_ref, norm_ref,
):
    tail = tail_ref[...]
    tops = tops_ref[...]
    backs = backs_ref[...]
    mean, rstd = norm_terms(tops, 0, sums_ref[4:5, :])
    grad_v = jnp.concatenate(
        [
            tail[0:5],
            backs[1:2],
            backs[0:1],
            backs[2:3],
            backs[0:1],
            tail[5:7],
            backs[3:4],
            (tops[3:4] - mean * tops[2:3]) * rstd,
            tops[2:3],
        ],
        axis=0,
    )
    square = jnp.sum(jnp.sum(grad_v * grad_v, axis=0, keepdims=True), axis=1, keepdims=True)
    norm = jnp.sqrt(tail[7:8, 0:1] + square)
    norm_ref[...] = norm
    factor = jnp.minimum(1.0, clip_limit / (norm + 1e-06))
    new_v_ref[...], new_v1_ref[...], new_v2_ref[...] = adamw(
        v_ref[...], factor * grad_v, v1_ref[...], v2_ref[...], rate_vecs, 0.0
    )
    mats, span = w_ref.shape
    _, rows, half = grad_ref.shape
    for piece in range(span // half):
        cols = slice(piece * half, (piece + 1) * half)
        if rows == mats:
            grad = grad_ref[piece]
        else:
            grad = grad_ref[piece % 2, pl.ds(piece // 2, mats, rows // mats), :]
        new_w_ref[:, cols], new_w1_ref[:, cols], new_w2_ref[:, cols] = adamw(
            w_ref[:, cols], factor * grad, w1_ref[:, cols], w2_ref[:, cols], rate_mats, decay_mats
        )


def rows_spec(rows, width, offset=0):
    if offset:
        return pl.BlockSpec((rows, width), lambda step, info: (step + info[0], 0))
    return pl.BlockSpec((rows, width), lambda step, info: (step, 0))


def whole_spec(shape):
    zeros = (0,) * len(shape)
    return pl.BlockSpec(shape, lambda step, info: zeros)


def call(kernel, steps, info, inputs, outputs, scratch=(), room=12, cost=5):
    in_specs = []
    arrays = []
    for array, spec in inputs:
        arrays.append(array)
        in_specs.append(whole_spec(array.shape) if spec is None else spec)
    out_specs = []
    out_shapes = []
    for shape, dtype, spec, *far in outputs:
        out_specs.append(whole_spec(shape) if spec is None else spec)
        out_shapes.append(pltpu.HBM(shape, dtype) if far else jax.ShapeDtypeStruct(shape, dtype))
    return pl.pallas_call(
        kernel,
        grid_spec=pltpu.PrefetchScalarGridSpec(
            num_scalar_prefetch=1,
            grid=(steps,),
            in_specs=in_specs,
            out_specs=out_specs,
            scratch_shapes=list(scratch),
        ),
        out_shape=out_shapes,
        compiler_params=pltpu.CompilerParams(
            dimension_semantics=("arbitrary",), vmem_limit_bytes=room * 1024 * 1024
        ),
        name=kernel.__name__,
        cost_estimate=pl.CostEstimate(
            flops=cost * 1000000000, bytes_accessed=cost * 1000000, transcendentals=0
        ),
    )(info, *arrays)


def swap_with(values, step, total):
    return lax.ppermute(values, axis_names, [(place, place ^ step) for place in range(total)])


def steps_of(total):
    return [1 << power for power in range(total.bit_length() - 1)]


def beside(start, transfer, info, work):
    info = lax.optimization_barrier((info, start))[0]
    return lax.optimization_barrier((transfer, work(info)))


def sum_small(values, total, info=None, works=()):
    results = []
    works = list(works)
    for step in steps_of(total):
        other = swap_with(values, step, total)
        if works and step > 1:
            other, done = beside(values, other, info, works.pop(0))
            results.append(done)
        values = values + other
    return (values, results) if results else values


def swap_chips(values, number, total):
    orders = chip_orders(total)
    return lax.ppermute(
        values,
        axis_names,
        [(place, place ^ orders[place % 2][number]) for place in range(total)],
    )


def in_rows(total, width):
    return width * width // total == 8 * width


def gather_matrices(shard, info, total, width, work):
    mats = shard.shape[0]
    if not in_rows(total, width):
        gathered = lax.all_gather(shard, axis_names, axis=1, tiled=True)
        return (gathered.reshape(mats, width, width), work(info))
    held = shard.reshape(1, mats * 8, width)
    for number in reversed(range(len(chip_orders(total)[0]))):
        got = swap_chips(held, number, total)
        if number == 0:
            got, done = beside(held, got, info, work)
        held = jnp.concatenate([held, got], axis=0)
    other = swap_with(held, 1, total)
    matrices = call(
        assemble_kernel,
        1,
        info,
        [(held, None), (other, None)],
        [((mats, width, width), bf16, None)],
    )[0]
    return (matrices, done)


def scatter_plain(grads, total):
    place = lax.axis_index(axis_names)
    mats, width, _ = grads.shape
    bits = total.bit_length() - 1
    held = grads.reshape((mats,) + (2,) * bits + (width * width // total,))
    held = held.transpose(tuple(reversed(range(1, bits + 1))) + (0, bits + 1))
    for step in steps_of(total):
        mine = ((place & step) != 0).astype(jnp.int32)
        sent = lax.dynamic_index_in_dim(held, 1 - mine, 0, keepdims=False)
        kept = lax.dynamic_index_in_dim(held, mine, 0, keepdims=False)
        got = swap_with(sent, step, total)
        if step * 2 < total:
            held = low(kept.astype(f32) + got.astype(f32))
    return (kept, got)


def scatter_packed(kept, sent, total, info, works):
    got = swap_with(sent, 1, total)
    results = []
    for number in range(len(chip_orders(total)[0])):
        half = kept.shape[0] // 2
        sent = low(kept[half:].astype(f32) + got[half:].astype(f32))
        kept = kept[:half].astype(f32) + got[:half].astype(f32)
        got = swap_chips(sent, number, total)
        if number < len(works):
            got, done = beside(sent, got, info, works[number])
            results.append(done)
    return ((kept[0], got[0]), results)


def adamw(params, gradient, moment_one, moment_two, rate, decay):
    first = beta_one * moment_one + (1.0 - beta_one) * gradient
    second = beta_two * moment_two + (1.0 - beta_two) * gradient * gradient
    first_hat = first / (1.0 - beta_one**STEP)
    second_hat = second / (1.0 - beta_two**STEP)
    updated = params - rate * (first_hat / (jnp.sqrt(second_hat) + adam_eps) + decay * params)
    return (updated, first, second)


def own_half(values, branch_index):
    half = values.shape[0] // 2
    return lax.dynamic_slice_in_dim(values, branch_index * half, half, 0)


def per_device(
    node_feats,
    edge_feats,
    cotangent,
    graph_ids,
    node_mask,
    edge_src,
    edge_dst,
    edge_mask,
    weights,
    weight_moment1,
    weight_moment2,
    vectors,
    vector_moment1,
    vector_moment2,
):
    total = lax.axis_size("rows") * lax.axis_size("branch")
    branch_index = lax.axis_index("branch")
    width = node_feats.shape[1]
    rows = node_feats.shape[0] // 2
    edges = edge_feats.shape[0] // 2
    blocks = rows // BLOCK
    group = math.gcd(blocks, GROUP)
    steps = blocks // group
    tall = group * BLOCK
    tall_edges = group * EB
    w_bf = low(weights)
    counts = jnp.sum(own_half(node_mask, branch_index).reshape(blocks, BLOCK), axis=1)
    info = jnp.concatenate(
        [(branch_index * steps)[None], counts, branch_index[None], lax.axis_index("rows")[None]]
    ).astype(jnp.int32)

    def by_step(values, slots):
        return own_half(values, branch_index).reshape(steps, group, slots)

    def step_spec(slots):
        return pl.BlockSpec((1, group, slots), lambda step, info: (step, 0, 0))

    edge_spec = rows_spec(tall_edges, width)
    node_spec = rows_spec(tall, width)
    def prep_work(info):
        return call(
            prep_kernel,
            steps,
            info,
            [
                (by_step(edge_src, EB), step_spec(EB)),
                (by_step(edge_dst, EB), step_spec(EB)),
                (by_step(edge_mask, EB), step_spec(EB)),
                (by_step(graph_ids, BLOCK), step_spec(BLOCK)),
            ],
            [
                ((edges, EB), bf16, edge_spec, True),
                ((edges, EB), bf16, edge_spec, True),
                ((rows, BLOCK), f32, rows_spec(tall, BLOCK)),
            ],
        )

    matrices, (hot, turned, bias) = gather_matrices(w_bf, info, total, width, prep_work)
    x_in = (node_feats, rows_spec(tall, width, 1))
    e_in = (edge_feats, rows_spec(tall_edges, width, 1))
    mats_in = (matrices, None)
    vec_in = (vectors, None)
    node_f32 = ((rows, width), f32, node_spec)
    node_bf = ((rows, width), bf16, node_spec)
    sums_out = ((8, width), f32, None)
    local_out, gate_slope, recip, fall, opened, bend, b_source, local_sums = call(
        local_kernel,
        steps,
        info,
        [x_in, e_in, (hot, edge_spec), (turned, edge_spec), mats_in, vec_in],
        [
            node_f32,
            node_bf,
            node_bf,
            node_bf,
            ((edges, width), bf16, edge_spec),
            ((edges, width), bf16, edge_spec),
            ((edges, width), bf16, edge_spec),
            sums_out,
        ],
    )
    prob_spec = rows_spec(tall, HEADS * BLOCK)
    global_out, queries, keyed, valued, attended, probs, global_sums = call(
        attend_kernel,
        steps,
        info,
        [x_in, (bias, rows_spec(tall, BLOCK)), mats_in, vec_in],
        [
            node_f32,
            node_bf,
            node_bf,
            node_bf,
            node_bf,
            ((rows, HEADS * BLOCK), bf16, prob_spec),
            sums_out,
        ],
    )
    count_row = jnp.full((1, width), jnp.sum(counts).astype(f32))
    sums = sum_small(
        jnp.concatenate(
            [local_sums[:2], global_sums[:2], count_row, jnp.zeros((3, width), f32)], axis=0
        ),
        total,
    )
    sums_in = (sums, None)
    cot_in = (cotangent, node_spec)
    wide_spec = rows_spec(tall, 2 * width)
    summed_low, hidden_low, hidden_slope, local_hat, global_hat, mixed, top_part = call(
        mix_kernel,
        steps,
        info,
        [(local_out, node_spec), (global_out, node_spec), cot_in, sums_in, mats_in, vec_in],
        [
            node_bf,
            ((rows, 2 * width), bf16, wide_spec),
            ((rows, 2 * width), bf16, wide_spec),
            node_bf,
            node_bf,
            node_f32,
            sums_out,
        ],
    )
    tops = sum_small(top_part, total)
    d_mixed, d_hidden, d_summed, back_part = call(
        mix_back_kernel,
        steps,
        info,
        [
            (mixed, node_spec),
            (hidden_slope, wide_spec),
            cot_in,
            (local_hat, node_spec),
            (global_hat, node_spec),
            sums_in,
            (tops, None),
            mats_in,
            vec_in,
        ],
        [
            node_bf,
            ((rows, 2 * width), bf16, wide_spec),
            node_bf,
            sums_out,
        ],
    )

    def mat_out(tall_by, wide_by):
        return ((tall_by * width, wide_by * width), f32, None)

    def inner_work(info):
        return call(
            inner_grad_kernel,
            steps,
            info,
            [(summed_low, node_spec), (d_hidden, wide_spec)],
            [mat_out(1, 2), ((8, 2 * width), f32, None)],
        )

    def outer_work(info):
        return call(
            outer_grad_kernel,
            steps,
            info,
            [(hidden_low, wide_spec), (d_mixed, node_spec)],
            [mat_out(2, 1)],
        )[0]

    def layer_work(info):
        return call(
            layer_kernel,
            steps,
            info,
            [(mixed, node_spec), sums_in, (tops, None), vec_in],
            [node_bf],
        )[0]

    backs, ((inner_grads, inner_bias), outer_grads, layer_out) = sum_small(
        back_part, total, info, [inner_work, outer_work, layer_work]
    )
    backs_in = (backs, None)
    dsum_in = (d_summed, node_spec)
    dnode_spec = rows_spec(tall, 4 * width)
    d_node, d_edge, local_bias = call(
        local_back_kernel,
        steps,
        info,
        [
            dsum_in,
            (local_hat, node_spec),
            (gate_slope, node_spec),
            (recip, node_spec),
            (fall, node_spec),
            (opened, edge_spec),
            (bend, edge_spec),
            (b_source, edge_spec),
            (hot, edge_spec),
            (turned, edge_spec),
            sums_in,
            backs_in,
            vec_in,
        ],
        [
            ((rows, 4 * width), bf16, dnode_spec),
            ((edges, width), bf16, edge_spec),
            sums_out,
        ],
    )
    dqkv_spec = rows_spec(tall, 3 * width)
    slots = total // 2
    packed = in_rows(total, width)
    grad_outs = [((MATS, width, width), bf16, None)]
    if packed:
        grad_outs = [((slots, MATS * 8, width), bf16, None)] * 2
    d_qkv, d_low, attend_bias = call(
        attend_back_kernel,
        steps,
        info,
        [
            dsum_in,
            (global_hat, node_spec),
            (queries, node_spec),
            (keyed, node_spec),
            (valued, node_spec),
            (probs, prob_spec),
            sums_in,
            backs_in,
            mats_in,
            vec_in,
        ],
        [((rows, 3 * width), bf16, dqkv_spec), node_bf, sums_out],
    )
    *grads, wide_bias = call(
        branch_grad_kernel,
        1,
        info,
        [
            (node_feats, pl.BlockSpec((rows, width), lambda step, info: (info[0] // steps, 0))),
            (edge_feats, pl.BlockSpec((edges, width), lambda step, info: (info[0] // steps, 0))),
            (attended, None),
            (d_node, None),
            (d_edge, None),
            (d_qkv, None),
            (d_low, None),
            (inner_grads, None),
            (outer_grads, None),
        ],
        grad_outs + [((8, 2 * width), f32, None)],
        [
            pltpu.VMEM((width, 4 * width), f32),
            pltpu.VMEM((width, 3 * width), f32),
            pltpu.VMEM((width, width), f32),
            pltpu.VMEM((width, width), f32),
        ],
    )

    def node_work(info):
        return call(
            node_grad_kernel,
            steps,
            info,
            [
                dsum_in,
                (local_hat, node_spec),
                (global_hat, node_spec),
                (d_node, dnode_spec),
                (d_qkv, dqkv_spec),
                sums_in,
                backs_in,
                mats_in,
                vec_in,
            ],
            [node_f32],
        )[0]

    def edge_work(info):
        return call(
            edge_grad_kernel,
            steps,
            info,
            [(d_edge, edge_spec), mats_in],
            [((edges, width), f32, edge_spec)],
        )[0]

    if packed:
        grad_shard, (node_grad, edge_grad) = scatter_packed(
            *grads, total, info, [node_work, edge_work]
        )
    else:
        grad_shard = scatter_plain(grads[0], total)
        node_grad, edge_grad = node_work(info), edge_work(info)
    grad_rows, tail_part = call(
        square_kernel,
        1,
        info,
        [(part, None) for part in grad_shard]
        + [(local_bias, None), (attend_bias, None), (inner_bias, None), (wide_bias, None)],
        [((2, grad_shard[0].shape[0], grad_shard[0].shape[1] // 2), f32, None), sums_out],
    )
    tail = sum_small(tail_part, total)
    like_mats = (weights.shape, f32, None)
    like_vecs = (vectors.shape, f32, None)
    new_weights, first_w, second_w, new_vectors, first_v, second_v, norm = call(
        update_kernel,
        1,
        info,
        [
            (array, None)
            for array in (
                grad_rows, tail, sums, tops, backs, weights, weight_moment1, weight_moment2,
                vectors, vector_moment1, vector_moment2,
            )
        ],
        [like_mats] * 3 + [like_vecs] * 3 + [((1, 1), f32, None)],
    )
    grad_norm = norm.reshape(())
    return (
        layer_out,
        node_grad,
        edge_grad,
        new_weights,
        first_w,
        second_w,
        new_vectors,
        first_v,
        second_v,
        grad_norm,
    )


def solution(mesh):
    in_specs = (
        P("rows", None),
        P("rows", None),
        P(("rows", "branch"), None),
        P("rows"),
        P("rows"),
        P("rows"),
        P("rows"),
        P("rows"),
        P(None, ("rows", "branch")),
        P(None, ("rows", "branch")),
        P(None, ("rows", "branch")),
        P(),
        P(),
        P(),
    )
    out_specs = (
        P(("rows", "branch"), None),
        P(("rows", "branch"), None),
        P(("rows", "branch"), None),
        P(None, ("rows", "branch")),
        P(None, ("rows", "branch")),
        P(None, ("rows", "branch")),
        P(),
        P(),
        P(),
        P(),
    )
    return jax.shard_map(
        per_device, mesh=mesh, in_specs=in_specs, out_specs=out_specs, check_vma=False
    )
```

```python
import functools
import math

import jax
import jax.numpy as jnp
from jax import lax
from jax.experimental import pallas as pl
from jax.experimental.pallas import tpu as pltpu
from jax.sharding import PartitionSpec as P

HEADS = 8
BLOCK = 128
EB = 256
MATS = 13
STEP = 7
GROUP = 8

eps_norm = 1e-05
clip_limit = 1.0
beta_one = 0.9
beta_two = 0.999
rate_mats = 0.1
rate_vecs = 0.8
decay_mats = 0.01
adam_eps = 1e-08
hidden_floor = -1e30
axis_names = ("rows", "branch")
f32 = jnp.float32
bf16 = jnp.bfloat16


def mm(left, right):
    return jnp.dot(left, right, preferred_element_type=f32)


def mm_back(left, right):
    return lax.dot_general(left, right, (((1,), (1,)), ((), ())), preferred_element_type=f32)


def mm_rows(left, right):
    return lax.dot_general(left, right, (((0,), (0,)), ((), ())), preferred_element_type=f32)


def low(values):
    return values.astype(bf16)


def sig(values):
    return 0.5 * jnp.tanh(0.5 * values) + 0.5


def col_sum(values):
    return jnp.sum(values, axis=0, keepdims=True)


def live_of(info_ref, first_block, group, width):
    slot = lax.broadcasted_iota(jnp.int32, (BLOCK, width), 0)
    return jnp.concatenate(
        [
            jnp.where(slot < info_ref[1 + first_block + place], 1.0, 0.0)
            for place in range(group)
        ],
        axis=0,
    )


def nodes_of(place):
    return slice(place * BLOCK, (place + 1) * BLOCK)


def edges_of(place):
    return slice(place * EB, (place + 1) * EB)


def add_rows(out_ref, rows):
    @pl.when(pl.program_id(0) == 0)
    def _():
        out_ref[...] = jnp.zeros_like(out_ref)

    for place, row in enumerate(rows):
        out_ref[place : place + 1, :] += row


def norm_terms(sums, first, count_row):
    mean = sums[first : first + 1] / count_row
    rstd = lax.rsqrt(sums[first + 1 : first + 2] / count_row - mean * mean + eps_norm)
    return (mean, rstd)


def prep_kernel(info_ref, src_ref, dst_ref, mask_ref, id_ref, hot_ref, turned_ref, bias_ref):
    for place in range(GROUP):
        row = pl.ds(place, 1)
        node = lax.broadcasted_iota(jnp.int32, (BLOCK, EB), 0)
        live = mask_ref[0, row, :] != 0
        dst_rows = jnp.where((node == dst_ref[0, row, :]) & live, 1.0, 0.0)
        src_rows = jnp.where((node == src_ref[0, row, :]) & live, 1.0, 0.0)
        turned = jnp.concatenate([dst_rows, src_rows], axis=0)
        turned_ref[place * EB : (place + 1) * EB, :] = low(turned)
        hot_ref[place * EB : (place + 1) * EB, :] = low(turned.T)
        ids = jnp.broadcast_to(id_ref[0, row, :].astype(f32), (BLOCK, BLOCK))
        bias_ref[place * BLOCK : (place + 1) * BLOCK, :] = jnp.where(
            ids == ids.T, 0.0, hidden_floor
        )


def local_kernel(
    info_ref, x_ref, e_ref, hot_ref, turned_ref, w_ref, vec_ref, other_ref,
    out_ref, slope_ref, recip_ref, fall_ref, open_ref, bend_ref, bsrc_ref, sums_ref,
):
    group = x_ref.shape[0] // BLOCK
    x = x_ref[...]
    a_part = mm(x, w_ref[0]) + vec_ref[0:1, :]
    b_part = low(mm(x, w_ref[1]))
    d_part = low(mm(x, w_ref[3]))
    e_part = low(mm(x, w_ref[4]))
    c_part = mm(e_ref[...], w_ref[2]) + vec_ref[1:2, :]
    gates = []
    picks = []
    for place in range(group):
        nodes = nodes_of(place)
        hot = hot_ref[edges_of(place), :]
        gates.append(mm(hot, jnp.concatenate([d_part[nodes], e_part[nodes]], axis=0)))
        picks.append(mm(hot[:, BLOCK:], b_part[nodes]))
    sums = []
    for place in range(group):
        edges = edges_of(place)
        opened = sig(c_part[edges] + gates[place])
        b_source = picks[place]
        opened_low = low(opened)
        open_ref[edges, :] = opened_low
        bend_ref[edges, :] = low(opened * (1.0 - opened))
        bsrc_ref[edges, :] = low(b_source)
        dst_turned = turned_ref[place * EB : place * EB + BLOCK, :]
        sums.append(
            mm(dst_turned, jnp.concatenate([low(opened * b_source), opened_low], axis=1))
        )
    both = jnp.concatenate(sums, axis=0)
    width = x.shape[1]
    recip = 1.0 / (both[:, width:] + 1.0)
    ratio = both[:, :width] * recip
    gated = a_part + ratio
    gated_sig = sig(gated)
    out = x.astype(f32) + gated * gated_sig
    slope_ref[...] = low(gated_sig * (1.0 + gated * (1.0 - gated_sig)))
    recip_ref[...] = low(recip)
    fall_ref[...] = low(ratio * recip)
    out_ref[...] = out
    live = live_of(info_ref, pl.program_id(0) * group, group, out.shape[1])
    kept = live * out
    add_rows(sums_ref, [col_sum(kept), col_sum(kept * out)])

    @pl.when(pl.program_id(0) == 0)
    def _():
        sums_ref[2:4, :] = other_ref[0:2, :]
        count = info_ref[1]
        for place in range(2, info_ref.shape[0] - 2):
            count = count + info_ref[place]
        sums_ref[4:5, :] = jnp.full((1, out.shape[1]), count, jnp.int32).astype(f32)


def head_masks(width):
    head = lax.broadcasted_iota(jnp.int32, (16, width), 1) // (width // HEADS)
    return [low(jnp.where(head == place, 1.0, 0.0))[:1] for place in range(HEADS)]


def head_stack(values, masks):
    return jnp.concatenate([values * mask for mask in masks], axis=0)


def tall_masks(width):
    head = lax.broadcasted_iota(jnp.int32, (width, BLOCK), 0) // (width // HEADS)
    return [low(jnp.where(head == place, 1.0, 0.0)) for place in range(HEADS)]


def side_stack(turned, masks):
    return jnp.concatenate([turned * mask for mask in masks], axis=1)


def turned_product(turned, weight, nodes, size):
    parts = []
    for head in range(0, HEADS, 2):
        both = mm(
            turned[head * size : (head + 2) * size],
            weight[nodes, head * BLOCK : (head + 2) * BLOCK],
        )
        parts += [both[:size, :BLOCK], both[size:, BLOCK:]]
    return low(jnp.concatenate(parts, axis=0)).T


def attend_kernel(
    info_ref, x_ref, bias_ref, w_ref, vec_ref,
    out_ref, q_ref, k_ref, v_ref, att_ref, prob_ref, sums_ref,
):
    group = x_ref.shape[0] // BLOCK
    x = x_ref[...]
    queries = low(mm(x, w_ref[5]) + vec_ref[2:3, :])
    keyed = low(mm(x, w_ref[6]))
    valued = low(mm(x, w_ref[7]) + vec_ref[3:4, :])
    q_ref[...] = queries
    k_ref[...] = keyed
    v_ref[...] = valued
    score_scale = (x.shape[1] // HEADS) ** (-0.5) * math.log2(math.e)
    tall = tall_masks(x.shape[1])
    queries_turned = queries.T
    valued_turned = valued.T
    size = x.shape[1] // HEADS
    raws = [
        mm(keyed[nodes_of(place)], side_stack(queries_turned[:, nodes_of(place)], tall))
        for place in range(group)
    ]
    for place in range(group):
        nodes = nodes_of(place)
        bias = bias_ref[nodes, :]
        for head in range(HEADS):
            cols = nodes_of(head)
            part = raws[place][:, cols] + bias
            part = jnp.exp2((part - jnp.max(part, axis=0, keepdims=True)) * score_scale)
            prob_ref[nodes, cols] = low(part * (1.0 / jnp.sum(part, axis=0, keepdims=True)))
    for place in range(group):
        nodes = nodes_of(place)
        att_ref[nodes, :] = turned_product(valued_turned[:, nodes], prob_ref, nodes, size)
    out = x.astype(f32) + mm(att_ref[...], w_ref[8]) + vec_ref[4:5, :]
    out_ref[...] = out
    live = live_of(info_ref, pl.program_id(0) * group, group, out.shape[1])
    kept = live * out
    add_rows(sums_ref, [col_sum(kept), col_sum(kept * out)])


def mix_kernel(
    info_ref, local_ref, global_ref, cot_ref, sums_ref, w_ref, vec_ref,
    low_ref, hlow_ref, hidden_ref, mixed_ref, stat_ref,
):
    group = local_ref.shape[0] // BLOCK
    width = local_ref.shape[1]
    sums = sums_ref[...]
    count_row = sums[4:5]
    local_mean, local_rstd = norm_terms(sums, 0, count_row)
    global_mean, global_rstd = norm_terms(sums, 2, count_row)
    local_gain = vec_ref[5:6, :] * local_rstd
    global_gain = vec_ref[7:8, :] * global_rstd
    local_norm = local_ref[...] * local_gain + (vec_ref[6:7, :] - local_mean * local_gain)
    global_norm = global_ref[...] * global_gain + (vec_ref[8:9, :] - global_mean * global_gain)
    summed = low(local_norm).astype(f32) + low(global_norm).astype(f32)
    summed_low = low(summed)
    low_ref[...] = summed_low
    mixed = summed + vec_ref[11:12, :]
    for half in range(2):
        hidden = mm(summed_low, w_ref[9 + half]) + vec_ref[9 + half : 10 + half, :]
        sig_value = sig(hidden)
        hidden_low = low(hidden * sig_value)
        hidden_ref[:, half * width : (half + 1) * width] = hidden
        hlow_ref[:, half * width : (half + 1) * width] = hidden_low
        mixed = mixed + mm(hidden_low, w_ref[11 + half])
    mixed_ref[...] = mixed
    live = live_of(info_ref, pl.program_id(0) * group, group, width)
    kept = live * mixed
    d_norm = live * cot_ref[...].astype(f32)
    add_rows(
        stat_ref, [col_sum(kept), col_sum(kept * mixed), col_sum(d_norm), col_sum(d_norm * mixed)]
    )


def hat_kernel(info_ref, local_ref, global_ref, sums_ref, lhat_ref, ghat_ref):
    sums = sums_ref[...]
    for value_ref, hat_ref, first in ((local_ref, lhat_ref, 0), (global_ref, ghat_ref, 2)):
        mean, rstd = norm_terms(sums, first, sums[4:5])
        hat_ref[...] = low((value_ref[...] - mean) * rstd)


def slope_kernel(info_ref, hidden_ref, slope_ref):
    hidden = hidden_ref[...]
    sig_value = sig(hidden)
    slope_ref[...] = low(sig_value * (1.0 + hidden * (1.0 - sig_value)))


def mix_back_kernel(
    info_ref, mixed_ref, slope_ref, cot_ref, lhat_ref, ghat_ref, sums_ref, tops_ref, w_ref,
    vec_ref,
    dmix_ref, dhid_ref, dsum_ref, stat_ref,
):
    group = mixed_ref.shape[0] // BLOCK
    width = mixed_ref.shape[1]
    sums = sums_ref[...]
    tops = tops_ref[...]
    count_row = sums[4:5]
    mean, rstd = norm_terms(tops, 0, count_row)
    live = live_of(info_ref, pl.program_id(0) * group, group, width)
    hat = (mixed_ref[...] - mean) * rstd
    d_norm = live * cot_ref[...].astype(f32)
    dz_sum = tops[2:3]
    dz_hat = (tops[3:4] - mean * dz_sum) * rstd
    d_mixed = (vec_ref[12:13, :] * rstd) * (
        d_norm - live * (dz_sum / count_row + hat * (dz_hat / count_row))
    )
    d_mixed_low = low(d_mixed)
    dmix_ref[...] = d_mixed_low
    d_summed = d_mixed
    for half in range(2):
        cols = slice(half * width, (half + 1) * width)
        d_hidden = low(mm_back(d_mixed_low, w_ref[11 + half]) * slope_ref[:, cols].astype(f32))
        dhid_ref[:, cols] = d_hidden
        d_summed = d_summed + mm_back(d_hidden, w_ref[9 + half])
    d_low = low(d_summed)
    dsum_ref[...] = d_low
    d_sum = d_low.astype(f32)
    add_rows(
        stat_ref,
        [
            col_sum(d_sum),
            col_sum(d_sum * lhat_ref[...].astype(f32)),
            col_sum(d_sum * ghat_ref[...].astype(f32)),
            col_sum(d_mixed),
        ],
    )


def accumulate(acc_ref, term):
    @pl.when(pl.program_id(0) == 0)
    def _():
        acc_ref[...] = jnp.zeros_like(acc_ref)

    acc_ref[...] += term


def layer_kernel(info_ref, mixed_ref, sums_ref, tops_ref, vec_ref, layer_ref):
    group = mixed_ref.shape[0] // BLOCK
    mean, rstd = norm_terms(tops_ref[...], 0, sums_ref[4:5, :])
    live = live_of(info_ref, pl.program_id(0) * group, group, mixed_ref.shape[1])
    hat = (mixed_ref[...] - mean) * rstd
    layer_ref[...] = low(live * (vec_ref[12:13, :] * hat + vec_ref[13:14, :]))


def ones_sum(ref, cols):
    return mm(jnp.ones((8, ref.shape[0]), bf16), ref[:, cols])


def inner_grad_kernel(info_ref, slow_ref, dhid_ref, out_ref, bias_ref):
    accumulate(out_ref, mm_rows(slow_ref[...], dhid_ref[...]))
    accumulate(bias_ref, ones_sum(dhid_ref, slice(None)))


def outer_grad_kernel(info_ref, hlow_ref, dmix_ref, out_ref):
    accumulate(out_ref, mm_rows(hlow_ref[...], dmix_ref[...]))


def norm_back(info_ref, dsum_ref, hat_ref, sums, backs, first, gain_row, hat_row):
    group = hat_ref.shape[0] // BLOCK
    count_row = sums[4:5]
    rstd = norm_terms(sums, first, count_row)[1]
    live = live_of(info_ref, pl.program_id(0) * group, group, hat_ref.shape[1])
    hat = hat_ref[...].astype(f32)
    return (gain_row * rstd) * (
        dsum_ref[...].astype(f32)
        - live * (backs[0:1] / count_row + hat * (backs[hat_row : hat_row + 1] / count_row))
    )


def local_back_kernel(
    info_ref, dsum_ref, local_ref, slope_ref, recip_ref, fall_ref, open_ref, bend_ref, bsrc_ref,
    hot_ref, turned_ref, sums_ref, backs_ref, vec_ref,
    dnode_ref, dedge_ref, stat_ref,
):
    group = local_ref.shape[0] // BLOCK
    width = local_ref.shape[1]
    d_local = norm_back(
        info_ref, dsum_ref, local_ref, sums_ref[...], backs_ref[...], 0, vec_ref[5:6, :], 1
    )
    d_gated = d_local * slope_ref[...].astype(f32)
    dnode_ref[:, :width] = low(d_gated)
    d_num = low(d_gated * recip_ref[...].astype(f32))
    d_den = low(-d_gated * fall_ref[...].astype(f32))
    pre_row = jnp.zeros((1, width), f32)
    picks = [
        mm(
            hot_ref[edges_of(place), :BLOCK],
            jnp.concatenate([d_num[nodes_of(place)], d_den[nodes_of(place)]], axis=1),
        )
        for place in range(group)
    ]
    sources = []
    for place in range(group):
        edges = edges_of(place)
        d_message = picks[place][:, :width]
        d_open = d_message * bsrc_ref[edges, :].astype(f32) + picks[place][:, width:]
        sources.append(low(d_message * open_ref[edges, :].astype(f32)))
        d_pre = d_open * bend_ref[edges, :].astype(f32)
        pre_row = pre_row + col_sum(d_pre)
        dedge_ref[edges, :] = low(d_pre)
    for place in range(group):
        nodes = nodes_of(place)
        turned = turned_ref[edges_of(place), :]
        d_both = low(mm(turned, dedge_ref[edges_of(place), :]))
        dnode_ref[nodes, width : 2 * width] = low(mm(turned[BLOCK:], sources[place]))
        dnode_ref[nodes, 2 * width : 3 * width] = d_both[:BLOCK]
        dnode_ref[nodes, 3 * width :] = d_both[BLOCK:]
    add_rows(stat_ref, [col_sum(d_gated), pre_row])


def attend_back_kernel(
    info_ref, dsum_ref, global_ref, q_ref, k_ref, v_ref, prob_ref, sums_ref,
    backs_ref, w_ref, vec_ref,
    dqkv_ref, dlow_ref, stat_ref, score_ref,
):
    group = global_ref.shape[0] // BLOCK
    width = global_ref.shape[1]
    score_scale = (width // HEADS) ** (-0.5)
    d_global = norm_back(
        info_ref, dsum_ref, global_ref, sums_ref[...], backs_ref[...], 2, vec_ref[7:8, :], 2
    )
    d_low = low(d_global)
    dlow_ref[...] = d_low
    d_att = low(mm_back(d_low, w_ref[8]))
    masks = head_masks(width)
    tall = tall_masks(width)
    turned_att = low(mm_back(w_ref[8], d_low))
    d_probs = [
        mm(v_ref[nodes_of(place), :], side_stack(turned_att[:, nodes_of(place)], tall))
        for place in range(group)
    ]
    for place in range(group):
        nodes = nodes_of(place)
        for head in range(HEADS):
            cols = nodes_of(head)
            prob = prob_ref[nodes, cols].astype(f32)
            part = d_probs[place][:, cols]
            inner = jnp.sum(prob * part, axis=0, keepdims=True)
            d_score = low(prob * ((part - inner) * score_scale))
            score_ref[nodes, cols] = d_score
    for place in range(group):
        nodes = nodes_of(place)
        dqkv_ref[nodes, :width] = turned_product(k_ref[nodes, :].T, score_ref, nodes, width // HEADS)
        dqkv_ref[nodes, width : 2 * width] = low(
            mm(score_ref[nodes, :], head_stack(q_ref[nodes, :], masks))
        )
        dqkv_ref[nodes, 2 * width :] = low(
            mm(prob_ref[nodes, :], head_stack(d_att[nodes], masks))
        )
    add_rows(
        stat_ref,
        [
            col_sum(d_global),
        ],
    )


def branch_grad_kernel(
    info_ref, x_ref, e_ref, att_ref, dnode_ref, dedge_ref, dqkv_ref, dlow_ref, igrad_ref, ograd_ref,
    *outs,
):
    outs, bias_ref, (node_ref, wide_ref, edge_ref, acc_ref) = outs[:-5], outs[-5], outs[-4:]
    width = x_ref.shape[1]
    for place in (0, 2):
        bias_ref[:, place // 2 * width : (place // 2 + 1) * width] = ones_sum(
            dqkv_ref, slice(place * width, (place + 1) * width)
        )
    x = x_ref[...]
    node_ref[...] = mm_rows(x, dnode_ref[...])
    wide_ref[...] = mm_rows(x, dqkv_ref[...])
    edge_ref[...] = mm_rows(e_ref[...], dedge_ref[...])
    acc_ref[...] = mm_rows(att_ref[...], dlow_ref[...])
    cols = [slice(place * width, (place + 1) * width) for place in range(4)]
    parts = [node_ref.at[:, cols[0]], node_ref.at[:, cols[1]], edge_ref]
    parts = parts + [node_ref.at[:, cols[2]], node_ref.at[:, cols[3]]]
    parts = parts + [wide_ref.at[:, cols[place]] for place in range(3)] + [acc_ref]
    parts = parts + [igrad_ref.at[:, cols[place]] for place in range(2)]
    parts = parts + [ograd_ref.at[cols[place], :] for place in range(2)]
    if len(outs) == 1:
        for place, part in enumerate(parts):
            outs[0][place] = low(part[...])
    else:
        pack(info_ref, parts, outs)


def reach(order, index):
    found = 0
    for place, step in enumerate(order):
        if index >> (len(order) - 1 - place) & 1:
            found ^= step >> 1
    return found


def chip_orders(total):
    chips = steps_of(total)[1:]
    return (chips, chips[1:-1] + chips[:1] + chips[-1:])


def pack(info_ref, parts, outs):
    half = outs[0].shape[0]
    slots = 2 * half
    orders = chip_orders(2 * slots)
    core = info_ref[info_ref.shape[0] - 2]
    chip = info_ref[info_ref.shape[0] - 1]
    for slot in range(slots):
        near = [reach(order, slot) for order in orders]
        for out_ref, owner in zip(outs[slot // half :: 2], (core, 1 - core)):
            step = jnp.where(owner == 0, near[0], near[1])
            row = pl.multiple_of(16 * jnp.bitwise_xor(chip, step) + 8 * owner, 8)
            for first in range(0, len(parts), 2):
                pair = [part[pl.ds(row, 8), :] for part in parts[first : first + 2]]
                out_ref[slot % half, first * 8 : first * 8 + 8 * len(pair), :] = low(
                    jnp.concatenate(pair, axis=0)
                )


def assemble_kernel(info_ref, near_ref, far_ref, near_other_ref, far_other_ref, out_ref):
    half, tall, _ = near_ref.shape
    slots = 2 * half
    orders = chip_orders(2 * slots)
    core = info_ref[info_ref.shape[0] - 2]
    chip = info_ref[info_ref.shape[0] - 1]

    def fill(even_refs, odd_refs):
        for far in range(slots):
            even, odd = [
                [slot for slot in range(slots) if reach(order, slot) == far][0] for order in orders
            ]
            row = pl.multiple_of(16 * jnp.bitwise_xor(chip, far), 16)
            for first in range(0, tall, 16):
                size = min(16, tall - first)
                part = slice(first, first + size)
                upper = even_refs[even // half][even % half, part, :].astype(f32)
                lower = odd_refs[odd // half][odd % half, part, :].astype(f32)
                for step in range(size // 8):
                    rows = slice(step * 8, step * 8 + 8)
                    out_ref[first // 8 + step, pl.ds(row, 16), :] = low(
                        jnp.concatenate([upper[rows], lower[rows]], axis=0)
                    )

    @pl.when(core == 0)
    def _():
        fill((near_ref, far_ref), (near_other_ref, far_other_ref))

    @pl.when(core != 0)
    def _():
        fill((near_other_ref, far_other_ref), (near_ref, far_ref))


def node_grad_kernel(
    info_ref, dsum_ref, lhat_ref, ghat_ref, dnode_ref, dqkv_ref, sums_ref, backs_ref, w_ref,
    vec_ref,
    node_ref,
):
    width = lhat_ref.shape[1]
    sums = sums_ref[...]
    backs = backs_ref[...]
    total = norm_back(info_ref, dsum_ref, lhat_ref, sums, backs, 0, vec_ref[5:6, :], 1)
    total = total + norm_back(info_ref, dsum_ref, ghat_ref, sums, backs, 2, vec_ref[7:8, :], 2)
    for place, mat in enumerate((0, 1, 3, 4)):
        total = total + mm_back(dnode_ref[:, place * width : (place + 1) * width], w_ref[mat])
    for place in range(3):
        total = total + mm_back(dqkv_ref[:, place * width : (place + 1) * width], w_ref[5 + place])
    node_ref[...] = total


def edge_grad_kernel(info_ref, dedge_ref, w_ref, edge_ref):
    edge_ref[...] = mm_back(dedge_ref[...], w_ref[2])


def bias_rows(local_ref, attend_ref, inner_ref, wide_ref):
    width = attend_ref.shape[1]
    return jnp.concatenate(
        [
            local_ref[0:2, :],
            wide_ref[0:1, :width],
            wide_ref[0:1, width:],
            attend_ref[0:1, :],
            inner_ref[0:1, :width],
            inner_ref[0:1, width:],
            jnp.zeros((1, width), f32),
        ],
        axis=0,
    )


def last_kernel(
    info_ref, kept_ref, got_ref, local_ref, attend_ref, inner_ref, wide_ref, out_ref
):
    biases = bias_rows(local_ref, attend_ref, inner_ref, wide_ref)
    upper = low(biases).astype(f32)
    for slot, extra in enumerate((upper, biases - upper)):
        total = kept_ref[slot].astype(f32) + got_ref[slot].astype(f32)
        out_ref[slot] = low(jnp.concatenate([total, extra], axis=0))


def total_square(values):
    return jnp.sum(jnp.sum(values * values, axis=0, keepdims=True), axis=1, keepdims=True)


def pair_kernel(info_ref, mine_ref, got_ref, grad_ref, tail_ref):
    rows = grad_ref.shape[1]
    half = grad_ref.shape[2]
    mine = [mine_ref[slot].astype(f32) for slot in range(2)]
    got = [got_ref[slot].astype(f32) for slot in range(2)]
    grad = mine[0][:rows] + got[1][:rows]
    other = mine[1][:rows] + got[0][:rows]
    grad_ref[0] = grad[:, :half]
    grad_ref[1] = grad[:, half:]
    tail_ref[...] = (mine[0][rows:] + mine[1][rows:]) + (got[0][rows:] + got[1][rows:])
    tail_ref[7:8, :] = jnp.broadcast_to(total_square(grad) + total_square(other), (1, 2 * half))


def square_kernel(
    info_ref, kept_ref, got_ref, local_ref, attend_ref, inner_ref, wide_ref, grad_ref, tail_ref
):
    grad = kept_ref[...].astype(f32) + got_ref[...].astype(f32)
    half = grad.shape[1] // 2
    grad_ref[0] = grad[:, :half]
    grad_ref[1] = grad[:, half:]
    tail_ref[...] = bias_rows(local_ref, attend_ref, inner_ref, wide_ref)
    tail_ref[7:8, :] = jnp.broadcast_to(total_square(grad), (1, tail_ref.shape[1]))


def update_kernel(
    info_ref, grad_ref, tail_ref, sums_ref, tops_ref, backs_ref, w_ref, w1_ref, w2_ref, v_ref,
    v1_ref, v2_ref,
    new_w_ref, new_w1_ref, new_w2_ref, new_v_ref, new_v1_ref, new_v2_ref, norm_ref,
):
    tail = tail_ref[...]
    tops = tops_ref[...]
    backs = backs_ref[...]
    mean, rstd = norm_terms(tops, 0, sums_ref[4:5, :])
    grad_v = jnp.concatenate(
        [
            tail[0:5],
            backs[1:2],
            backs[0:1],
            backs[2:3],
            backs[0:1],
            tail[5:7],
            backs[3:4],
            (tops[3:4] - mean * tops[2:3]) * rstd,
            tops[2:3],
        ],
        axis=0,
    )
    square = jnp.sum(jnp.sum(grad_v * grad_v, axis=0, keepdims=True), axis=1, keepdims=True)
    norm = jnp.sqrt(tail[7:8, 0:1] + square)
    norm_ref[...] = norm
    factor = jnp.minimum(1.0, clip_limit / (norm + 1e-06))
    new_v_ref[...], new_v1_ref[...], new_v2_ref[...] = adamw(
        v_ref[...], factor * grad_v, v1_ref[...], v2_ref[...], rate_vecs, 0.0
    )
    mats, span = w_ref.shape
    _, rows, half = grad_ref.shape
    for piece in range(span // half):
        cols = slice(piece * half, (piece + 1) * half)
        if rows == mats:
            grad = grad_ref[piece]
        else:
            grad = grad_ref[piece % 2, pl.ds(piece // 2, mats, rows // mats), :]
        new_w_ref[:, cols], new_w1_ref[:, cols], new_w2_ref[:, cols] = adamw(
            w_ref[:, cols], factor * grad, w1_ref[:, cols], w2_ref[:, cols], rate_mats, decay_mats
        )


def rows_spec(rows, width, offset=0):
    if offset:
        return pl.BlockSpec((rows, width), lambda step, info: (step + info[0], 0))
    return pl.BlockSpec((rows, width), lambda step, info: (step, 0))


def whole_spec(shape):
    zeros = (0,) * len(shape)
    return pl.BlockSpec(shape, lambda step, info: zeros)


def call(kernel, steps, info, inputs, outputs, scratch=(), room=10, cost=5):
    in_specs = []
    arrays = []
    for array, spec in inputs:
        arrays.append(array)
        in_specs.append(whole_spec(array.shape) if spec is None else spec)
    out_specs = []
    out_shapes = []
    for shape, dtype, spec, *far in outputs:
        out_specs.append(whole_spec(shape) if spec is None else spec)
        out_shapes.append(pltpu.HBM(shape, dtype) if far else jax.ShapeDtypeStruct(shape, dtype))
    return pl.pallas_call(
        kernel,
        grid_spec=pltpu.PrefetchScalarGridSpec(
            num_scalar_prefetch=1,
            grid=(steps,),
            in_specs=in_specs,
            out_specs=out_specs,
            scratch_shapes=list(scratch),
        ),
        out_shape=out_shapes,
        compiler_params=pltpu.CompilerParams(
            dimension_semantics=("arbitrary",), vmem_limit_bytes=room * 1024 * 1024
        ),
        name=kernel.__name__,
        cost_estimate=pl.CostEstimate(
            flops=cost * 1000000000, bytes_accessed=cost * 1000000, transcendentals=0
        ),
    )(info, *arrays)


def swap_with(values, step, total):
    return lax.ppermute(values, axis_names, [(place, place ^ step) for place in range(total)])


def steps_of(total):
    return [1 << power for power in range(total.bit_length() - 1)]


def beside(start, transfer, info, work):
    info = lax.optimization_barrier((info, start))[0]
    return lax.optimization_barrier((transfer, work(info)))


def sum_small(values, total, info=None, works=()):
    results = []
    works = list(works)
    for step in steps_of(total):
        other = swap_with(values, step, total)
        if works and step > 1:
            other, done = beside(values, other, info, works.pop(0))
            results.append(done)
        values = values + other
    return (values, results) if results else values


def swap_chips(values, number, total):
    orders = chip_orders(total)
    return lax.ppermute(
        values,
        axis_names,
        [(place, place ^ orders[place % 2][number]) for place in range(total)],
    )


def in_rows(total, width):
    return width * width // total == 8 * width


def gather_matrices(shard, info, total, width, work):
    mats = shard.shape[0]
    if not in_rows(total, width):
        gathered = lax.all_gather(shard, axis_names, axis=1, tiled=True)
        return (gathered.reshape(mats, width, width), work(info))
    held = shard.reshape(1, mats * 8, width)
    for number in reversed(range(1, len(chip_orders(total)[0]))):
        held = jnp.concatenate([held, swap_chips(held, number, total)], axis=0)
    got = swap_chips(held, 0, total)
    other = swap_with(held, 1, total)

    def both(info):
        return (work(info), other)

    got, (done, other) = beside(held, got, info, both)
    far_other = swap_with(got, 1, total)
    matrices = call(
        assemble_kernel,
        1,
        info,
        [(held, None), (got, None), (other, None), (far_other, None)],
        [((mats, width, width), bf16, None)],
    )[0]
    return (matrices, done)


def scatter_plain(grads, total):
    place = lax.axis_index(axis_names)
    mats, width, _ = grads.shape
    bits = total.bit_length() - 1
    held = grads.reshape((mats,) + (2,) * bits + (width * width // total,))
    held = held.transpose(tuple(reversed(range(1, bits + 1))) + (0, bits + 1))
    for step in steps_of(total):
        mine = ((place & step) != 0).astype(jnp.int32)
        sent = lax.dynamic_index_in_dim(held, 1 - mine, 0, keepdims=False)
        kept = lax.dynamic_index_in_dim(held, mine, 0, keepdims=False)
        got = swap_with(sent, step, total)
        if step * 2 < total:
            held = low(kept.astype(f32) + got.astype(f32))
    return (kept, got)


def scatter_packed(kept, far_kept, sent, far_sent, total, info, works, biases):
    far_got = swap_with(far_sent, 1, total)
    got = swap_with(sent, 1, total)
    results = []
    rounds = len(chip_orders(total)[0])
    for number in range(rounds - 1):
        if number:
            half = kept.shape[0] // 2
            far_kept, far_got = kept[half:], got[half:]
            kept, got = kept[:half], got[:half]
        sent = low(far_kept.astype(f32) + far_got.astype(f32))
        kept = kept.astype(f32) + got.astype(f32)
        got = swap_chips(sent, number, total)
        if number < len(works):
            got, done = beside(sent, got, info, works[number])
            results.append(done)
    mine = call(
        last_kernel,
        1,
        info,
        [(array, None) for array in (kept, got, *biases)],
        [((2, kept.shape[1] + 8, kept.shape[2]), bf16, None)],
    )[0]
    got = swap_chips(mine, rounds - 1, total)
    grad_rows, tail = call(
        pair_kernel,
        1,
        info,
        [(mine, None), (got, None)],
        [((2, kept.shape[1], kept.shape[2] // 2), f32, None), ((8, kept.shape[2]), f32, None)],
    )
    for step in steps_of(total)[:-1]:
        tail = tail + swap_with(tail, step, total)
    return (grad_rows, tail, results)


def adamw(params, gradient, moment_one, moment_two, rate, decay):
    first = beta_one * moment_one + (1.0 - beta_one) * gradient
    second = beta_two * moment_two + (1.0 - beta_two) * gradient * gradient
    first_hat = first / (1.0 - beta_one**STEP)
    second_hat = second / (1.0 - beta_two**STEP)
    updated = params - rate * (first_hat / (jnp.sqrt(second_hat) + adam_eps) + decay * params)
    return (updated, first, second)


def own_half(values, branch_index):
    half = values.shape[0] // 2
    return lax.dynamic_slice_in_dim(values, branch_index * half, half, 0)


def per_device(
    node_feats,
    edge_feats,
    cotangent,
    graph_ids,
    node_mask,
    edge_src,
    edge_dst,
    edge_mask,
    weights,
    weight_moment1,
    weight_moment2,
    vectors,
    vector_moment1,
    vector_moment2,
):
    total = lax.axis_size("rows") * lax.axis_size("branch")
    branch_index = lax.axis_index("branch")
    width = node_feats.shape[1]
    rows = node_feats.shape[0] // 2
    edges = edge_feats.shape[0] // 2
    blocks = rows // BLOCK
    group = math.gcd(blocks, GROUP)
    steps = blocks // group
    tall = group * BLOCK
    tall_edges = group * EB
    w_bf = low(weights)
    own_nodes = own_half(node_feats, branch_index)
    own_edges = own_half(edge_feats, branch_index)
    counts = jnp.sum(own_half(node_mask, branch_index).reshape(blocks, BLOCK), axis=1)
    info = jnp.concatenate(
        [(branch_index * steps)[None], counts, branch_index[None], lax.axis_index("rows")[None]]
    ).astype(jnp.int32)

    def by_step(values, slots):
        return own_half(values, branch_index).reshape(steps, group, slots)

    def step_spec(slots):
        return pl.BlockSpec((1, group, slots), lambda step, info: (step, 0, 0))

    edge_spec = rows_spec(tall_edges, width)
    node_spec = rows_spec(tall, width)
    def prep_work(info):
        return call(
            prep_kernel,
            steps,
            info,
            [
                (by_step(edge_src, EB), step_spec(EB)),
                (by_step(edge_dst, EB), step_spec(EB)),
                (by_step(edge_mask, EB), step_spec(EB)),
                (by_step(graph_ids, BLOCK), step_spec(BLOCK)),
            ],
            [
                ((edges, EB), bf16, edge_spec, True),
                ((edges, EB), bf16, edge_spec, True),
                ((rows, BLOCK), f32, rows_spec(tall, BLOCK)),
            ],
        )

    matrices, (hot, turned, bias) = gather_matrices(w_bf, info, total, width, prep_work)
    x_in = (own_nodes, node_spec)
    e_in = (own_edges, edge_spec)
    mats_in = (matrices, None)
    vec_in = (vectors, None)
    node_f32 = ((rows, width), f32, node_spec)
    node_bf = ((rows, width), bf16, node_spec)
    sums_out = ((8, width), f32, None)
    prob_spec = rows_spec(tall, HEADS * BLOCK)
    global_out, queries, keyed, valued, attended, probs, global_sums = call(
        attend_kernel,
        steps,
        info,
        [x_in, (bias, rows_spec(tall, BLOCK)), mats_in, vec_in],
        [
            node_f32,
            node_bf,
            node_bf,
            node_bf,
            node_bf,
            ((rows, HEADS * BLOCK), bf16, prob_spec),
            sums_out,
        ],
    )
    local_out, gate_slope, recip, fall, opened, bend, b_source, sums_part = call(
        local_kernel,
        steps,
        info,
        [
            x_in,
            e_in,
            (hot, edge_spec),
            (turned, edge_spec),
            mats_in,
            vec_in,
            (global_sums, None),
        ],
        [
            node_f32,
            node_bf,
            node_bf,
            node_bf,
            ((edges, width), bf16, edge_spec),
            ((edges, width), bf16, edge_spec),
            ((edges, width), bf16, edge_spec),
            sums_out,
        ],
    )
    sums = sum_small(sums_part, total)
    sums_in = (sums, None)
    cot_in = (cotangent, node_spec)
    wide_spec = rows_spec(tall, 2 * width)
    summed_low, hidden_low, hidden, mixed, top_part = call(
        mix_kernel,
        steps,
        info,
        [(local_out, node_spec), (global_out, node_spec), cot_in, sums_in, mats_in, vec_in],
        [
            node_bf,
            ((rows, 2 * width), bf16, wide_spec),
            ((rows, 2 * width), f32, wide_spec),
            node_f32,
            sums_out,
        ],
    )

    def hat_work(info):
        return call(
            hat_kernel,
            steps,
            info,
            [(local_out, node_spec), (global_out, node_spec), sums_in],
            [node_bf, node_bf],
        )

    def slope_work(info):
        return call(
            slope_kernel,
            steps,
            info,
            [(hidden, wide_spec)],
            [((rows, 2 * width), bf16, wide_spec)],
        )[0]

    tops, ((local_hat, global_hat), hidden_slope) = sum_small(
        top_part, total, info, [hat_work, slope_work]
    )
    d_mixed, d_hidden, d_summed, back_part = call(
        mix_back_kernel,
        steps,
        info,
        [
            (mixed, node_spec),
            (hidden_slope, wide_spec),
            cot_in,
            (local_hat, node_spec),
            (global_hat, node_spec),
            sums_in,
            (tops, None),
            mats_in,
            vec_in,
        ],
        [
            node_bf,
            ((rows, 2 * width), bf16, wide_spec),
            node_bf,
            sums_out,
        ],
    )

    def mat_out(tall_by, wide_by):
        return ((tall_by * width, wide_by * width), f32, None)

    def inner_work(info):
        return call(
            inner_grad_kernel,
            steps,
            info,
            [(summed_low, node_spec), (d_hidden, wide_spec)],
            [mat_out(1, 2), ((8, 2 * width), f32, None)],
        )

    def outer_work(info):
        return call(
            outer_grad_kernel,
            steps,
            info,
            [(hidden_low, wide_spec), (d_mixed, node_spec)],
            [mat_out(2, 1)],
        )[0]

    def layer_work(info):
        return call(
            layer_kernel,
            steps,
            info,
            [(mixed, node_spec), sums_in, (tops, None), vec_in],
            [node_bf],
        )[0]

    backs, ((inner_grads, inner_bias), outer_grads, layer_out) = sum_small(
        back_part, total, info, [inner_work, outer_work, layer_work]
    )
    backs_in = (backs, None)
    dsum_in = (d_summed, node_spec)
    dnode_spec = rows_spec(tall, 4 * width)
    d_node, d_edge, local_bias = call(
        local_back_kernel,
        steps,
        info,
        [
            dsum_in,
            (local_hat, node_spec),
            (gate_slope, node_spec),
            (recip, node_spec),
            (fall, node_spec),
            (opened, edge_spec),
            (bend, edge_spec),
            (b_source, edge_spec),
            (hot, edge_spec),
            (turned, edge_spec),
            sums_in,
            backs_in,
            vec_in,
        ],
        [
            ((rows, 4 * width), bf16, dnode_spec),
            ((edges, width), bf16, edge_spec),
            sums_out,
        ],
    )
    dqkv_spec = rows_spec(tall, 3 * width)
    slots = total // 2
    packed = in_rows(total, width)
    grad_outs = [((MATS, width, width), bf16, None)]
    if packed:
        grad_outs = [((slots // 2, MATS * 8, width), bf16, None)] * 4
    d_qkv, d_low, attend_bias = call(
        attend_back_kernel,
        steps,
        info,
        [
            dsum_in,
            (global_hat, node_spec),
            (queries, node_spec),
            (keyed, node_spec),
            (valued, node_spec),
            (probs, prob_spec),
            sums_in,
            backs_in,
            mats_in,
            vec_in,
        ],
        [((rows, 3 * width), bf16, dqkv_spec), node_bf, sums_out],
        [pltpu.VMEM((tall, HEADS * BLOCK), bf16)],
    )
    *grads, wide_bias = call(
        branch_grad_kernel,
        1,
        info,
        [
            (own_nodes, None),
            (own_edges, None),
            (attended, None),
            (d_node, None),
            (d_edge, None),
            (d_qkv, None),
            (d_low, None),
            (inner_grads, None),
            (outer_grads, None),
        ],
        grad_outs + [((8, 2 * width), f32, None)],
        [
            pltpu.VMEM((width, 4 * width), f32),
            pltpu.VMEM((width, 3 * width), f32),
            pltpu.VMEM((width, width), f32),
            pltpu.VMEM((width, width), f32),
        ],
    )

    def node_work(info):
        return call(
            node_grad_kernel,
            steps,
            info,
            [
                dsum_in,
                (local_hat, node_spec),
                (global_hat, node_spec),
                (d_node, dnode_spec),
                (d_qkv, dqkv_spec),
                sums_in,
                backs_in,
                mats_in,
                vec_in,
            ],
            [node_f32],
        )[0]

    def edge_work(info):
        return call(
            edge_grad_kernel,
            steps,
            info,
            [(d_edge, edge_spec), mats_in],
            [((edges, width), f32, edge_spec)],
        )[0]

    biases = (local_bias, attend_bias, inner_bias, wide_bias)
    if packed:
        grad_rows, tail, (node_grad, edge_grad) = scatter_packed(
            *grads, total, info, [node_work, edge_work], biases
        )
    else:
        grad_shard = scatter_plain(grads[0], total)
        node_grad, edge_grad = node_work(info), edge_work(info)
        grad_rows, tail_part = call(
            square_kernel,
            1,
            info,
            [(array, None) for array in (*grad_shard, *biases)],
            [
                ((2, grad_shard[0].shape[0], grad_shard[0].shape[1] // 2), f32, None),
                sums_out,
            ],
        )
        tail = sum_small(tail_part, total)
    like_mats = (weights.shape, f32, None)
    like_vecs = (vectors.shape, f32, None)
    new_weights, first_w, second_w, new_vectors, first_v, second_v, norm = call(
        update_kernel,
        1,
        info,
        [
            (array, None)
            for array in (
                grad_rows, tail, sums, tops, backs, weights, weight_moment1, weight_moment2,
                vectors, vector_moment1, vector_moment2,
            )
        ],
        [like_mats] * 3 + [like_vecs] * 3 + [((1, 1), f32, None)],
    )
    grad_norm = norm.reshape(())
    return (
        layer_out,
        node_grad,
        edge_grad,
        new_weights,
        first_w,
        second_w,
        new_vectors,
        first_v,
        second_v,
        grad_norm,
    )


def solution(mesh):
    in_specs = (
        P("rows", None),
        P("rows", None),
        P(("rows", "branch"), None),
        P("rows"),
        P("rows"),
        P("rows"),
        P("rows"),
        P("rows"),
        P(None, ("rows", "branch")),
        P(None, ("rows", "branch")),
        P(None, ("rows", "branch")),
        P(),
        P(),
        P(),
    )
    out_specs = (
        P(("rows", "branch"), None),
        P(("rows", "branch"), None),
        P(("rows", "branch"), None),
        P(None, ("rows", "branch")),
        P(None, ("rows", "branch")),
        P(None, ("rows", "branch")),
        P(),
        P(),
        P(),
        P(),
    )
    return jax.shard_map(
        per_device, mesh=mesh, in_specs=in_specs, out_specs=out_specs, check_vma=False
    )
```

```python
import functools
import math

import jax
import jax.numpy as jnp
from jax import lax
from jax.experimental import pallas as pl
from jax.experimental.pallas import tpu as pltpu
from jax.sharding import PartitionSpec as P

HEADS = 8
BLOCK = 128
EB = 256
MATS = 13
STEP = 7
GROUP = 8
BACK_ROOM = 12
FRONT_ROOM = 12

eps_norm = 1e-05
clip_limit = 1.0
beta_one = 0.9
beta_two = 0.999
rate_mats = 0.1
rate_vecs = 0.8
decay_mats = 0.01
adam_eps = 1e-08
hidden_floor = -1e30
axis_names = ("rows", "branch")
f32 = jnp.float32
bf16 = jnp.bfloat16


def mm(left, right):
    return jnp.dot(left, right, preferred_element_type=f32)


def mm_back(left, right):
    return lax.dot_general(left, right, (((1,), (1,)), ((), ())), preferred_element_type=f32)


def mm_rows(left, right):
    return lax.dot_general(left, right, (((0,), (0,)), ((), ())), preferred_element_type=f32)


def low(values):
    return values.astype(bf16)


def sig(values):
    return 0.5 * jnp.tanh(0.5 * values) + 0.5


def col_sum(values):
    return jnp.sum(values, axis=0, keepdims=True)


def live_of(info_ref, first_block, group, width):
    slot = lax.broadcasted_iota(jnp.int32, (BLOCK, width), 0)
    return jnp.concatenate(
        [
            jnp.where(slot < info_ref[1 + first_block + place], 1.0, 0.0)
            for place in range(group)
        ],
        axis=0,
    )


def nodes_of(place):
    return slice(place * BLOCK, (place + 1) * BLOCK)


def edges_of(place):
    return slice(place * EB, (place + 1) * EB)


def add_rows(out_ref, rows):
    @pl.when(pl.program_id(0) == 0)
    def _():
        out_ref[...] = jnp.zeros_like(out_ref)

    for place, row in enumerate(rows):
        out_ref[place : place + 1, :] += row


def norm_terms(sums, first, count_row):
    mean = sums[first : first + 1] / count_row
    rstd = lax.rsqrt(sums[first + 1 : first + 2] / count_row - mean * mean + eps_norm)
    return (mean, rstd)


def prep_kernel(info_ref, src_ref, dst_ref, mask_ref, id_ref, hot_ref, turned_ref, bias_ref):
    for place in range(GROUP):
        row = pl.ds(place, 1)
        node = lax.broadcasted_iota(jnp.int32, (BLOCK, EB), 0)
        live = mask_ref[0, row, :] != 0
        dst_rows = jnp.where((node == dst_ref[0, row, :]) & live, 1.0, 0.0)
        src_rows = jnp.where((node == src_ref[0, row, :]) & live, 1.0, 0.0)
        turned = jnp.concatenate([dst_rows, src_rows], axis=0)
        turned_ref[place * EB : (place + 1) * EB, :] = low(turned)
        hot_ref[place * EB : (place + 1) * EB, :] = low(turned.T)
        ids = jnp.broadcast_to(id_ref[0, row, :].astype(f32), (BLOCK, BLOCK))
        bias_ref[place * BLOCK : (place + 1) * BLOCK, :] = jnp.where(
            ids == ids.T, 0.0, hidden_floor
        )


def local_steps(
    info_ref, x_ref, e_ref, hot_ref, turned_ref, w_ref, vec_ref,
    out_ref, slope_ref, recip_ref, fall_ref, open_ref, bend_ref, bsrc_ref, stats,
):
    group = x_ref.shape[0] // BLOCK
    x = x_ref[...]
    a_part = mm(x, w_ref[0]) + vec_ref[0:1, :]
    b_part = low(mm(x, w_ref[1]))
    d_part = low(mm(x, w_ref[3]))
    e_part = low(mm(x, w_ref[4]))
    c_part = mm(e_ref[...], w_ref[2]) + vec_ref[1:2, :]
    gates = []
    picks = []
    for place in range(group):
        nodes = nodes_of(place)
        hot = hot_ref[edges_of(place), :]
        gates.append(mm(hot, jnp.concatenate([d_part[nodes], e_part[nodes]], axis=0)))
        picks.append(mm(hot[:, BLOCK:], b_part[nodes]))
    yield
    sums = []
    for place in range(group):
        edges = edges_of(place)
        opened = sig(c_part[edges] + gates[place])
        b_source = picks[place]
        opened_low = low(opened)
        open_ref[edges, :] = opened_low
        bend_ref[edges, :] = low(opened * (1.0 - opened))
        bsrc_ref[edges, :] = low(b_source)
        dst_turned = turned_ref[place * EB : place * EB + BLOCK, :]
        sums.append(
            mm(dst_turned, jnp.concatenate([low(opened * b_source), opened_low], axis=1))
        )
    yield
    both = jnp.concatenate(sums, axis=0)
    width = x.shape[1]
    recip = 1.0 / (both[:, width:] + 1.0)
    ratio = both[:, :width] * recip
    gated = a_part + ratio
    gated_sig = sig(gated)
    out = x.astype(f32) + gated * gated_sig
    slope_ref[...] = low(gated_sig * (1.0 + gated * (1.0 - gated_sig)))
    recip_ref[...] = low(recip)
    fall_ref[...] = low(ratio * recip)
    out_ref[...] = out
    live = live_of(info_ref, pl.program_id(0) * group, group, out.shape[1])
    kept = live * out
    stats[0:2] = [col_sum(kept), col_sum(kept * out)]


def head_masks(width):
    head = lax.broadcasted_iota(jnp.int32, (16, width), 1) // (width // HEADS)
    return [low(jnp.where(head == place, 1.0, 0.0))[:1] for place in range(HEADS)]


def head_stack(values, masks):
    return jnp.concatenate([values * mask for mask in masks], axis=0)


def tall_masks(width):
    head = lax.broadcasted_iota(jnp.int32, (width, BLOCK), 0) // (width // HEADS)
    return [low(jnp.where(head == place, 1.0, 0.0)) for place in range(HEADS)]


def side_stack(turned, masks):
    return jnp.concatenate([turned * mask for mask in masks], axis=1)


def turned_product(turned, weight, nodes, size):
    parts = []
    for head in range(0, HEADS, 2):
        both = mm(
            turned[head * size : (head + 2) * size],
            weight[nodes, head * BLOCK : (head + 2) * BLOCK],
        )
        parts += [both[:size, :BLOCK], both[size:, BLOCK:]]
    return low(jnp.concatenate(parts, axis=0)).T


def attend_steps(
    info_ref, x_ref, bias_ref, w_ref, vec_ref,
    out_ref, q_ref, k_ref, v_ref, att_ref, prob_ref, stats,
):
    group = x_ref.shape[0] // BLOCK
    x = x_ref[...]
    queries = low(mm(x, w_ref[5]) + vec_ref[2:3, :])
    keyed = low(mm(x, w_ref[6]))
    valued = low(mm(x, w_ref[7]) + vec_ref[3:4, :])
    q_ref[...] = queries
    k_ref[...] = keyed
    v_ref[...] = valued
    score_scale = (x.shape[1] // HEADS) ** (-0.5) * math.log2(math.e)
    tall = tall_masks(x.shape[1])
    queries_turned = queries.T
    valued_turned = valued.T
    size = x.shape[1] // HEADS
    raws = [
        mm(keyed[nodes_of(place)], side_stack(queries_turned[:, nodes_of(place)], tall))
        for place in range(group)
    ]
    yield
    for place in range(group):
        nodes = nodes_of(place)
        bias = bias_ref[nodes, :]
        for head in range(HEADS):
            cols = nodes_of(head)
            part = raws[place][:, cols] + bias
            part = jnp.exp2((part - jnp.max(part, axis=0, keepdims=True)) * score_scale)
            prob_ref[nodes, cols] = low(part * (1.0 / jnp.sum(part, axis=0, keepdims=True)))
    yield
    for place in range(group):
        nodes = nodes_of(place)
        att_ref[nodes, :] = turned_product(valued_turned[:, nodes], prob_ref, nodes, size)
    out = x.astype(f32) + mm(att_ref[...], w_ref[8]) + vec_ref[4:5, :]
    out_ref[...] = out
    live = live_of(info_ref, pl.program_id(0) * group, group, out.shape[1])
    kept = live * out
    stats[2:4] = [col_sum(kept), col_sum(kept * out)]


def forward_kernel(
    info_ref, x_ref, e_ref, bias_ref, hot_ref, turned_ref, w_ref, vec_ref,
    lout_ref, slope_ref, recip_ref, fall_ref, open_ref, bend_ref, bsrc_ref,
    gout_ref, q_ref, k_ref, v_ref, att_ref, prob_ref, sums_ref,
):
    stats = [None] * 4
    runs = [
        attend_steps(
            info_ref, x_ref, bias_ref, w_ref, vec_ref, gout_ref, q_ref, k_ref, v_ref, att_ref,
            prob_ref, stats,
        ),
        local_steps(
            info_ref, x_ref, e_ref, hot_ref, turned_ref, w_ref, vec_ref, lout_ref, slope_ref,
            recip_ref, fall_ref, open_ref, bend_ref, bsrc_ref, stats,
        ),
    ]
    while runs:
        runs = [run for run in runs if next(run, 1) is None]
    add_rows(sums_ref, stats)

    @pl.when(pl.program_id(0) == 0)
    def _():
        count = info_ref[1]
        for place in range(2, info_ref.shape[0] - 2):
            count = count + info_ref[place]
        sums_ref[4:5, :] = jnp.full((1, x_ref.shape[1]), count, jnp.int32).astype(f32)


def mix_kernel(
    info_ref, local_ref, global_ref, cot_ref, sums_ref, w_ref, vec_ref,
    low_ref, hlow_ref, slope_ref, mixed_ref, stat_ref,
):
    group = local_ref.shape[0] // BLOCK
    width = local_ref.shape[1]
    sums = sums_ref[...]
    count_row = sums[4:5]
    local_mean, local_rstd = norm_terms(sums, 0, count_row)
    global_mean, global_rstd = norm_terms(sums, 2, count_row)
    local_gain = vec_ref[5:6, :] * local_rstd
    global_gain = vec_ref[7:8, :] * global_rstd
    local_norm = local_ref[...] * local_gain + (vec_ref[6:7, :] - local_mean * local_gain)
    global_norm = global_ref[...] * global_gain + (vec_ref[8:9, :] - global_mean * global_gain)
    summed = low(local_norm).astype(f32) + low(global_norm).astype(f32)
    summed_low = low(summed)
    low_ref[...] = summed_low
    mixed = summed + vec_ref[11:12, :]
    for half in range(2):
        hidden = mm(summed_low, w_ref[9 + half]) + vec_ref[9 + half : 10 + half, :]
        sig_value = sig(hidden)
        hidden_low = low(hidden * sig_value)
        slope_ref[:, half * width : (half + 1) * width] = low(
            sig_value * (1.0 + hidden * (1.0 - sig_value))
        )
        hlow_ref[:, half * width : (half + 1) * width] = hidden_low
        mixed = mixed + mm(hidden_low, w_ref[11 + half])
    mixed_ref[...] = mixed
    live = live_of(info_ref, pl.program_id(0) * group, group, width)
    kept = live * mixed
    d_norm = live * cot_ref[...].astype(f32)
    add_rows(
        stat_ref, [col_sum(kept), col_sum(kept * mixed), col_sum(d_norm), col_sum(d_norm * mixed)]
    )


def hat_kernel(info_ref, local_ref, global_ref, sums_ref, lhat_ref, ghat_ref):
    sums = sums_ref[...]
    for value_ref, hat_ref, first in ((local_ref, lhat_ref, 0), (global_ref, ghat_ref, 2)):
        mean, rstd = norm_terms(sums, first, sums[4:5])
        hat_ref[...] = low((value_ref[...] - mean) * rstd)


def mix_back_kernel(
    info_ref, mixed_ref, slope_ref, cot_ref, lhat_ref, ghat_ref, sums_ref, tops_ref, w_ref,
    vec_ref,
    dmix_ref, dhid_ref, dsum_ref, stat_ref,
):
    group = mixed_ref.shape[0] // BLOCK
    width = mixed_ref.shape[1]
    sums = sums_ref[...]
    tops = tops_ref[...]
    count_row = sums[4:5]
    mean, rstd = norm_terms(tops, 0, count_row)
    live = live_of(info_ref, pl.program_id(0) * group, group, width)
    hat = (mixed_ref[...] - mean) * rstd
    d_norm = live * cot_ref[...].astype(f32)
    dz_sum = tops[2:3]
    dz_hat = (tops[3:4] - mean * dz_sum) * rstd
    d_mixed = (vec_ref[12:13, :] * rstd) * (
        d_norm - live * (dz_sum / count_row + hat * (dz_hat / count_row))
    )
    d_mixed_low = low(d_mixed)
    dmix_ref[...] = d_mixed_low
    d_summed = d_mixed
    for half in range(2):
        cols = slice(half * width, (half + 1) * width)
        d_hidden = low(mm_back(d_mixed_low, w_ref[11 + half]) * slope_ref[:, cols].astype(f32))
        dhid_ref[:, cols] = d_hidden
        d_summed = d_summed + mm_back(d_hidden, w_ref[9 + half])
    d_low = low(d_summed)
    dsum_ref[...] = d_low
    d_sum = d_low.astype(f32)
    add_rows(
        stat_ref,
        [
            col_sum(d_sum),
            col_sum(d_sum * lhat_ref[...].astype(f32)),
            col_sum(d_sum * ghat_ref[...].astype(f32)),
            col_sum(d_mixed),
        ],
    )


def accumulate(acc_ref, term):
    @pl.when(pl.program_id(0) == 0)
    def _():
        acc_ref[...] = jnp.zeros_like(acc_ref)

    acc_ref[...] += term


def layer_kernel(info_ref, mixed_ref, sums_ref, tops_ref, vec_ref, layer_ref):
    group = mixed_ref.shape[0] // BLOCK
    mean, rstd = norm_terms(tops_ref[...], 0, sums_ref[4:5, :])
    live = live_of(info_ref, pl.program_id(0) * group, group, mixed_ref.shape[1])
    hat = (mixed_ref[...] - mean) * rstd
    layer_ref[...] = low(live * (vec_ref[12:13, :] * hat + vec_ref[13:14, :]))


def ones_sum(ref, cols):
    return mm(jnp.ones((8, ref.shape[0]), bf16), ref[:, cols])


def inner_grad_kernel(info_ref, slow_ref, dhid_ref, out_ref, bias_ref):
    accumulate(out_ref, mm_rows(slow_ref[...], dhid_ref[...]))
    accumulate(bias_ref, ones_sum(dhid_ref, slice(None)))


def outer_grad_kernel(info_ref, hlow_ref, dmix_ref, out_ref):
    accumulate(out_ref, mm_rows(hlow_ref[...], dmix_ref[...]))


def norm_back(info_ref, dsum_ref, hat_ref, sums, backs, first, gain_row, hat_row):
    group = hat_ref.shape[0] // BLOCK
    count_row = sums[4:5]
    rstd = norm_terms(sums, first, count_row)[1]
    live = live_of(info_ref, pl.program_id(0) * group, group, hat_ref.shape[1])
    hat = hat_ref[...].astype(f32)
    return (gain_row * rstd) * (
        dsum_ref[...].astype(f32)
        - live * (backs[0:1] / count_row + hat * (backs[hat_row : hat_row + 1] / count_row))
    )


def local_back_steps(
    info_ref, dsum_ref, local_ref, slope_ref, recip_ref, fall_ref, open_ref, bend_ref, bsrc_ref,
    hot_ref, turned_ref, sums_ref, backs_ref, vec_ref,
    dnode_ref, dedge_ref, stat_ref,
):
    group = local_ref.shape[0] // BLOCK
    width = local_ref.shape[1]
    d_local = norm_back(
        info_ref, dsum_ref, local_ref, sums_ref[...], backs_ref[...], 0, vec_ref[5:6, :], 1
    )
    d_gated = d_local * slope_ref[...].astype(f32)
    dnode_ref[:, :width] = low(d_gated)
    d_num = low(d_gated * recip_ref[...].astype(f32))
    d_den = low(-d_gated * fall_ref[...].astype(f32))
    pre_row = jnp.zeros((1, width), f32)
    yield
    picks = [
        mm(
            hot_ref[edges_of(place), :BLOCK],
            jnp.concatenate([d_num[nodes_of(place)], d_den[nodes_of(place)]], axis=1),
        )
        for place in range(group)
    ]
    yield
    sources = []
    for place in range(group):
        edges = edges_of(place)
        d_message = picks[place][:, :width]
        d_open = d_message * bsrc_ref[edges, :].astype(f32) + picks[place][:, width:]
        sources.append(low(d_message * open_ref[edges, :].astype(f32)))
        d_pre = d_open * bend_ref[edges, :].astype(f32)
        pre_row = pre_row + col_sum(d_pre)
        dedge_ref[edges, :] = low(d_pre)
    yield
    for place in range(group):
        nodes = nodes_of(place)
        turned = turned_ref[edges_of(place), :]
        d_both = low(mm(turned, dedge_ref[edges_of(place), :]))
        dnode_ref[nodes, width : 2 * width] = low(mm(turned[BLOCK:], sources[place]))
        dnode_ref[nodes, 2 * width : 3 * width] = d_both[:BLOCK]
        dnode_ref[nodes, 3 * width :] = d_both[BLOCK:]
    add_rows(stat_ref, [col_sum(d_gated), pre_row])


def attend_back_steps(
    info_ref, dsum_ref, global_ref, q_ref, k_ref, v_ref, prob_ref, sums_ref,
    backs_ref, w_ref, vec_ref,
    dqkv_ref, dlow_ref, stat_ref, score_ref,
):
    group = global_ref.shape[0] // BLOCK
    width = global_ref.shape[1]
    score_scale = (width // HEADS) ** (-0.5)
    d_global = norm_back(
        info_ref, dsum_ref, global_ref, sums_ref[...], backs_ref[...], 2, vec_ref[7:8, :], 2
    )
    d_low = low(d_global)
    dlow_ref[...] = d_low
    d_att = low(mm_back(d_low, w_ref[8]))
    masks = head_masks(width)
    tall = tall_masks(width)
    turned_att = low(mm_back(w_ref[8], d_low))
    yield
    d_probs = [
        mm(v_ref[nodes_of(place), :], side_stack(turned_att[:, nodes_of(place)], tall))
        for place in range(group)
    ]
    yield
    for place in range(group):
        nodes = nodes_of(place)
        for head in range(HEADS):
            cols = nodes_of(head)
            prob = prob_ref[nodes, cols].astype(f32)
            part = d_probs[place][:, cols]
            inner = jnp.sum(prob * part, axis=0, keepdims=True)
            d_score = low(prob * ((part - inner) * score_scale))
            score_ref[nodes, cols] = d_score
    yield
    for place in range(group):
        nodes = nodes_of(place)
        dqkv_ref[nodes, :width] = turned_product(k_ref[nodes, :].T, score_ref, nodes, width // HEADS)
        dqkv_ref[nodes, width : 2 * width] = low(
            mm(score_ref[nodes, :], head_stack(q_ref[nodes, :], masks))
        )
        dqkv_ref[nodes, 2 * width :] = low(
            mm(prob_ref[nodes, :], head_stack(d_att[nodes], masks))
        )
    add_rows(
        stat_ref,
        [
            col_sum(d_global),
        ],
    )


def back_kernel(
    info_ref, dsum_ref, lhat_ref, slope_ref, recip_ref, fall_ref, open_ref, bend_ref, bsrc_ref,
    hot_ref, turned_ref, ghat_ref, q_ref, k_ref, v_ref, prob_ref, sums_ref, backs_ref, w_ref,
    vec_ref,
    dnode_ref, dedge_ref, lstat_ref, dqkv_ref, dlow_ref, gstat_ref, score_ref,
):
    runs = [
        attend_back_steps(
            info_ref, dsum_ref, ghat_ref, q_ref, k_ref, v_ref, prob_ref, sums_ref, backs_ref,
            w_ref, vec_ref, dqkv_ref, dlow_ref, gstat_ref, score_ref,
        ),
        local_back_steps(
            info_ref, dsum_ref, lhat_ref, slope_ref, recip_ref, fall_ref, open_ref, bend_ref,
            bsrc_ref, hot_ref, turned_ref, sums_ref, backs_ref, vec_ref, dnode_ref, dedge_ref,
            lstat_ref,
        ),
    ]
    while runs:
        runs = [run for run in runs if next(run, 1) is None]


def branch_grad_kernel(
    info_ref, x_ref, e_ref, att_ref, dnode_ref, dedge_ref, dqkv_ref, dlow_ref, igrad_ref, ograd_ref,
    *outs,
):
    outs, bias_ref, (node_ref, wide_ref, edge_ref, acc_ref) = outs[:-5], outs[-5], outs[-4:]
    width = x_ref.shape[1]
    for place in (0, 2):
        bias_ref[:, place // 2 * width : (place // 2 + 1) * width] = ones_sum(
            dqkv_ref, slice(place * width, (place + 1) * width)
        )
    x = x_ref[...]
    node_ref[...] = mm_rows(x, dnode_ref[...])
    wide_ref[...] = mm_rows(x, dqkv_ref[...])
    edge_ref[...] = mm_rows(e_ref[...], dedge_ref[...])
    acc_ref[...] = mm_rows(att_ref[...], dlow_ref[...])
    cols = [slice(place * width, (place + 1) * width) for place in range(4)]
    parts = [node_ref.at[:, cols[0]], node_ref.at[:, cols[1]], edge_ref]
    parts = parts + [node_ref.at[:, cols[2]], node_ref.at[:, cols[3]]]
    parts = parts + [wide_ref.at[:, cols[place]] for place in range(3)] + [acc_ref]
    parts = parts + [igrad_ref.at[:, cols[place]] for place in range(2)]
    parts = parts + [ograd_ref.at[cols[place], :] for place in range(2)]
    if len(outs) == 1:
        for place, part in enumerate(parts):
            outs[0][place] = low(part[...])
    else:
        pack(info_ref, parts, outs)


def reach(order, index):
    found = 0
    for place, step in enumerate(order):
        if index >> (len(order) - 1 - place) & 1:
            found ^= step >> 1
    return found


def chip_orders(total):
    chips = steps_of(total)[1:]
    return (chips, chips[1:-1] + chips[:1] + chips[-1:])


def pack(info_ref, parts, outs):
    half = outs[0].shape[0]
    slots = 2 * half
    orders = chip_orders(2 * slots)
    core = info_ref[info_ref.shape[0] - 2]
    chip = info_ref[info_ref.shape[0] - 1]
    for slot in range(slots):
        near = [reach(order, slot) for order in orders]
        for out_ref, owner in zip(outs[slot // half :: 2], (core, 1 - core)):
            step = jnp.where(owner == 0, near[0], near[1])
            row = pl.multiple_of(16 * jnp.bitwise_xor(chip, step) + 8 * owner, 8)
            for first in range(0, len(parts), 2):
                pair = [part[pl.ds(row, 8), :] for part in parts[first : first + 2]]
                out_ref[slot % half, first * 8 : first * 8 + 8 * len(pair), :] = low(
                    jnp.concatenate(pair, axis=0)
                )


def assemble_kernel(info_ref, near_ref, far_ref, near_other_ref, far_other_ref, out_ref):
    half, tall, _ = near_ref.shape
    slots = 2 * half
    orders = chip_orders(2 * slots)
    core = info_ref[info_ref.shape[0] - 2]
    chip = info_ref[info_ref.shape[0] - 1]

    def fill(even_refs, odd_refs):
        for far in range(slots):
            even, odd = [
                [slot for slot in range(slots) if reach(order, slot) == far][0] for order in orders
            ]
            row = pl.multiple_of(16 * jnp.bitwise_xor(chip, far), 16)
            for first in range(0, tall, 16):
                size = min(16, tall - first)
                part = slice(first, first + size)
                upper = even_refs[even // half][even % half, part, :].astype(f32)
                lower = odd_refs[odd // half][odd % half, part, :].astype(f32)
                for step in range(size // 8):
                    rows = slice(step * 8, step * 8 + 8)
                    out_ref[first // 8 + step, pl.ds(row, 16), :] = low(
                        jnp.concatenate([upper[rows], lower[rows]], axis=0)
                    )

    @pl.when(core == 0)
    def _():
        fill((near_ref, far_ref), (near_other_ref, far_other_ref))

    @pl.when(core != 0)
    def _():
        fill((near_other_ref, far_other_ref), (near_ref, far_ref))


def node_grad_kernel(
    info_ref, dsum_ref, lhat_ref, ghat_ref, dnode_ref, dqkv_ref, sums_ref, backs_ref, w_ref,
    vec_ref,
    node_ref,
):
    width = lhat_ref.shape[1]
    sums = sums_ref[...]
    backs = backs_ref[...]
    total = norm_back(info_ref, dsum_ref, lhat_ref, sums, backs, 0, vec_ref[5:6, :], 1)
    total = total + norm_back(info_ref, dsum_ref, ghat_ref, sums, backs, 2, vec_ref[7:8, :], 2)
    for place, mat in enumerate((0, 1, 3, 4)):
        total = total + mm_back(dnode_ref[:, place * width : (place + 1) * width], w_ref[mat])
    for place in range(3):
        total = total + mm_back(dqkv_ref[:, place * width : (place + 1) * width], w_ref[5 + place])
    node_ref[...] = total


def edge_grad_kernel(info_ref, dedge_ref, w_ref, edge_ref):
    edge_ref[...] = mm_back(dedge_ref[...], w_ref[2])


def bias_rows(local_ref, attend_ref, inner_ref, wide_ref):
    width = attend_ref.shape[1]
    return jnp.concatenate(
        [
            local_ref[0:2, :],
            wide_ref[0:1, :width],
            wide_ref[0:1, width:],
            attend_ref[0:1, :],
            inner_ref[0:1, :width],
            inner_ref[0:1, width:],
            jnp.zeros((1, width), f32),
        ],
        axis=0,
    )


def last_kernel(
    info_ref, kept_ref, got_ref, local_ref, attend_ref, inner_ref, wide_ref, out_ref
):
    biases = bias_rows(local_ref, attend_ref, inner_ref, wide_ref)
    upper = low(biases).astype(f32)
    for slot, extra in enumerate((upper, biases - upper)):
        total = kept_ref[slot].astype(f32) + got_ref[slot].astype(f32)
        out_ref[slot] = low(jnp.concatenate([total, extra], axis=0))


def total_square(values):
    return jnp.sum(jnp.sum(values * values, axis=0, keepdims=True), axis=1, keepdims=True)


def pair_kernel(info_ref, mine_ref, got_ref, grad_ref, tail_ref):
    rows = grad_ref.shape[1]
    half = grad_ref.shape[2]
    mine = [mine_ref[slot].astype(f32) for slot in range(2)]
    got = [got_ref[slot].astype(f32) for slot in range(2)]
    grad = mine[0][:rows] + got[1][:rows]
    other = mine[1][:rows] + got[0][:rows]
    grad_ref[0] = grad[:, :half]
    grad_ref[1] = grad[:, half:]
    tail_ref[...] = (mine[0][rows:] + mine[1][rows:]) + (got[0][rows:] + got[1][rows:])
    tail_ref[7:8, :] = jnp.broadcast_to(total_square(grad) + total_square(other), (1, 2 * half))


def square_kernel(
    info_ref, kept_ref, got_ref, local_ref, attend_ref, inner_ref, wide_ref, grad_ref, tail_ref
):
    grad = kept_ref[...].astype(f32) + got_ref[...].astype(f32)
    half = grad.shape[1] // 2
    grad_ref[0] = grad[:, :half]
    grad_ref[1] = grad[:, half:]
    tail_ref[...] = bias_rows(local_ref, attend_ref, inner_ref, wide_ref)
    tail_ref[7:8, :] = jnp.broadcast_to(total_square(grad), (1, tail_ref.shape[1]))


def update_kernel(
    info_ref, grad_ref, tail_ref, sums_ref, tops_ref, backs_ref, w_ref, w1_ref, w2_ref, v_ref,
    v1_ref, v2_ref,
    new_w_ref, new_w1_ref, new_w2_ref, new_v_ref, new_v1_ref, new_v2_ref, norm_ref,
):
    tail = tail_ref[...]
    tops = tops_ref[...]
    backs = backs_ref[...]
    mean, rstd = norm_terms(tops, 0, sums_ref[4:5, :])
    grad_v = jnp.concatenate(
        [
            tail[0:5],
            backs[1:2],
            backs[0:1],
            backs[2:3],
            backs[0:1],
            tail[5:7],
            backs[3:4],
            (tops[3:4] - mean * tops[2:3]) * rstd,
            tops[2:3],
        ],
        axis=0,
    )
    square = jnp.sum(jnp.sum(grad_v * grad_v, axis=0, keepdims=True), axis=1, keepdims=True)
    norm = jnp.sqrt(tail[7:8, 0:1] + square)
    norm_ref[...] = norm
    factor = jnp.minimum(1.0, clip_limit / (norm + 1e-06))
    new_v_ref[...], new_v1_ref[...], new_v2_ref[...] = adamw(
        v_ref[...], factor * grad_v, v1_ref[...], v2_ref[...], rate_vecs, 0.0
    )
    mats, span = w_ref.shape
    _, rows, half = grad_ref.shape
    for piece in range(span // half):
        cols = slice(piece * half, (piece + 1) * half)
        if rows == mats:
            grad = grad_ref[piece]
        else:
            grad = grad_ref[piece % 2, pl.ds(piece // 2, mats, rows // mats), :]
        new_w_ref[:, cols], new_w1_ref[:, cols], new_w2_ref[:, cols] = adamw(
            w_ref[:, cols], factor * grad, w1_ref[:, cols], w2_ref[:, cols], rate_mats, decay_mats
        )


def rows_spec(rows, width, offset=0):
    if offset:
        return pl.BlockSpec((rows, width), lambda step, info: (step + info[0], 0))
    return pl.BlockSpec((rows, width), lambda step, info: (step, 0))


def whole_spec(shape):
    zeros = (0,) * len(shape)
    return pl.BlockSpec(shape, lambda step, info: zeros)


def call(kernel, steps, info, inputs, outputs, scratch=(), room=10, cost=5):
    in_specs = []
    arrays = []
    for array, spec in inputs:
        arrays.append(array)
        in_specs.append(whole_spec(array.shape) if spec is None else spec)
    out_specs = []
    out_shapes = []
    for shape, dtype, spec, *far in outputs:
        out_specs.append(whole_spec(shape) if spec is None else spec)
        out_shapes.append(pltpu.HBM(shape, dtype) if far else jax.ShapeDtypeStruct(shape, dtype))
    return pl.pallas_call(
        kernel,
        grid_spec=pltpu.PrefetchScalarGridSpec(
            num_scalar_prefetch=1,
            grid=(steps,),
            in_specs=in_specs,
            out_specs=out_specs,
            scratch_shapes=list(scratch),
        ),
        out_shape=out_shapes,
        compiler_params=pltpu.CompilerParams(
            dimension_semantics=("arbitrary",), vmem_limit_bytes=room * 1024 * 1024
        ),
        name=kernel.__name__,
        cost_estimate=pl.CostEstimate(
            flops=cost * 1000000000, bytes_accessed=cost * 1000000, transcendentals=0
        ),
    )(info, *arrays)


def swap_with(values, step, total):
    return lax.ppermute(values, axis_names, [(place, place ^ step) for place in range(total)])


def steps_of(total):
    return [1 << power for power in range(total.bit_length() - 1)]


def beside(start, transfer, info, work):
    info = lax.optimization_barrier((info, start))[0]
    return lax.optimization_barrier((transfer, work(info)))


def sum_small(values, total, info=None, works=()):
    results = []
    works = list(works)
    for step in steps_of(total):
        other = swap_with(values, step, total)
        if works and step > 1:
            other, done = beside(values, other, info, works.pop(0))
            results.append(done)
        values = values + other
    return (values, results) if results else values


def swap_chips(values, number, total):
    orders = chip_orders(total)
    return lax.ppermute(
        values,
        axis_names,
        [(place, place ^ orders[place % 2][number]) for place in range(total)],
    )


def in_rows(total, width):
    return width * width // total == 8 * width


def gather_matrices(shard, info, total, width, work):
    mats = shard.shape[0]
    if not in_rows(total, width):
        gathered = lax.all_gather(shard, axis_names, axis=1, tiled=True)
        return (gathered.reshape(mats, width, width), work(info))
    held = shard.reshape(1, mats * 8, width)
    for number in reversed(range(1, len(chip_orders(total)[0]))):
        held = jnp.concatenate([held, swap_chips(held, number, total)], axis=0)
    got = swap_chips(held, 0, total)
    other = swap_with(held, 1, total)

    def both(info):
        return (work(info), other)

    got, (done, other) = beside(held, got, info, both)
    far_other = swap_with(got, 1, total)
    matrices = call(
        assemble_kernel,
        1,
        info,
        [(held, None), (got, None), (other, None), (far_other, None)],
        [((mats, width, width), bf16, None)],
    )[0]
    return (matrices, done)


def scatter_plain(grads, total):
    place = lax.axis_index(axis_names)
    mats, width, _ = grads.shape
    bits = total.bit_length() - 1
    held = grads.reshape((mats,) + (2,) * bits + (width * width // total,))
    held = held.transpose(tuple(reversed(range(1, bits + 1))) + (0, bits + 1))
    for step in steps_of(total):
        mine = ((place & step) != 0).astype(jnp.int32)
        sent = lax.dynamic_index_in_dim(held, 1 - mine, 0, keepdims=False)
        kept = lax.dynamic_index_in_dim(held, mine, 0, keepdims=False)
        got = swap_with(sent, step, total)
        if step * 2 < total:
            held = low(kept.astype(f32) + got.astype(f32))
    return (kept, got)


def scatter_packed(kept, far_kept, sent, far_sent, total, info, works, biases):
    far_got = swap_with(far_sent, 1, total)
    got = swap_with(sent, 1, total)
    results = []
    rounds = len(chip_orders(total)[0])
    for number in range(rounds - 1):
        if number:
            half = kept.shape[0] // 2
            far_kept, far_got = kept[half:], got[half:]
            kept, got = kept[:half], got[:half]
        sent = low(far_kept.astype(f32) + far_got.astype(f32))
        kept = kept.astype(f32) + got.astype(f32)
        got = swap_chips(sent, number, total)
        if number < len(works):
            got, done = beside(sent, got, info, works[number])
            results.append(done)
    mine = call(
        last_kernel,
        1,
        info,
        [(array, None) for array in (kept, got, *biases)],
        [((2, kept.shape[1] + 8, kept.shape[2]), bf16, None)],
    )[0]
    got = swap_chips(mine, rounds - 1, total)
    grad_rows, tail = call(
        pair_kernel,
        1,
        info,
        [(mine, None), (got, None)],
        [((2, kept.shape[1], kept.shape[2] // 2), f32, None), ((8, kept.shape[2]), f32, None)],
    )
    for step in steps_of(total)[:-1]:
        tail = tail + swap_with(tail, step, total)
    return (grad_rows, tail, results)


def adamw(params, gradient, moment_one, moment_two, rate, decay):
    first = beta_one * moment_one + (1.0 - beta_one) * gradient
    second = beta_two * moment_two + (1.0 - beta_two) * gradient * gradient
    first_hat = first / (1.0 - beta_one**STEP)
    second_hat = second / (1.0 - beta_two**STEP)
    updated = params - rate * (first_hat / (jnp.sqrt(second_hat) + adam_eps) + decay * params)
    return (updated, first, second)


def own_half(values, branch_index):
    half = values.shape[0] // 2
    return lax.dynamic_slice_in_dim(values, branch_index * half, half, 0)


def per_device(
    node_feats,
    edge_feats,
    cotangent,
    graph_ids,
    node_mask,
    edge_src,
    edge_dst,
    edge_mask,
    weights,
    weight_moment1,
    weight_moment2,
    vectors,
    vector_moment1,
    vector_moment2,
):
    total = lax.axis_size("rows") * lax.axis_size("branch")
    branch_index = lax.axis_index("branch")
    width = node_feats.shape[1]
    rows = node_feats.shape[0] // 2
    edges = edge_feats.shape[0] // 2
    blocks = rows // BLOCK
    group = math.gcd(blocks, GROUP)
    steps = blocks // group
    tall = group * BLOCK
    tall_edges = group * EB
    w_bf = low(weights)
    own_nodes = own_half(node_feats, branch_index)
    own_edges = own_half(edge_feats, branch_index)
    counts = jnp.sum(own_half(node_mask, branch_index).reshape(blocks, BLOCK), axis=1)
    info = jnp.concatenate(
        [(branch_index * steps)[None], counts, branch_index[None], lax.axis_index("rows")[None]]
    ).astype(jnp.int32)

    def by_step(values, slots):
        return own_half(values, branch_index).reshape(steps, group, slots)

    def step_spec(slots):
        return pl.BlockSpec((1, group, slots), lambda step, info: (step, 0, 0))

    edge_spec = rows_spec(tall_edges, width)
    node_spec = rows_spec(tall, width)
    def prep_work(info):
        return call(
            prep_kernel,
            steps,
            info,
            [
                (by_step(edge_src, EB), step_spec(EB)),
                (by_step(edge_dst, EB), step_spec(EB)),
                (by_step(edge_mask, EB), step_spec(EB)),
                (by_step(graph_ids, BLOCK), step_spec(BLOCK)),
            ],
            [
                ((edges, EB), bf16, edge_spec, True),
                ((edges, EB), bf16, edge_spec, True),
                ((rows, BLOCK), f32, rows_spec(tall, BLOCK)),
            ],
        )

    matrices, (hot, turned, bias) = gather_matrices(w_bf, info, total, width, prep_work)
    x_in = (own_nodes, node_spec)
    e_in = (own_edges, edge_spec)
    mats_in = (matrices, None)
    vec_in = (vectors, None)
    node_f32 = ((rows, width), f32, node_spec)
    node_bf = ((rows, width), bf16, node_spec)
    sums_out = ((8, width), f32, None)
    prob_spec = rows_spec(tall, HEADS * BLOCK)
    (
        local_out, gate_slope, recip, fall, opened, bend, b_source,
        global_out, queries, keyed, valued, attended, probs, sums_part,
    ) = call(
        forward_kernel,
        steps,
        info,
        [
            x_in,
            e_in,
            (bias, rows_spec(tall, BLOCK)),
            (hot, edge_spec),
            (turned, edge_spec),
            mats_in,
            vec_in,
        ],
        [
            node_f32,
            node_bf,
            node_bf,
            node_bf,
            ((edges, width), bf16, edge_spec),
            ((edges, width), bf16, edge_spec),
            ((edges, width), bf16, edge_spec),
            node_f32,
            node_bf,
            node_bf,
            node_bf,
            node_bf,
            ((rows, HEADS * BLOCK), bf16, prob_spec),
            sums_out,
        ],
        room=FRONT_ROOM,
    )
    sums = sum_small(sums_part, total)
    sums_in = (sums, None)
    cot_in = (cotangent, node_spec)
    wide_spec = rows_spec(tall, 2 * width)
    summed_low, hidden_low, hidden_slope, mixed, top_part = call(
        mix_kernel,
        steps,
        info,
        [(local_out, node_spec), (global_out, node_spec), cot_in, sums_in, mats_in, vec_in],
        [
            node_bf,
            ((rows, 2 * width), bf16, wide_spec),
            ((rows, 2 * width), bf16, wide_spec),
            node_f32,
            sums_out,
        ],
    )

    def hat_work(info):
        return call(
            hat_kernel,
            steps,
            info,
            [(local_out, node_spec), (global_out, node_spec), sums_in],
            [node_bf, node_bf],
        )

    tops, ((local_hat, global_hat),) = sum_small(top_part, total, info, [hat_work])
    d_mixed, d_hidden, d_summed, back_part = call(
        mix_back_kernel,
        steps,
        info,
        [
            (mixed, node_spec),
            (hidden_slope, wide_spec),
            cot_in,
            (local_hat, node_spec),
            (global_hat, node_spec),
            sums_in,
            (tops, None),
            mats_in,
            vec_in,
        ],
        [
            node_bf,
            ((rows, 2 * width), bf16, wide_spec),
            node_bf,
            sums_out,
        ],
    )

    def mat_out(tall_by, wide_by):
        return ((tall_by * width, wide_by * width), f32, None)

    def inner_work(info):
        return call(
            inner_grad_kernel,
            steps,
            info,
            [(summed_low, node_spec), (d_hidden, wide_spec)],
            [mat_out(1, 2), ((8, 2 * width), f32, None)],
        )

    def outer_work(info):
        return call(
            outer_grad_kernel,
            steps,
            info,
            [(hidden_low, wide_spec), (d_mixed, node_spec)],
            [mat_out(2, 1)],
        )[0]

    def layer_work(info):
        return call(
            layer_kernel,
            steps,
            info,
            [(mixed, node_spec), sums_in, (tops, None), vec_in],
            [node_bf],
        )[0]

    backs, ((inner_grads, inner_bias), outer_grads, layer_out) = sum_small(
        back_part, total, info, [inner_work, outer_work, layer_work]
    )
    backs_in = (backs, None)
    dsum_in = (d_summed, node_spec)
    dnode_spec = rows_spec(tall, 4 * width)
    dqkv_spec = rows_spec(tall, 3 * width)
    slots = total // 2
    packed = in_rows(total, width)
    grad_outs = [((MATS, width, width), bf16, None)]
    if packed:
        grad_outs = [((slots // 2, MATS * 8, width), bf16, None)] * 4
    d_node, d_edge, local_bias, d_qkv, d_low, attend_bias = call(
        back_kernel,
        steps,
        info,
        [
            dsum_in,
            (local_hat, node_spec),
            (gate_slope, node_spec),
            (recip, node_spec),
            (fall, node_spec),
            (opened, edge_spec),
            (bend, edge_spec),
            (b_source, edge_spec),
            (hot, edge_spec),
            (turned, edge_spec),
            (global_hat, node_spec),
            (queries, node_spec),
            (keyed, node_spec),
            (valued, node_spec),
            (probs, prob_spec),
            sums_in,
            backs_in,
            mats_in,
            vec_in,
        ],
        [
            ((rows, 4 * width), bf16, dnode_spec),
            ((edges, width), bf16, edge_spec),
            sums_out,
            ((rows, 3 * width), bf16, dqkv_spec),
            node_bf,
            sums_out,
        ],
        [pltpu.VMEM((tall, HEADS * BLOCK), bf16)],
        room=BACK_ROOM,
    )
    *grads, wide_bias = call(
        branch_grad_kernel,
        1,
        info,
        [
            (own_nodes, None),
            (own_edges, None),
            (attended, None),
            (d_node, None),
            (d_edge, None),
            (d_qkv, None),
            (d_low, None),
            (inner_grads, None),
            (outer_grads, None),
        ],
        grad_outs + [((8, 2 * width), f32, None)],
        [
            pltpu.VMEM((width, 4 * width), f32),
            pltpu.VMEM((width, 3 * width), f32),
            pltpu.VMEM((width, width), f32),
            pltpu.VMEM((width, width), f32),
        ],
    )

    def node_work(info):
        return call(
            node_grad_kernel,
            steps,
            info,
            [
                dsum_in,
                (local_hat, node_spec),
                (global_hat, node_spec),
                (d_node, dnode_spec),
                (d_qkv, dqkv_spec),
                sums_in,
                backs_in,
                mats_in,
                vec_in,
            ],
            [node_f32],
        )[0]

    def edge_work(info):
        return call(
            edge_grad_kernel,
            steps,
            info,
            [(d_edge, edge_spec), mats_in],
            [((edges, width), f32, edge_spec)],
        )[0]

    biases = (local_bias, attend_bias, inner_bias, wide_bias)
    if packed:
        grad_rows, tail, (node_grad, edge_grad) = scatter_packed(
            *grads, total, info, [node_work, edge_work], biases
        )
    else:
        grad_shard = scatter_plain(grads[0], total)
        node_grad, edge_grad = node_work(info), edge_work(info)
        grad_rows, tail_part = call(
            square_kernel,
            1,
            info,
            [(array, None) for array in (*grad_shard, *biases)],
            [
                ((2, grad_shard[0].shape[0], grad_shard[0].shape[1] // 2), f32, None),
                sums_out,
            ],
        )
        tail = sum_small(tail_part, total)
    like_mats = (weights.shape, f32, None)
    like_vecs = (vectors.shape, f32, None)
    new_weights, first_w, second_w, new_vectors, first_v, second_v, norm = call(
        update_kernel,
        1,
        info,
        [
            (array, None)
            for array in (
                grad_rows, tail, sums, tops, backs, weights, weight_moment1, weight_moment2,
                vectors, vector_moment1, vector_moment2,
            )
        ],
        [like_mats] * 3 + [like_vecs] * 3 + [((1, 1), f32, None)],
    )
    grad_norm = norm.reshape(())
    return (
        layer_out,
        node_grad,
        edge_grad,
        new_weights,
        first_w,
        second_w,
        new_vectors,
        first_v,
        second_v,
        grad_norm,
    )


def solution(mesh):
    in_specs = (
        P("rows", None),
        P("rows", None),
        P(("rows", "branch"), None),
        P("rows"),
        P("rows"),
        P("rows"),
        P("rows"),
        P("rows"),
        P(None, ("rows", "branch")),
        P(None, ("rows", "branch")),
        P(None, ("rows", "branch")),
        P(),
        P(),
        P(),
    )
    out_specs = (
        P(("rows", "branch"), None),
        P(("rows", "branch"), None),
        P(("rows", "branch"), None),
        P(None, ("rows", "branch")),
        P(None, ("rows", "branch")),
        P(None, ("rows", "branch")),
        P(),
        P(),
        P(),
        P(),
    )
    return jax.shard_map(
        per_device, mesh=mesh, in_specs=in_specs, out_specs=out_specs, check_vma=False
    )
```

```python
import functools
import math

import jax
import jax.numpy as jnp
from jax import lax
from jax.experimental import pallas as pl
from jax.experimental.pallas import tpu as pltpu
from jax.sharding import PartitionSpec as P

HEADS = 8
BLOCK = 128
EB = 256
MATS = 13
STEP = 7
GROUP = 8
BACK_ROOM = 12
FRONT_ROOM = 12

eps_norm = 1e-05
clip_limit = 1.0
beta_one = 0.9
beta_two = 0.999
rate_mats = 0.1
rate_vecs = 0.8
decay_mats = 0.01
adam_eps = 1e-08
hidden_floor = -1e30
axis_names = ("rows", "branch")
f32 = jnp.float32
bf16 = jnp.bfloat16


def mm(left, right):
    return jnp.dot(left, right, preferred_element_type=f32)


def mm_back(left, right):
    return lax.dot_general(left, right, (((1,), (1,)), ((), ())), preferred_element_type=f32)


def mm_rows(left, right):
    return lax.dot_general(left, right, (((0,), (0,)), ((), ())), preferred_element_type=f32)


def low(values):
    return values.astype(bf16)


def sig(values):
    return 0.5 * jnp.tanh(0.5 * values) + 0.5


def col_sum(values):
    return jnp.sum(values, axis=0, keepdims=True)


def live_of(info_ref, first_block, group, width):
    slot = lax.broadcasted_iota(jnp.int32, (BLOCK, width), 0)
    return jnp.concatenate(
        [
            jnp.where(slot < info_ref[1 + first_block + place], 1.0, 0.0)
            for place in range(group)
        ],
        axis=0,
    )


def nodes_of(place):
    return slice(place * BLOCK, (place + 1) * BLOCK)


def edges_of(place):
    return slice(place * EB, (place + 1) * EB)


def add_rows(out_ref, rows):
    @pl.when(pl.program_id(0) == 0)
    def _():
        out_ref[...] = jnp.zeros_like(out_ref)

    for place, row in enumerate(rows):
        out_ref[place : place + 1, :] += row


def norm_terms(sums, first, count_row):
    mean = sums[first : first + 1] / count_row
    rstd = lax.rsqrt(sums[first + 1 : first + 2] / count_row - mean * mean + eps_norm)
    return (mean, rstd)


def prep_kernel(info_ref, src_ref, dst_ref, mask_ref, id_ref, hot_ref, turned_ref, bias_ref):
    for place in range(GROUP):
        row = pl.ds(place, 1)
        node = lax.broadcasted_iota(jnp.int32, (BLOCK, EB), 0)
        live = mask_ref[0, row, :] != 0
        dst_rows = jnp.where((node == dst_ref[0, row, :]) & live, 1.0, 0.0)
        src_rows = jnp.where((node == src_ref[0, row, :]) & live, 1.0, 0.0)
        turned = jnp.concatenate([dst_rows, src_rows], axis=0)
        turned_ref[place * EB : (place + 1) * EB, :] = low(turned)
        hot_ref[place * EB : (place + 1) * EB, :] = low(turned.T)
        ids = jnp.broadcast_to(id_ref[0, row, :].astype(f32), (BLOCK, BLOCK))
        bias_ref[place * BLOCK : (place + 1) * BLOCK, :] = jnp.where(
            ids == ids.T, 0.0, hidden_floor
        )


def local_steps(
    info_ref, x_ref, e_ref, hot_ref, turned_ref, w_ref, vec_ref,
    out_ref, slope_ref, recip_ref, fall_ref, open_ref, bend_ref, bsrc_ref, stats,
):
    group = x_ref.shape[0] // BLOCK
    x = x_ref[...]
    a_part = mm(x, w_ref[0]) + vec_ref[0:1, :]
    b_part = low(mm(x, w_ref[1]))
    d_part = low(mm(x, w_ref[3]))
    e_part = low(mm(x, w_ref[4]))
    c_part = mm(e_ref[...], w_ref[2]) + vec_ref[1:2, :]
    gates = []
    picks = []
    for place in range(group):
        nodes = nodes_of(place)
        hot = hot_ref[edges_of(place), :]
        gates.append(mm(hot, jnp.concatenate([d_part[nodes], e_part[nodes]], axis=0)))
        picks.append(mm(hot[:, BLOCK:], b_part[nodes]))
    yield
    sums = []
    for place in range(group):
        edges = edges_of(place)
        opened = sig(c_part[edges] + gates[place])
        b_source = picks[place]
        opened_low = low(opened)
        open_ref[edges, :] = opened_low
        bend_ref[edges, :] = low(opened * (1.0 - opened))
        bsrc_ref[edges, :] = low(b_source)
        dst_turned = turned_ref[place * EB : place * EB + BLOCK, :]
        sums.append(
            mm(dst_turned, jnp.concatenate([low(opened * b_source), opened_low], axis=1))
        )
    yield
    both = jnp.concatenate(sums, axis=0)
    width = x.shape[1]
    recip = 1.0 / (both[:, width:] + 1.0)
    ratio = both[:, :width] * recip
    gated = a_part + ratio
    gated_sig = sig(gated)
    out = x.astype(f32) + gated * gated_sig
    slope_ref[...] = low(gated_sig * (1.0 + gated * (1.0 - gated_sig)))
    recip_ref[...] = low(recip)
    fall_ref[...] = low(ratio * recip)
    out_ref[...] = out
    live = live_of(info_ref, pl.program_id(0) * group, group, out.shape[1])
    kept = live * out
    stats[0:2] = [col_sum(kept), col_sum(kept * out)]


def head_masks(width):
    head = lax.broadcasted_iota(jnp.int32, (16, width), 1) // (width // HEADS)
    return [low(jnp.where(head == place, 1.0, 0.0))[:1] for place in range(HEADS)]


def head_stack(values, masks):
    return jnp.concatenate([values * mask for mask in masks], axis=0)


def tall_masks(width):
    head = lax.broadcasted_iota(jnp.int32, (width, BLOCK), 0) // (width // HEADS)
    return [low(jnp.where(head == place, 1.0, 0.0)) for place in range(HEADS)]


def side_stack(turned, masks):
    return jnp.concatenate([turned * mask for mask in masks], axis=1)


def turned_product(turned, weight, nodes, size):
    parts = []
    for head in range(0, HEADS, 2):
        both = mm(
            turned[head * size : (head + 2) * size],
            weight[nodes, head * BLOCK : (head + 2) * BLOCK],
        )
        parts += [both[:size, :BLOCK], both[size:, BLOCK:]]
    return low(jnp.concatenate(parts, axis=0)).T


def attend_steps(
    info_ref, x_ref, bias_ref, w_ref, vec_ref,
    out_ref, q_ref, k_ref, v_ref, att_ref, prob_ref, stats,
):
    group = x_ref.shape[0] // BLOCK
    x = x_ref[...]
    queries = low(mm(x, w_ref[5]) + vec_ref[2:3, :])
    keyed = low(mm(x, w_ref[6]))
    valued = low(mm(x, w_ref[7]) + vec_ref[3:4, :])
    q_ref[...] = queries
    k_ref[...] = keyed
    v_ref[...] = valued
    score_scale = (x.shape[1] // HEADS) ** (-0.5) * math.log2(math.e)
    tall = tall_masks(x.shape[1])
    queries_turned = queries.T
    valued_turned = valued.T
    size = x.shape[1] // HEADS
    raws = [
        mm(keyed[nodes_of(place)], side_stack(queries_turned[:, nodes_of(place)], tall))
        for place in range(group)
    ]
    yield
    for place in range(group):
        nodes = nodes_of(place)
        bias = bias_ref[nodes, :]
        for head in range(HEADS):
            cols = nodes_of(head)
            part = raws[place][:, cols] + bias
            part = jnp.exp2((part - jnp.max(part, axis=0, keepdims=True)) * score_scale)
            prob_ref[nodes, cols] = low(part * (1.0 / jnp.sum(part, axis=0, keepdims=True)))
    yield
    for place in range(group):
        nodes = nodes_of(place)
        att_ref[nodes, :] = turned_product(valued_turned[:, nodes], prob_ref, nodes, size)
    out = x.astype(f32) + mm(att_ref[...], w_ref[8]) + vec_ref[4:5, :]
    out_ref[...] = out
    live = live_of(info_ref, pl.program_id(0) * group, group, out.shape[1])
    kept = live * out
    stats[2:4] = [col_sum(kept), col_sum(kept * out)]


def forward_kernel(
    info_ref, x_ref, e_ref, bias_ref, hot_ref, turned_ref, w_ref, vec_ref,
    lout_ref, slope_ref, recip_ref, fall_ref, open_ref, bend_ref, bsrc_ref,
    gout_ref, q_ref, k_ref, v_ref, att_ref, prob_ref, sums_ref,
):
    stats = [None] * 4
    runs = [
        attend_steps(
            info_ref, x_ref, bias_ref, w_ref, vec_ref, gout_ref, q_ref, k_ref, v_ref, att_ref,
            prob_ref, stats,
        ),
        local_steps(
            info_ref, x_ref, e_ref, hot_ref, turned_ref, w_ref, vec_ref, lout_ref, slope_ref,
            recip_ref, fall_ref, open_ref, bend_ref, bsrc_ref, stats,
        ),
    ]
    while runs:
        runs = [run for run in runs if next(run, 1) is None]
    add_rows(sums_ref, stats)

    @pl.when(pl.program_id(0) == 0)
    def _():
        count = info_ref[1]
        for place in range(2, info_ref.shape[0] - 2):
            count = count + info_ref[place]
        sums_ref[4:5, :] = jnp.full((1, x_ref.shape[1]), count, jnp.int32).astype(f32)


def mix_kernel(
    info_ref, local_ref, global_ref, cot_ref, sums_ref, w_ref, vec_ref,
    low_ref, hlow_ref, slope_ref, mixed_ref, stat_ref,
):
    group = local_ref.shape[0] // BLOCK
    width = local_ref.shape[1]
    sums = sums_ref[...]
    count_row = sums[4:5]
    local_mean, local_rstd = norm_terms(sums, 0, count_row)
    global_mean, global_rstd = norm_terms(sums, 2, count_row)
    local_gain = vec_ref[5:6, :] * local_rstd
    global_gain = vec_ref[7:8, :] * global_rstd
    local_norm = local_ref[...] * local_gain + (vec_ref[6:7, :] - local_mean * local_gain)
    global_norm = global_ref[...] * global_gain + (vec_ref[8:9, :] - global_mean * global_gain)
    summed = low(local_norm).astype(f32) + low(global_norm).astype(f32)
    summed_low = low(summed)
    low_ref[...] = summed_low
    mixed = summed + vec_ref[11:12, :]
    for half in range(2):
        hidden = mm(summed_low, w_ref[9 + half]) + vec_ref[9 + half : 10 + half, :]
        sig_value = sig(hidden)
        hidden_low = low(hidden * sig_value)
        slope_ref[:, half * width : (half + 1) * width] = low(
            sig_value * (1.0 + hidden * (1.0 - sig_value))
        )
        hlow_ref[:, half * width : (half + 1) * width] = hidden_low
        mixed = mixed + mm(hidden_low, w_ref[11 + half])
    mixed_ref[...] = mixed
    live = live_of(info_ref, pl.program_id(0) * group, group, width)
    kept = live * mixed
    d_norm = live * cot_ref[...].astype(f32)
    add_rows(
        stat_ref, [col_sum(kept), col_sum(kept * mixed), col_sum(d_norm), col_sum(d_norm * mixed)]
    )


def hat_kernel(info_ref, local_ref, global_ref, sums_ref, lhat_ref, ghat_ref):
    sums = sums_ref[...]
    for value_ref, hat_ref, first in ((local_ref, lhat_ref, 0), (global_ref, ghat_ref, 2)):
        mean, rstd = norm_terms(sums, first, sums[4:5])
        hat_ref[...] = low((value_ref[...] - mean) * rstd)


def mix_back_kernel(
    info_ref, mixed_ref, slope_ref, cot_ref, lhat_ref, ghat_ref, sums_ref, tops_ref, w_ref,
    vec_ref,
    dmix_ref, dhid_ref, dsum_ref, stat_ref,
):
    group = mixed_ref.shape[0] // BLOCK
    width = mixed_ref.shape[1]
    sums = sums_ref[...]
    tops = tops_ref[...]
    count_row = sums[4:5]
    mean, rstd = norm_terms(tops, 0, count_row)
    live = live_of(info_ref, pl.program_id(0) * group, group, width)
    hat = (mixed_ref[...] - mean) * rstd
    d_norm = live * cot_ref[...].astype(f32)
    dz_sum = tops[2:3]
    dz_hat = (tops[3:4] - mean * dz_sum) * rstd
    d_mixed = (vec_ref[12:13, :] * rstd) * (
        d_norm - live * (dz_sum / count_row + hat * (dz_hat / count_row))
    )
    d_mixed_low = low(d_mixed)
    dmix_ref[...] = d_mixed_low
    d_summed = d_mixed
    for half in range(2):
        cols = slice(half * width, (half + 1) * width)
        d_hidden = low(mm_back(d_mixed_low, w_ref[11 + half]) * slope_ref[:, cols].astype(f32))
        dhid_ref[:, cols] = d_hidden
        d_summed = d_summed + mm_back(d_hidden, w_ref[9 + half])
    d_low = low(d_summed)
    dsum_ref[...] = d_low
    d_sum = d_low.astype(f32)
    add_rows(
        stat_ref,
        [
            col_sum(d_sum),
            col_sum(d_sum * lhat_ref[...].astype(f32)),
            col_sum(d_sum * ghat_ref[...].astype(f32)),
            col_sum(d_mixed),
        ],
    )


def accumulate(acc_ref, term):
    @pl.when(pl.program_id(0) == 0)
    def _():
        acc_ref[...] = jnp.zeros_like(acc_ref)

    acc_ref[...] += term


def layer_kernel(info_ref, mixed_ref, sums_ref, tops_ref, vec_ref, layer_ref):
    group = mixed_ref.shape[0] // BLOCK
    mean, rstd = norm_terms(tops_ref[...], 0, sums_ref[4:5, :])
    live = live_of(info_ref, pl.program_id(0) * group, group, mixed_ref.shape[1])
    hat = (mixed_ref[...] - mean) * rstd
    layer_ref[...] = low(live * (vec_ref[12:13, :] * hat + vec_ref[13:14, :]))


def ones_sum(ref, cols):
    return mm(jnp.ones((8, ref.shape[0]), bf16), ref[:, cols])


def inner_grad_kernel(info_ref, slow_ref, dhid_ref, out_ref, bias_ref):
    accumulate(out_ref, mm_rows(slow_ref[...], dhid_ref[...]))
    accumulate(bias_ref, ones_sum(dhid_ref, slice(None)))


def outer_grad_kernel(info_ref, hlow_ref, dmix_ref, out_ref):
    accumulate(out_ref, mm_rows(hlow_ref[...], dmix_ref[...]))


def norm_back(info_ref, dsum_ref, hat_ref, sums, backs, first, gain_row, hat_row):
    group = hat_ref.shape[0] // BLOCK
    count_row = sums[4:5]
    rstd = norm_terms(sums, first, count_row)[1]
    live = live_of(info_ref, pl.program_id(0) * group, group, hat_ref.shape[1])
    hat = hat_ref[...].astype(f32)
    return (gain_row * rstd) * (
        dsum_ref[...].astype(f32)
        - live * (backs[0:1] / count_row + hat * (backs[hat_row : hat_row + 1] / count_row))
    )


def local_back_steps(
    info_ref, dsum_ref, local_ref, slope_ref, recip_ref, fall_ref, open_ref, bend_ref, bsrc_ref,
    hot_ref, turned_ref, sums_ref, backs_ref, vec_ref,
    dnode_ref, dedge_ref, stat_ref,
):
    group = local_ref.shape[0] // BLOCK
    width = local_ref.shape[1]
    d_local = norm_back(
        info_ref, dsum_ref, local_ref, sums_ref[...], backs_ref[...], 0, vec_ref[5:6, :], 1
    )
    d_gated = d_local * slope_ref[...].astype(f32)
    dnode_ref[:, :width] = low(d_gated)
    d_num = low(d_gated * recip_ref[...].astype(f32))
    d_den = low(-d_gated * fall_ref[...].astype(f32))
    pre_row = jnp.zeros((1, width), f32)
    yield
    picks = [
        mm(
            hot_ref[edges_of(place), :BLOCK],
            jnp.concatenate([d_num[nodes_of(place)], d_den[nodes_of(place)]], axis=1),
        )
        for place in range(group)
    ]
    yield
    sources = []
    for place in range(group):
        edges = edges_of(place)
        d_message = picks[place][:, :width]
        d_open = d_message * bsrc_ref[edges, :].astype(f32) + picks[place][:, width:]
        sources.append(low(d_message * open_ref[edges, :].astype(f32)))
        d_pre = d_open * bend_ref[edges, :].astype(f32)
        pre_row = pre_row + col_sum(d_pre)
        dedge_ref[edges, :] = low(d_pre)
    yield
    for place in range(group):
        nodes = nodes_of(place)
        turned = turned_ref[edges_of(place), :]
        d_both = low(mm(turned, dedge_ref[edges_of(place), :]))
        dnode_ref[nodes, width : 2 * width] = low(mm(turned[BLOCK:], sources[place]))
        dnode_ref[nodes, 2 * width : 3 * width] = d_both[:BLOCK]
        dnode_ref[nodes, 3 * width :] = d_both[BLOCK:]
    add_rows(stat_ref, [col_sum(d_gated), pre_row])


def attend_back_steps(
    info_ref, dsum_ref, global_ref, q_ref, k_ref, v_ref, prob_ref, sums_ref,
    backs_ref, w_ref, vec_ref,
    dqkv_ref, dlow_ref, stat_ref, score_ref,
):
    group = global_ref.shape[0] // BLOCK
    width = global_ref.shape[1]
    score_scale = (width // HEADS) ** (-0.5)
    d_global = norm_back(
        info_ref, dsum_ref, global_ref, sums_ref[...], backs_ref[...], 2, vec_ref[7:8, :], 2
    )
    d_low = low(d_global)
    dlow_ref[...] = d_low
    d_att = low(mm_back(d_low, w_ref[8]))
    masks = head_masks(width)
    tall = tall_masks(width)
    turned_att = low(mm_back(w_ref[8], d_low))
    yield
    d_probs = [
        mm(v_ref[nodes_of(place), :], side_stack(turned_att[:, nodes_of(place)], tall))
        for place in range(group)
    ]
    yield
    for place in range(group):
        nodes = nodes_of(place)
        for head in range(HEADS):
            cols = nodes_of(head)
            prob = prob_ref[nodes, cols].astype(f32)
            part = d_probs[place][:, cols]
            inner = jnp.sum(prob * part, axis=0, keepdims=True)
            d_score = low(prob * ((part - inner) * score_scale))
            score_ref[nodes, cols] = d_score
    yield
    for place in range(group):
        nodes = nodes_of(place)
        dqkv_ref[nodes, :width] = turned_product(k_ref[nodes, :].T, score_ref, nodes, width // HEADS)
        dqkv_ref[nodes, width : 2 * width] = low(
            mm(score_ref[nodes, :], head_stack(q_ref[nodes, :], masks))
        )
        dqkv_ref[nodes, 2 * width :] = low(
            mm(prob_ref[nodes, :], head_stack(d_att[nodes], masks))
        )
    add_rows(
        stat_ref,
        [
            col_sum(d_global),
        ],
    )


def back_kernel(
    info_ref, dsum_ref, lhat_ref, slope_ref, recip_ref, fall_ref, open_ref, bend_ref, bsrc_ref,
    hot_ref, turned_ref, ghat_ref, q_ref, k_ref, v_ref, prob_ref, sums_ref, backs_ref, w_ref,
    vec_ref,
    dnode_ref, dedge_ref, lstat_ref, dqkv_ref, dlow_ref, gstat_ref, score_ref,
):
    runs = [
        attend_back_steps(
            info_ref, dsum_ref, ghat_ref, q_ref, k_ref, v_ref, prob_ref, sums_ref, backs_ref,
            w_ref, vec_ref, dqkv_ref, dlow_ref, gstat_ref, score_ref,
        ),
        local_back_steps(
            info_ref, dsum_ref, lhat_ref, slope_ref, recip_ref, fall_ref, open_ref, bend_ref,
            bsrc_ref, hot_ref, turned_ref, sums_ref, backs_ref, vec_ref, dnode_ref, dedge_ref,
            lstat_ref,
        ),
    ]
    while runs:
        runs = [run for run in runs if next(run, 1) is None]


def branch_grad_kernel(
    info_ref, x_ref, e_ref, att_ref, dnode_ref, dedge_ref, dqkv_ref, dlow_ref, igrad_ref, ograd_ref,
    *outs,
):
    outs, bias_ref, (node_ref, wide_ref, edge_ref, acc_ref) = outs[:-5], outs[-5], outs[-4:]
    width = x_ref.shape[1]
    for place in (0, 2):
        bias_ref[:, place // 2 * width : (place // 2 + 1) * width] = ones_sum(
            dqkv_ref, slice(place * width, (place + 1) * width)
        )
    x = x_ref[...]
    node_ref[...] = mm_rows(x, dnode_ref[...])
    wide_ref[...] = mm_rows(x, dqkv_ref[...])
    edge_ref[...] = mm_rows(e_ref[...], dedge_ref[...])
    acc_ref[...] = mm_rows(att_ref[...], dlow_ref[...])
    cols = [slice(place * width, (place + 1) * width) for place in range(4)]
    parts = [node_ref.at[:, cols[0]], node_ref.at[:, cols[1]], edge_ref]
    parts = parts + [node_ref.at[:, cols[2]], node_ref.at[:, cols[3]]]
    parts = parts + [wide_ref.at[:, cols[place]] for place in range(3)] + [acc_ref]
    parts = parts + [igrad_ref.at[:, cols[place]] for place in range(2)]
    parts = parts + [ograd_ref.at[cols[place], :] for place in range(2)]
    if len(outs) == 1:
        for place, part in enumerate(parts):
            outs[0][place] = low(part[...])
    else:
        pack(info_ref, parts, outs)


def reach(order, index):
    found = 0
    for place, step in enumerate(order):
        if index >> (len(order) - 1 - place) & 1:
            found ^= step >> 1
    return found


def chip_orders(total):
    chips = steps_of(total)[1:]
    return (chips, chips[1:-1] + chips[:1] + chips[-1:])


def pack(info_ref, parts, outs):
    half = outs[0].shape[0]
    slots = 2 * half
    orders = chip_orders(2 * slots)
    core = info_ref[info_ref.shape[0] - 2]
    chip = info_ref[info_ref.shape[0] - 1]
    for slot in range(slots):
        near = [reach(order, slot) for order in orders]
        for out_ref, owner in zip(outs[slot // half :: 2], (core, 1 - core)):
            step = jnp.where(owner == 0, near[0], near[1])
            row = pl.multiple_of(16 * jnp.bitwise_xor(chip, step) + 8 * owner, 8)
            for first in range(0, len(parts), 2):
                pair = [part[pl.ds(row, 8), :] for part in parts[first : first + 2]]
                out_ref[slot % half, first * 8 : first * 8 + 8 * len(pair), :] = low(
                    jnp.concatenate(pair, axis=0)
                )


def assemble_kernel(info_ref, near_ref, far_ref, near_other_ref, far_other_ref, out_ref):
    half, tall, _ = near_ref.shape
    slots = 2 * half
    orders = chip_orders(2 * slots)
    core = info_ref[info_ref.shape[0] - 2]
    chip = info_ref[info_ref.shape[0] - 1]

    def fill(even_refs, odd_refs):
        for far in range(slots):
            even, odd = [
                [slot for slot in range(slots) if reach(order, slot) == far][0] for order in orders
            ]
            row = pl.multiple_of(16 * jnp.bitwise_xor(chip, far), 16)
            for first in range(0, tall, 16):
                size = min(16, tall - first)
                part = slice(first, first + size)
                upper = even_refs[even // half][even % half, part, :].astype(f32)
                lower = odd_refs[odd // half][odd % half, part, :].astype(f32)
                for step in range(size // 8):
                    rows = slice(step * 8, step * 8 + 8)
                    out_ref[first // 8 + step, pl.ds(row, 16), :] = low(
                        jnp.concatenate([upper[rows], lower[rows]], axis=0)
                    )

    @pl.when(core == 0)
    def _():
        fill((near_ref, far_ref), (near_other_ref, far_other_ref))

    @pl.when(core != 0)
    def _():
        fill((near_other_ref, far_other_ref), (near_ref, far_ref))


def node_grad_kernel(
    info_ref, dsum_ref, lhat_ref, ghat_ref, dnode_ref, dqkv_ref, sums_ref, backs_ref, w_ref,
    vec_ref,
    node_ref,
):
    width = lhat_ref.shape[1]
    sums = sums_ref[...]
    backs = backs_ref[...]
    total = norm_back(info_ref, dsum_ref, lhat_ref, sums, backs, 0, vec_ref[5:6, :], 1)
    total = total + norm_back(info_ref, dsum_ref, ghat_ref, sums, backs, 2, vec_ref[7:8, :], 2)
    for place, mat in enumerate((0, 1, 3, 4)):
        total = total + mm_back(dnode_ref[:, place * width : (place + 1) * width], w_ref[mat])
    for place in range(3):
        total = total + mm_back(dqkv_ref[:, place * width : (place + 1) * width], w_ref[5 + place])
    node_ref[...] = total


def edge_grad_kernel(info_ref, dedge_ref, w_ref, edge_ref):
    edge_ref[...] = mm_back(dedge_ref[...], w_ref[2])


def bias_rows(local_ref, attend_ref, inner_ref, wide_ref):
    width = attend_ref.shape[1]
    return jnp.concatenate(
        [
            local_ref[0:2, :],
            wide_ref[0:1, :width],
            wide_ref[0:1, width:],
            attend_ref[0:1, :],
            inner_ref[0:1, :width],
            inner_ref[0:1, width:],
            jnp.zeros((1, width), f32),
        ],
        axis=0,
    )


def last_kernel(
    info_ref, kept_ref, got_ref, local_ref, attend_ref, inner_ref, wide_ref, out_ref
):
    biases = bias_rows(local_ref, attend_ref, inner_ref, wide_ref)
    upper = low(biases).astype(f32)
    for slot, extra in enumerate((upper, biases - upper)):
        total = kept_ref[slot].astype(f32) + got_ref[slot].astype(f32)
        out_ref[slot] = low(jnp.concatenate([total, extra], axis=0))


def total_square(values):
    return jnp.sum(jnp.sum(values * values, axis=0, keepdims=True), axis=1, keepdims=True)


def pair_kernel(info_ref, mine_ref, got_ref, grad_ref, tail_ref):
    rows = grad_ref.shape[1]
    half = grad_ref.shape[2]
    mine = [mine_ref[slot].astype(f32) for slot in range(2)]
    got = [got_ref[slot].astype(f32) for slot in range(2)]
    grad = mine[0][:rows] + got[1][:rows]
    other = mine[1][:rows] + got[0][:rows]
    grad_ref[0] = grad[:, :half]
    grad_ref[1] = grad[:, half:]
    tail_ref[...] = (mine[0][rows:] + mine[1][rows:]) + (got[0][rows:] + got[1][rows:])
    tail_ref[7:8, :] = jnp.broadcast_to(total_square(grad) + total_square(other), (1, 2 * half))


def square_kernel(
    info_ref, kept_ref, got_ref, local_ref, attend_ref, inner_ref, wide_ref, grad_ref, tail_ref
):
    grad = kept_ref[...].astype(f32) + got_ref[...].astype(f32)
    half = grad.shape[1] // 2
    grad_ref[0] = grad[:, :half]
    grad_ref[1] = grad[:, half:]
    tail_ref[...] = bias_rows(local_ref, attend_ref, inner_ref, wide_ref)
    tail_ref[7:8, :] = jnp.broadcast_to(total_square(grad), (1, tail_ref.shape[1]))


def update_kernel(
    info_ref, grad_ref, tail_ref, sums_ref, tops_ref, backs_ref, w_ref, w1_ref, w2_ref, v_ref,
    v1_ref, v2_ref,
    new_w_ref, new_w1_ref, new_w2_ref, new_v_ref, new_v1_ref, new_v2_ref, norm_ref,
):
    tail = tail_ref[...]
    tops = tops_ref[...]
    backs = backs_ref[...]
    mean, rstd = norm_terms(tops, 0, sums_ref[4:5, :])
    grad_v = jnp.concatenate(
        [
            tail[0:5],
            backs[1:2],
            backs[0:1],
            backs[2:3],
            backs[0:1],
            tail[5:7],
            backs[3:4],
            (tops[3:4] - mean * tops[2:3]) * rstd,
            tops[2:3],
        ],
        axis=0,
    )
    square = jnp.sum(jnp.sum(grad_v * grad_v, axis=0, keepdims=True), axis=1, keepdims=True)
    norm = jnp.sqrt(tail[7:8, 0:1] + square)
    norm_ref[...] = norm
    factor = jnp.minimum(1.0, clip_limit / (norm + 1e-06))
    new_v_ref[...], new_v1_ref[...], new_v2_ref[...] = adamw(
        v_ref[...], factor * grad_v, v1_ref[...], v2_ref[...], rate_vecs, 0.0
    )
    mats, span = w_ref.shape
    _, rows, half = grad_ref.shape
    for piece in range(span // half):
        cols = slice(piece * half, (piece + 1) * half)
        if rows == mats:
            grad = grad_ref[piece]
        else:
            grad = grad_ref[piece % 2, pl.ds(piece // 2, mats, rows // mats), :]
        new_w_ref[:, cols], new_w1_ref[:, cols], new_w2_ref[:, cols] = adamw(
            w_ref[:, cols], factor * grad, w1_ref[:, cols], w2_ref[:, cols], rate_mats, decay_mats
        )


def rows_spec(rows, width, offset=0):
    if offset:
        return pl.BlockSpec((rows, width), lambda step, info: (step + info[0], 0))
    return pl.BlockSpec((rows, width), lambda step, info: (step, 0))


def whole_spec(shape):
    zeros = (0,) * len(shape)
    return pl.BlockSpec(shape, lambda step, info: zeros)


def call(kernel, steps, info, inputs, outputs, scratch=(), room=10, cost=5):
    in_specs = []
    arrays = []
    for array, spec in inputs:
        arrays.append(array)
        in_specs.append(whole_spec(array.shape) if spec is None else spec)
    out_specs = []
    out_shapes = []
    for shape, dtype, spec, *far in outputs:
        out_specs.append(whole_spec(shape) if spec is None else spec)
        out_shapes.append(pltpu.HBM(shape, dtype) if far else jax.ShapeDtypeStruct(shape, dtype))
    return pl.pallas_call(
        kernel,
        grid_spec=pltpu.PrefetchScalarGridSpec(
            num_scalar_prefetch=1,
            grid=(steps,),
            in_specs=in_specs,
            out_specs=out_specs,
            scratch_shapes=list(scratch),
        ),
        out_shape=out_shapes,
        compiler_params=pltpu.CompilerParams(
            dimension_semantics=("arbitrary",), vmem_limit_bytes=room * 1024 * 1024
        ),
        name=kernel.__name__,
        cost_estimate=pl.CostEstimate(
            flops=cost * 1000000000, bytes_accessed=cost * 1000000, transcendentals=0
        ),
    )(info, *arrays)


def swap_with(values, step, total):
    return lax.ppermute(values, axis_names, [(place, place ^ step) for place in range(total)])


def steps_of(total):
    return [1 << power for power in range(total.bit_length() - 1)]


def beside(start, transfer, info, work):
    info = lax.optimization_barrier((info, start))[0]
    return lax.optimization_barrier((transfer, work(info)))


def sum_steps(total):
    return [step | 1 for step in steps_of(total)]


def sum_small(values, total, info=None, works=()):
    results = []
    works = list(works)
    for step in sum_steps(total):
        other = swap_with(values, step, total)
        if works and step > 1:
            other, done = beside(values, other, info, works.pop(0))
            results.append(done)
        values = values + other
    return (values, results) if results else values


def swap_chips(values, number, total):
    orders = chip_orders(total)
    return lax.ppermute(
        values,
        axis_names,
        [(place, place ^ orders[place % 2][number]) for place in range(total)],
    )


def in_rows(total, width):
    return width * width // total == 8 * width


def gather_matrices(shard, info, total, width, work):
    mats = shard.shape[0]
    if not in_rows(total, width):
        gathered = lax.all_gather(shard, axis_names, axis=1, tiled=True)
        return (gathered.reshape(mats, width, width), work(info))
    held = shard.reshape(1, mats * 8, width)
    for number in reversed(range(1, len(chip_orders(total)[0]))):
        held = jnp.concatenate([held, swap_chips(held, number, total)], axis=0)
    got = swap_chips(held, 0, total)
    other = swap_with(held, 1, total)

    def both(info):
        return (work(info), other)

    got, (done, other) = beside(held, got, info, both)
    far_other = swap_with(got, 1, total)
    matrices = call(
        assemble_kernel,
        1,
        info,
        [(held, None), (got, None), (other, None), (far_other, None)],
        [((mats, width, width), bf16, None)],
    )[0]
    return (matrices, done)


def scatter_plain(grads, total):
    place = lax.axis_index(axis_names)
    mats, width, _ = grads.shape
    bits = total.bit_length() - 1
    held = grads.reshape((mats,) + (2,) * bits + (width * width // total,))
    held = held.transpose(tuple(reversed(range(1, bits + 1))) + (0, bits + 1))
    for step in steps_of(total):
        mine = ((place & step) != 0).astype(jnp.int32)
        sent = lax.dynamic_index_in_dim(held, 1 - mine, 0, keepdims=False)
        kept = lax.dynamic_index_in_dim(held, mine, 0, keepdims=False)
        got = swap_with(sent, step, total)
        if step * 2 < total:
            held = low(kept.astype(f32) + got.astype(f32))
    return (kept, got)


def scatter_packed(kept, far_kept, sent, far_sent, total, info, works, biases):
    far_got = swap_with(far_sent, 1, total)
    got = swap_with(sent, 1, total)
    results = []
    rounds = len(chip_orders(total)[0])
    for number in range(rounds - 1):
        if number:
            half = kept.shape[0] // 2
            far_kept, far_got = kept[half:], got[half:]
            kept, got = kept[:half], got[:half]
        sent = low(far_kept.astype(f32) + far_got.astype(f32))
        kept = kept.astype(f32) + got.astype(f32)
        got = swap_chips(sent, number, total)
        if number < len(works):
            got, done = beside(sent, got, info, works[number])
            results.append(done)
    mine = call(
        last_kernel,
        1,
        info,
        [(array, None) for array in (kept, got, *biases)],
        [((2, kept.shape[1] + 8, kept.shape[2]), bf16, None)],
    )[0]
    got = swap_chips(mine, rounds - 1, total)
    grad_rows, tail = call(
        pair_kernel,
        1,
        info,
        [(mine, None), (got, None)],
        [((2, kept.shape[1], kept.shape[2] // 2), f32, None), ((8, kept.shape[2]), f32, None)],
    )
    for step in sum_steps(total)[:-1]:
        tail = tail + swap_with(tail, step, total)
    return (grad_rows, tail, results)


def adamw(params, gradient, moment_one, moment_two, rate, decay):
    first = beta_one * moment_one + (1.0 - beta_one) * gradient
    second = beta_two * moment_two + (1.0 - beta_two) * gradient * gradient
    first_hat = first / (1.0 - beta_one**STEP)
    second_hat = second / (1.0 - beta_two**STEP)
    updated = params - rate * (first_hat / (jnp.sqrt(second_hat) + adam_eps) + decay * params)
    return (updated, first, second)


def own_half(values, branch_index):
    half = values.shape[0] // 2
    return lax.dynamic_slice_in_dim(values, branch_index * half, half, 0)


def per_device(
    node_feats,
    edge_feats,
    cotangent,
    graph_ids,
    node_mask,
    edge_src,
    edge_dst,
    edge_mask,
    weights,
    weight_moment1,
    weight_moment2,
    vectors,
    vector_moment1,
    vector_moment2,
):
    total = lax.axis_size("rows") * lax.axis_size("branch")
    branch_index = lax.axis_index("branch")
    width = node_feats.shape[1]
    rows = node_feats.shape[0] // 2
    edges = edge_feats.shape[0] // 2
    blocks = rows // BLOCK
    group = math.gcd(blocks, GROUP)
    steps = blocks // group
    tall = group * BLOCK
    tall_edges = group * EB
    w_bf = low(weights)
    own_nodes = own_half(node_feats, branch_index)
    own_edges = own_half(edge_feats, branch_index)
    counts = jnp.sum(own_half(node_mask, branch_index).reshape(blocks, BLOCK), axis=1)
    info = jnp.concatenate(
        [(branch_index * steps)[None], counts, branch_index[None], lax.axis_index("rows")[None]]
    ).astype(jnp.int32)

    def by_step(values, slots):
        return own_half(values, branch_index).reshape(steps, group, slots)

    def step_spec(slots):
        return pl.BlockSpec((1, group, slots), lambda step, info: (step, 0, 0))

    edge_spec = rows_spec(tall_edges, width)
    node_spec = rows_spec(tall, width)
    def prep_work(info):
        return call(
            prep_kernel,
            steps,
            info,
            [
                (by_step(edge_src, EB), step_spec(EB)),
                (by_step(edge_dst, EB), step_spec(EB)),
                (by_step(edge_mask, EB), step_spec(EB)),
                (by_step(graph_ids, BLOCK), step_spec(BLOCK)),
            ],
            [
                ((edges, EB), bf16, edge_spec, True),
                ((edges, EB), bf16, edge_spec, True),
                ((rows, BLOCK), f32, rows_spec(tall, BLOCK)),
            ],
        )

    matrices, (hot, turned, bias) = gather_matrices(w_bf, info, total, width, prep_work)
    x_in = (own_nodes, node_spec)
    e_in = (own_edges, edge_spec)
    mats_in = (matrices, None)
    vec_in = (vectors, None)
    node_f32 = ((rows, width), f32, node_spec)
    node_bf = ((rows, width), bf16, node_spec)
    sums_out = ((8, width), f32, None)
    prob_spec = rows_spec(tall, HEADS * BLOCK)
    (
        local_out, gate_slope, recip, fall, opened, bend, b_source,
        global_out, queries, keyed, valued, attended, probs, sums_part,
    ) = call(
        forward_kernel,
        steps,
        info,
        [
            x_in,
            e_in,
            (bias, rows_spec(tall, BLOCK)),
            (hot, edge_spec),
            (turned, edge_spec),
            mats_in,
            vec_in,
        ],
        [
            node_f32,
            node_bf,
            node_bf,
            node_bf,
            ((edges, width), bf16, edge_spec),
            ((edges, width), bf16, edge_spec),
            ((edges, width), bf16, edge_spec),
            node_f32,
            node_bf,
            node_bf,
            node_bf,
            node_bf,
            ((rows, HEADS * BLOCK), bf16, prob_spec),
            sums_out,
        ],
        room=FRONT_ROOM,
    )
    sums = sum_small(sums_part, total)
    sums_in = (sums, None)
    cot_in = (cotangent, node_spec)
    wide_spec = rows_spec(tall, 2 * width)
    summed_low, hidden_low, hidden_slope, mixed, top_part = call(
        mix_kernel,
        steps,
        info,
        [(local_out, node_spec), (global_out, node_spec), cot_in, sums_in, mats_in, vec_in],
        [
            node_bf,
            ((rows, 2 * width), bf16, wide_spec),
            ((rows, 2 * width), bf16, wide_spec),
            node_f32,
            sums_out,
        ],
    )

    def hat_work(info):
        return call(
            hat_kernel,
            steps,
            info,
            [(local_out, node_spec), (global_out, node_spec), sums_in],
            [node_bf, node_bf],
        )

    tops, ((local_hat, global_hat),) = sum_small(top_part, total, info, [hat_work])
    d_mixed, d_hidden, d_summed, back_part = call(
        mix_back_kernel,
        steps,
        info,
        [
            (mixed, node_spec),
            (hidden_slope, wide_spec),
            cot_in,
            (local_hat, node_spec),
            (global_hat, node_spec),
            sums_in,
            (tops, None),
            mats_in,
            vec_in,
        ],
        [
            node_bf,
            ((rows, 2 * width), bf16, wide_spec),
            node_bf,
            sums_out,
        ],
    )

    def mat_out(tall_by, wide_by):
        return ((tall_by * width, wide_by * width), f32, None)

    def inner_work(info):
        return call(
            inner_grad_kernel,
            steps,
            info,
            [(summed_low, node_spec), (d_hidden, wide_spec)],
            [mat_out(1, 2), ((8, 2 * width), f32, None)],
        )

    def outer_work(info):
        return call(
            outer_grad_kernel,
            steps,
            info,
            [(hidden_low, wide_spec), (d_mixed, node_spec)],
            [mat_out(2, 1)],
        )[0]

    def layer_work(info):
        return call(
            layer_kernel,
            steps,
            info,
            [(mixed, node_spec), sums_in, (tops, None), vec_in],
            [node_bf],
        )[0]

    backs, ((inner_grads, inner_bias), outer_grads, layer_out) = sum_small(
        back_part, total, info, [inner_work, outer_work, layer_work]
    )
    backs_in = (backs, None)
    dsum_in = (d_summed, node_spec)
    dnode_spec = rows_spec(tall, 4 * width)
    dqkv_spec = rows_spec(tall, 3 * width)
    slots = total // 2
    packed = in_rows(total, width)
    grad_outs = [((MATS, width, width), bf16, None)]
    if packed:
        grad_outs = [((slots // 2, MATS * 8, width), bf16, None)] * 4
    d_node, d_edge, local_bias, d_qkv, d_low, attend_bias = call(
        back_kernel,
        steps,
        info,
        [
            dsum_in,
            (local_hat, node_spec),
            (gate_slope, node_spec),
            (recip, node_spec),
            (fall, node_spec),
            (opened, edge_spec),
            (bend, edge_spec),
            (b_source, edge_spec),
            (hot, edge_spec),
            (turned, edge_spec),
            (global_hat, node_spec),
            (queries, node_spec),
            (keyed, node_spec),
            (valued, node_spec),
            (probs, prob_spec),
            sums_in,
            backs_in,
            mats_in,
            vec_in,
        ],
        [
            ((rows, 4 * width), bf16, dnode_spec),
            ((edges, width), bf16, edge_spec),
            sums_out,
            ((rows, 3 * width), bf16, dqkv_spec),
            node_bf,
            sums_out,
        ],
        [pltpu.VMEM((tall, HEADS * BLOCK), bf16)],
        room=BACK_ROOM,
    )
    *grads, wide_bias = call(
        branch_grad_kernel,
        1,
        info,
        [
            (own_nodes, None),
            (own_edges, None),
            (attended, None),
            (d_node, None),
            (d_edge, None),
            (d_qkv, None),
            (d_low, None),
            (inner_grads, None),
            (outer_grads, None),
        ],
        grad_outs + [((8, 2 * width), f32, None)],
        [
            pltpu.VMEM((width, 4 * width), f32),
            pltpu.VMEM((width, 3 * width), f32),
            pltpu.VMEM((width, width), f32),
            pltpu.VMEM((width, width), f32),
        ],
    )

    def node_work(info):
        return call(
            node_grad_kernel,
            steps,
            info,
            [
                dsum_in,
                (local_hat, node_spec),
                (global_hat, node_spec),
                (d_node, dnode_spec),
                (d_qkv, dqkv_spec),
                sums_in,
                backs_in,
                mats_in,
                vec_in,
            ],
            [node_f32],
        )[0]

    def edge_work(info):
        return call(
            edge_grad_kernel,
            steps,
            info,
            [(d_edge, edge_spec), mats_in],
            [((edges, width), f32, edge_spec)],
        )[0]

    biases = (local_bias, attend_bias, inner_bias, wide_bias)
    if packed:
        grad_rows, tail, (node_grad, edge_grad) = scatter_packed(
            *grads, total, info, [node_work, edge_work], biases
        )
    else:
        grad_shard = scatter_plain(grads[0], total)
        node_grad, edge_grad = node_work(info), edge_work(info)
        grad_rows, tail_part = call(
            square_kernel,
            1,
            info,
            [(array, None) for array in (*grad_shard, *biases)],
            [
                ((2, grad_shard[0].shape[0], grad_shard[0].shape[1] // 2), f32, None),
                sums_out,
            ],
        )
        tail = sum_small(tail_part, total)
    like_mats = (weights.shape, f32, None)
    like_vecs = (vectors.shape, f32, None)
    new_weights, first_w, second_w, new_vectors, first_v, second_v, norm = call(
        update_kernel,
        1,
        info,
        [
            (array, None)
            for array in (
                grad_rows, tail, sums, tops, backs, weights, weight_moment1, weight_moment2,
                vectors, vector_moment1, vector_moment2,
            )
        ],
        [like_mats] * 3 + [like_vecs] * 3 + [((1, 1), f32, None)],
    )
    grad_norm = norm.reshape(())
    return (
        layer_out,
        node_grad,
        edge_grad,
        new_weights,
        first_w,
        second_w,
        new_vectors,
        first_v,
        second_v,
        grad_norm,
    )


def solution(mesh):
    in_specs = (
        P("rows", None),
        P("rows", None),
        P(("rows", "branch"), None),
        P("rows"),
        P("rows"),
        P("rows"),
        P("rows"),
        P("rows"),
        P(None, ("rows", "branch")),
        P(None, ("rows", "branch")),
        P(None, ("rows", "branch")),
        P(),
        P(),
        P(),
    )
    out_specs = (
        P(("rows", "branch"), None),
        P(("rows", "branch"), None),
        P(("rows", "branch"), None),
        P(None, ("rows", "branch")),
        P(None, ("rows", "branch")),
        P(None, ("rows", "branch")),
        P(),
        P(),
        P(),
        P(),
    )
    return jax.shard_map(
        per_device, mesh=mesh, in_specs=in_specs, out_specs=out_specs, check_vma=False
    )
```

```python
import functools
import math

import jax
import jax.numpy as jnp
from jax import lax
from jax.experimental import pallas as pl
from jax.experimental.pallas import tpu as pltpu
from jax.sharding import PartitionSpec as P

HEADS = 8
BLOCK = 128
EB = 256
MATS = 13
STEP = 7
GROUP = 8
BACK_ROOM = 12
FRONT_ROOM = 12

eps_norm = 1e-05
clip_limit = 1.0
beta_one = 0.9
beta_two = 0.999
rate_mats = 0.1
rate_vecs = 0.8
decay_mats = 0.01
adam_eps = 1e-08
hidden_floor = -1e30
axis_names = ("rows", "branch")
f32 = jnp.float32
bf16 = jnp.bfloat16


def mm(left, right):
    return jnp.dot(left, right, preferred_element_type=f32)


def mm_back(left, right):
    return lax.dot_general(left, right, (((1,), (1,)), ((), ())), preferred_element_type=f32)


def mm_rows(left, right):
    return lax.dot_general(left, right, (((0,), (0,)), ((), ())), preferred_element_type=f32)


def low(values):
    return values.astype(bf16)


def sig(values):
    return 0.5 * jnp.tanh(0.5 * values) + 0.5


def col_sum(values):
    return jnp.sum(values, axis=0, keepdims=True)


def live_of(info_ref, first_block, group, width):
    slot = lax.broadcasted_iota(jnp.int32, (BLOCK, width), 0)
    return jnp.concatenate(
        [
            jnp.where(slot < info_ref[1 + first_block + place], 1.0, 0.0)
            for place in range(group)
        ],
        axis=0,
    )


def nodes_of(place):
    return slice(place * BLOCK, (place + 1) * BLOCK)


def edges_of(place):
    return slice(place * EB, (place + 1) * EB)


def add_rows(out_ref, rows):
    @pl.when(pl.program_id(0) == 0)
    def _():
        out_ref[...] = jnp.zeros_like(out_ref)

    for place, row in enumerate(rows):
        out_ref[place : place + 1, :] += row


def norm_terms(sums, first, count_row):
    mean = sums[first : first + 1] / count_row
    rstd = lax.rsqrt(sums[first + 1 : first + 2] / count_row - mean * mean + eps_norm)
    return (mean, rstd)


def prep_kernel(info_ref, src_ref, dst_ref, mask_ref, id_ref, hot_ref, turned_ref, bias_ref):
    for place in range(GROUP):
        row = pl.ds(place, 1)
        node = lax.broadcasted_iota(jnp.int32, (BLOCK, EB), 0)
        live = mask_ref[0, row, :] != 0
        dst_rows = jnp.where((node == dst_ref[0, row, :]) & live, 1.0, 0.0)
        src_rows = jnp.where((node == src_ref[0, row, :]) & live, 1.0, 0.0)
        turned = jnp.concatenate([dst_rows, src_rows], axis=0)
        turned_ref[place * EB : (place + 1) * EB, :] = low(turned)
        hot_ref[place * EB : (place + 1) * EB, :] = low(turned.T)
        ids = jnp.broadcast_to(id_ref[0, row, :].astype(f32), (BLOCK, BLOCK))
        bias_ref[place * BLOCK : (place + 1) * BLOCK, :] = jnp.where(
            ids == ids.T, 0.0, hidden_floor
        )


def local_steps(
    info_ref, x_ref, e_ref, hot_ref, turned_ref, w_ref, vec_ref,
    out_ref, slope_ref, recip_ref, fall_ref, open_ref, bend_ref, bsrc_ref, stats,
):
    group = x_ref.shape[0] // BLOCK
    x = x_ref[...]
    a_part = mm(x, w_ref[0]) + vec_ref[0:1, :]
    b_part = low(mm(x, w_ref[1]))
    d_part = low(mm(x, w_ref[3]))
    e_part = low(mm(x, w_ref[4]))
    c_part = mm(e_ref[...], w_ref[2]) + vec_ref[1:2, :]
    gates = []
    picks = []
    for place in range(group):
        nodes = nodes_of(place)
        hot = hot_ref[edges_of(place), :]
        gates.append(mm(hot, jnp.concatenate([d_part[nodes], e_part[nodes]], axis=0)))
        picks.append(mm(hot[:, BLOCK:], b_part[nodes]))
    yield
    sums = []
    for place in range(group):
        edges = edges_of(place)
        opened = sig(c_part[edges] + gates[place])
        b_source = picks[place]
        opened_low = low(opened)
        open_ref[edges, :] = opened_low
        bend_ref[edges, :] = low(opened * (1.0 - opened))
        bsrc_ref[edges, :] = low(b_source)
        dst_turned = turned_ref[place * EB : place * EB + BLOCK, :]
        sums.append(
            mm(dst_turned, jnp.concatenate([low(opened * b_source), opened_low], axis=1))
        )
    yield
    both = jnp.concatenate(sums, axis=0)
    width = x.shape[1]
    recip = 1.0 / (both[:, width:] + 1.0)
    ratio = both[:, :width] * recip
    gated = a_part + ratio
    gated_sig = sig(gated)
    out = x.astype(f32) + gated * gated_sig
    slope_ref[...] = low(gated_sig * (1.0 + gated * (1.0 - gated_sig)))
    recip_ref[...] = low(recip)
    fall_ref[...] = low(ratio * recip)
    out_ref[...] = out
    live = live_of(info_ref, pl.program_id(0) * group, group, out.shape[1])
    kept = live * out
    stats[0:2] = [col_sum(kept), col_sum(kept * out)]


def head_masks(width):
    head = lax.broadcasted_iota(jnp.int32, (16, width), 1) // (width // HEADS)
    return [low(jnp.where(head == place, 1.0, 0.0))[:1] for place in range(HEADS)]


def head_stack(values, masks):
    return jnp.concatenate([values * mask for mask in masks], axis=0)


def tall_masks(width):
    head = lax.broadcasted_iota(jnp.int32, (width, BLOCK), 0) // (width // HEADS)
    return [low(jnp.where(head == place, 1.0, 0.0)) for place in range(HEADS)]


def side_stack(turned, masks):
    return jnp.concatenate([turned * mask for mask in masks], axis=1)


def turned_product(turned, weight, nodes, size):
    parts = []
    for head in range(0, HEADS, 2):
        both = mm(
            turned[head * size : (head + 2) * size],
            weight[nodes, head * BLOCK : (head + 2) * BLOCK],
        )
        parts += [both[:size, :BLOCK], both[size:, BLOCK:]]
    return low(jnp.concatenate(parts, axis=0)).T


def attend_steps(
    info_ref, x_ref, bias_ref, w_ref, vec_ref,
    out_ref, q_ref, k_ref, v_ref, att_ref, prob_ref, stats,
):
    group = x_ref.shape[0] // BLOCK
    x = x_ref[...]
    queries = low(mm(x, w_ref[5]) + vec_ref[2:3, :])
    keyed = low(mm(x, w_ref[6]))
    valued = low(mm(x, w_ref[7]) + vec_ref[3:4, :])
    q_ref[...] = queries
    k_ref[...] = keyed
    v_ref[...] = valued
    score_scale = (x.shape[1] // HEADS) ** (-0.5) * math.log2(math.e)
    tall = tall_masks(x.shape[1])
    queries_turned = queries.T
    valued_turned = valued.T
    size = x.shape[1] // HEADS
    raws = [
        mm(keyed[nodes_of(place)], side_stack(queries_turned[:, nodes_of(place)], tall))
        for place in range(group)
    ]
    yield
    for place in range(group):
        nodes = nodes_of(place)
        bias = bias_ref[nodes, :]
        for head in range(HEADS):
            cols = nodes_of(head)
            part = raws[place][:, cols] + bias
            part = jnp.exp2((part - jnp.max(part, axis=0, keepdims=True)) * score_scale)
            prob_ref[nodes, cols] = low(part * (1.0 / jnp.sum(part, axis=0, keepdims=True)))
    yield
    for place in range(group):
        nodes = nodes_of(place)
        att_ref[nodes, :] = turned_product(valued_turned[:, nodes], prob_ref, nodes, size)
    out = x.astype(f32) + mm(att_ref[...], w_ref[8]) + vec_ref[4:5, :]
    out_ref[...] = out
    live = live_of(info_ref, pl.program_id(0) * group, group, out.shape[1])
    kept = live * out
    stats[2:4] = [col_sum(kept), col_sum(kept * out)]


def forward_kernel(
    info_ref, x_ref, e_ref, bias_ref, hot_ref, turned_ref, w_ref, vec_ref,
    lout_ref, slope_ref, recip_ref, fall_ref, open_ref, bend_ref, bsrc_ref,
    gout_ref, q_ref, k_ref, v_ref, att_ref, prob_ref, sums_ref,
):
    stats = [None] * 4
    runs = [
        attend_steps(
            info_ref, x_ref, bias_ref, w_ref, vec_ref, gout_ref, q_ref, k_ref, v_ref, att_ref,
            prob_ref, stats,
        ),
        local_steps(
            info_ref, x_ref, e_ref, hot_ref, turned_ref, w_ref, vec_ref, lout_ref, slope_ref,
            recip_ref, fall_ref, open_ref, bend_ref, bsrc_ref, stats,
        ),
    ]
    while runs:
        runs = [run for run in runs if next(run, 1) is None]
    add_rows(sums_ref, stats)

    @pl.when(pl.program_id(0) == 0)
    def _():
        count = info_ref[1]
        for place in range(2, info_ref.shape[0] - 2):
            count = count + info_ref[place]
        sums_ref[4:5, :] = jnp.full((1, x_ref.shape[1]), count, jnp.int32).astype(f32)


def mix_kernel(
    info_ref, local_ref, global_ref, cot_ref, sums_ref, w_ref, vec_ref,
    low_ref, hlow_ref, slope_ref, mixed_ref, stat_ref,
):
    group = local_ref.shape[0] // BLOCK
    width = local_ref.shape[1]
    sums = sums_ref[...]
    count_row = sums[4:5]
    local_mean, local_rstd = norm_terms(sums, 0, count_row)
    global_mean, global_rstd = norm_terms(sums, 2, count_row)
    local_gain = vec_ref[5:6, :] * local_rstd
    global_gain = vec_ref[7:8, :] * global_rstd
    local_norm = local_ref[...] * local_gain + (vec_ref[6:7, :] - local_mean * local_gain)
    global_norm = global_ref[...] * global_gain + (vec_ref[8:9, :] - global_mean * global_gain)
    summed = low(local_norm).astype(f32) + low(global_norm).astype(f32)
    summed_low = low(summed)
    low_ref[...] = summed_low
    mixed = summed + vec_ref[11:12, :]
    for half in range(2):
        hidden = mm(summed_low, w_ref[9 + half]) + vec_ref[9 + half : 10 + half, :]
        sig_value = sig(hidden)
        hidden_low = low(hidden * sig_value)
        slope_ref[:, half * width : (half + 1) * width] = low(
            sig_value * (1.0 + hidden * (1.0 - sig_value))
        )
        hlow_ref[:, half * width : (half + 1) * width] = hidden_low
        mixed = mixed + mm(hidden_low, w_ref[11 + half])
    mixed_ref[...] = mixed
    live = live_of(info_ref, pl.program_id(0) * group, group, width)
    kept = live * mixed
    d_norm = live * cot_ref[...].astype(f32)
    add_rows(
        stat_ref, [col_sum(kept), col_sum(kept * mixed), col_sum(d_norm), col_sum(d_norm * mixed)]
    )


def hat_kernel(info_ref, local_ref, global_ref, sums_ref, lhat_ref, ghat_ref):
    sums = sums_ref[...]
    for value_ref, hat_ref, first in ((local_ref, lhat_ref, 0), (global_ref, ghat_ref, 2)):
        mean, rstd = norm_terms(sums, first, sums[4:5])
        hat_ref[...] = low((value_ref[...] - mean) * rstd)


def mix_back_kernel(
    info_ref, mixed_ref, slope_ref, cot_ref, lhat_ref, ghat_ref, sums_ref, tops_ref, w_ref,
    vec_ref,
    dmix_ref, dhid_ref, dsum_ref, stat_ref,
):
    group = mixed_ref.shape[0] // BLOCK
    width = mixed_ref.shape[1]
    sums = sums_ref[...]
    tops = tops_ref[...]
    count_row = sums[4:5]
    mean, rstd = norm_terms(tops, 0, count_row)
    live = live_of(info_ref, pl.program_id(0) * group, group, width)
    hat = (mixed_ref[...] - mean) * rstd
    d_norm = live * cot_ref[...].astype(f32)
    dz_sum = tops[2:3]
    dz_hat = (tops[3:4] - mean * dz_sum) * rstd
    d_mixed = (vec_ref[12:13, :] * rstd) * (
        d_norm - live * (dz_sum / count_row + hat * (dz_hat / count_row))
    )
    d_mixed_low = low(d_mixed)
    dmix_ref[...] = d_mixed_low
    d_summed = d_mixed
    for half in range(2):
        cols = slice(half * width, (half + 1) * width)
        d_hidden = low(mm_back(d_mixed_low, w_ref[11 + half]) * slope_ref[:, cols].astype(f32))
        dhid_ref[:, cols] = d_hidden
        d_summed = d_summed + mm_back(d_hidden, w_ref[9 + half])
    d_low = low(d_summed)
    dsum_ref[...] = d_low
    d_sum = d_low.astype(f32)
    add_rows(
        stat_ref,
        [
            col_sum(d_sum),
            col_sum(d_sum * lhat_ref[...].astype(f32)),
            col_sum(d_sum * ghat_ref[...].astype(f32)),
            col_sum(d_mixed),
        ],
    )


def accumulate(acc_ref, term):
    @pl.when(pl.program_id(0) == 0)
    def _():
        acc_ref[...] = jnp.zeros_like(acc_ref)

    acc_ref[...] += term


def layer_kernel(info_ref, mixed_ref, sums_ref, tops_ref, vec_ref, layer_ref):
    group = mixed_ref.shape[0] // BLOCK
    mean, rstd = norm_terms(tops_ref[...], 0, sums_ref[4:5, :])
    live = live_of(info_ref, pl.program_id(0) * group, group, mixed_ref.shape[1])
    hat = (mixed_ref[...] - mean) * rstd
    layer_ref[...] = low(live * (vec_ref[12:13, :] * hat + vec_ref[13:14, :]))


def ones_sum(ref, cols):
    return mm(jnp.ones((8, ref.shape[0]), bf16), ref[:, cols])


def inner_grad_kernel(info_ref, slow_ref, dhid_ref, out_ref, bias_ref):
    accumulate(out_ref, mm_rows(slow_ref[...], dhid_ref[...]))
    accumulate(bias_ref, ones_sum(dhid_ref, slice(None)))


def outer_grad_kernel(info_ref, hlow_ref, dmix_ref, out_ref):
    accumulate(out_ref, mm_rows(hlow_ref[...], dmix_ref[...]))


def norm_back(info_ref, dsum_ref, hat_ref, sums, backs, first, gain_row, hat_row):
    group = hat_ref.shape[0] // BLOCK
    count_row = sums[4:5]
    rstd = norm_terms(sums, first, count_row)[1]
    live = live_of(info_ref, pl.program_id(0) * group, group, hat_ref.shape[1])
    hat = hat_ref[...].astype(f32)
    return (gain_row * rstd) * (
        dsum_ref[...].astype(f32)
        - live * (backs[0:1] / count_row + hat * (backs[hat_row : hat_row + 1] / count_row))
    )


def local_back_steps(
    info_ref, dsum_ref, local_ref, slope_ref, recip_ref, fall_ref, open_ref, bend_ref, bsrc_ref,
    hot_ref, turned_ref, sums_ref, backs_ref, vec_ref,
    dnode_ref, dedge_ref, stat_ref,
):
    group = local_ref.shape[0] // BLOCK
    width = local_ref.shape[1]
    d_local = norm_back(
        info_ref, dsum_ref, local_ref, sums_ref[...], backs_ref[...], 0, vec_ref[5:6, :], 1
    )
    d_gated = d_local * slope_ref[...].astype(f32)
    dnode_ref[:, :width] = low(d_gated)
    d_num = low(d_gated * recip_ref[...].astype(f32))
    d_den = low(-d_gated * fall_ref[...].astype(f32))
    pre_row = jnp.zeros((1, width), f32)
    yield
    picks = [
        mm(
            hot_ref[edges_of(place), :BLOCK],
            jnp.concatenate([d_num[nodes_of(place)], d_den[nodes_of(place)]], axis=1),
        )
        for place in range(group)
    ]
    yield
    sources = []
    for place in range(group):
        edges = edges_of(place)
        d_message = picks[place][:, :width]
        d_open = d_message * bsrc_ref[edges, :].astype(f32) + picks[place][:, width:]
        sources.append(low(d_message * open_ref[edges, :].astype(f32)))
        d_pre = d_open * bend_ref[edges, :].astype(f32)
        pre_row = pre_row + col_sum(d_pre)
        dedge_ref[edges, :] = low(d_pre)
    yield
    for place in range(group):
        nodes = nodes_of(place)
        turned = turned_ref[edges_of(place), :]
        d_both = low(mm(turned, dedge_ref[edges_of(place), :]))
        dnode_ref[nodes, width : 2 * width] = low(mm(turned[BLOCK:], sources[place]))
        dnode_ref[nodes, 2 * width : 3 * width] = d_both[:BLOCK]
        dnode_ref[nodes, 3 * width :] = d_both[BLOCK:]
    add_rows(stat_ref, [col_sum(d_gated), pre_row])


def attend_back_steps(
    info_ref, dsum_ref, global_ref, q_ref, k_ref, v_ref, prob_ref, sums_ref,
    backs_ref, w_ref, vec_ref,
    dqkv_ref, dlow_ref, stat_ref, score_ref,
):
    group = global_ref.shape[0] // BLOCK
    width = global_ref.shape[1]
    score_scale = (width // HEADS) ** (-0.5)
    d_global = norm_back(
        info_ref, dsum_ref, global_ref, sums_ref[...], backs_ref[...], 2, vec_ref[7:8, :], 2
    )
    d_low = low(d_global)
    dlow_ref[...] = d_low
    d_att = low(mm_back(d_low, w_ref[8]))
    masks = head_masks(width)
    tall = tall_masks(width)
    turned_att = low(mm_back(w_ref[8], d_low))
    yield
    d_probs = [
        mm(v_ref[nodes_of(place), :], side_stack(turned_att[:, nodes_of(place)], tall))
        for place in range(group)
    ]
    yield
    for place in range(group):
        nodes = nodes_of(place)
        for head in range(HEADS):
            cols = nodes_of(head)
            prob = prob_ref[nodes, cols].astype(f32)
            part = d_probs[place][:, cols]
            inner = jnp.sum(prob * part, axis=0, keepdims=True)
            d_score = low(prob * ((part - inner) * score_scale))
            score_ref[nodes, cols] = d_score
    yield
    for place in range(group):
        nodes = nodes_of(place)
        dqkv_ref[nodes, :width] = turned_product(k_ref[nodes, :].T, score_ref, nodes, width // HEADS)
        dqkv_ref[nodes, width : 2 * width] = low(
            mm(score_ref[nodes, :], head_stack(q_ref[nodes, :], masks))
        )
        dqkv_ref[nodes, 2 * width :] = low(
            mm(prob_ref[nodes, :], head_stack(d_att[nodes], masks))
        )
    add_rows(
        stat_ref,
        [
            col_sum(d_global),
        ],
    )


def back_kernel(
    info_ref, dsum_ref, lhat_ref, slope_ref, recip_ref, fall_ref, open_ref, bend_ref, bsrc_ref,
    hot_ref, turned_ref, ghat_ref, q_ref, k_ref, v_ref, prob_ref, sums_ref, backs_ref, w_ref,
    vec_ref,
    dnode_ref, dedge_ref, lstat_ref, dqkv_ref, dlow_ref, gstat_ref, score_ref,
):
    runs = [
        attend_back_steps(
            info_ref, dsum_ref, ghat_ref, q_ref, k_ref, v_ref, prob_ref, sums_ref, backs_ref,
            w_ref, vec_ref, dqkv_ref, dlow_ref, gstat_ref, score_ref,
        ),
        local_back_steps(
            info_ref, dsum_ref, lhat_ref, slope_ref, recip_ref, fall_ref, open_ref, bend_ref,
            bsrc_ref, hot_ref, turned_ref, sums_ref, backs_ref, vec_ref, dnode_ref, dedge_ref,
            lstat_ref,
        ),
    ]
    while runs:
        runs = [run for run in runs if next(run, 1) is None]


def branch_grad_kernel(
    info_ref, x_ref, e_ref, att_ref, dnode_ref, dedge_ref, dqkv_ref, dlow_ref, igrad_ref, ograd_ref,
    *outs,
):
    outs, bias_ref, (node_ref, wide_ref, edge_ref, acc_ref) = outs[:-5], outs[-5], outs[-4:]
    width = x_ref.shape[1]
    for place in (0, 2):
        bias_ref[:, place // 2 * width : (place // 2 + 1) * width] = ones_sum(
            dqkv_ref, slice(place * width, (place + 1) * width)
        )
    x = x_ref[...]
    node_ref[...] = mm_rows(x, dnode_ref[...])
    wide_ref[...] = mm_rows(x, dqkv_ref[...])
    edge_ref[...] = mm_rows(e_ref[...], dedge_ref[...])
    acc_ref[...] = mm_rows(att_ref[...], dlow_ref[...])
    cols = [slice(place * width, (place + 1) * width) for place in range(4)]
    parts = [node_ref.at[:, cols[0]], node_ref.at[:, cols[1]], edge_ref]
    parts = parts + [node_ref.at[:, cols[2]], node_ref.at[:, cols[3]]]
    parts = parts + [wide_ref.at[:, cols[place]] for place in range(3)] + [acc_ref]
    parts = parts + [igrad_ref.at[:, cols[place]] for place in range(2)]
    parts = parts + [ograd_ref.at[cols[place], :] for place in range(2)]
    if len(outs) == 1:
        for place, part in enumerate(parts):
            outs[0][place] = low(part[...])
    else:
        pack(info_ref, parts, outs)


def reach(order, index):
    found = 0
    for place, step in enumerate(order):
        if index >> (len(order) - 1 - place) & 1:
            found ^= step >> 1
    return found


def odd_bits(number):
    return bin(number).count("1") & 1


def parity(chip, slots):
    bits = chip
    for place in range(1, slots.bit_length() - 1):
        bits = jnp.bitwise_xor(bits, lax.shift_right_logical(chip, jnp.int32(place)))
    return jnp.bitwise_and(bits, 1)


def chip_orders(total):
    chips = steps_of(total)[1:]
    return (chips, chips[1:-1] + chips[:1] + chips[-1:])


def pack(info_ref, parts, outs):
    half = outs[0].shape[0]
    slots = 2 * half
    orders = chip_orders(2 * slots)
    core = info_ref[info_ref.shape[0] - 2]
    chip = info_ref[info_ref.shape[0] - 1]
    even = parity(jnp.bitwise_and(chip, slots // 2 - 1), slots)
    for slot in range(slots):
        near = [reach(order, slot) for order in orders]
        for out_ref, owner in zip(outs[slot // half :: 2], (core, 1 - core)):
            step = jnp.where(owner == even, near[0], near[1])
            side = 1 - owner if odd_bits(slot >> 1) else owner
            row = pl.multiple_of(16 * jnp.bitwise_xor(chip, step) + 8 * side, 8)
            for first in range(0, len(parts), 2):
                pair = [part[pl.ds(row, 8), :] for part in parts[first : first + 2]]
                out_ref[slot % half, first * 8 : first * 8 + 8 * len(pair), :] = low(
                    jnp.concatenate(pair, axis=0)
                )


def assemble_kernel(info_ref, near_ref, far_ref, near_other_ref, far_other_ref, out_ref):
    half, tall, _ = near_ref.shape
    slots = 2 * half
    orders = chip_orders(2 * slots)
    core = info_ref[info_ref.shape[0] - 2]
    chip = info_ref[info_ref.shape[0] - 1]

    held = (near_ref, far_ref)
    others = (near_other_ref, far_other_ref)

    def fill(role, own):
        for far in range(slots):
            mine, other = [
                [slot for slot in range(slots) if reach(order, slot) == far][0]
                for order in (orders[role], orders[1 - role])
            ]
            row = pl.multiple_of(16 * jnp.bitwise_xor(chip, far), 16)
            for first in range(0, tall, 16):
                size = min(16, tall - first)
                part = slice(first, first + size)
                pair = [
                    held[mine // half][mine % half, part, :].astype(f32),
                    others[other // half][other % half, part, :].astype(f32),
                ]
                upper, lower = pair if own == odd_bits(far) else pair[::-1]
                for step in range(size // 8):
                    rows = slice(step * 8, step * 8 + 8)
                    out_ref[first // 8 + step, pl.ds(row, 16), :] = low(
                        jnp.concatenate([upper[rows], lower[rows]], axis=0)
                    )

    even = parity(chip, slots)
    for own in range(2):
        for role in range(2):

            @pl.when((core == own) & (jnp.bitwise_xor(even, own) == role))
            def _(own=own, role=role):
                fill(role, own)


def node_grad_kernel(
    info_ref, dsum_ref, lhat_ref, ghat_ref, dnode_ref, dqkv_ref, sums_ref, backs_ref, w_ref,
    vec_ref,
    node_ref,
):
    width = lhat_ref.shape[1]
    sums = sums_ref[...]
    backs = backs_ref[...]
    total = norm_back(info_ref, dsum_ref, lhat_ref, sums, backs, 0, vec_ref[5:6, :], 1)
    total = total + norm_back(info_ref, dsum_ref, ghat_ref, sums, backs, 2, vec_ref[7:8, :], 2)
    for place, mat in enumerate((0, 1, 3, 4)):
        total = total + mm_back(dnode_ref[:, place * width : (place + 1) * width], w_ref[mat])
    for place in range(3):
        total = total + mm_back(dqkv_ref[:, place * width : (place + 1) * width], w_ref[5 + place])
    node_ref[...] = total


def edge_grad_kernel(info_ref, dedge_ref, w_ref, edge_ref):
    edge_ref[...] = mm_back(dedge_ref[...], w_ref[2])


def bias_rows(local_ref, attend_ref, inner_ref, wide_ref):
    width = attend_ref.shape[1]
    return jnp.concatenate(
        [
            local_ref[0:2, :],
            wide_ref[0:1, :width],
            wide_ref[0:1, width:],
            attend_ref[0:1, :],
            inner_ref[0:1, :width],
            inner_ref[0:1, width:],
            jnp.zeros((1, width), f32),
        ],
        axis=0,
    )


def last_kernel(
    info_ref, kept_ref, got_ref, local_ref, attend_ref, inner_ref, wide_ref, out_ref
):
    biases = bias_rows(local_ref, attend_ref, inner_ref, wide_ref)
    upper = low(biases).astype(f32)
    for slot, extra in enumerate((upper, biases - upper)):
        total = kept_ref[slot].astype(f32) + got_ref[slot].astype(f32)
        out_ref[slot] = low(jnp.concatenate([total, extra], axis=0))


def total_square(values):
    return jnp.sum(jnp.sum(values * values, axis=0, keepdims=True), axis=1, keepdims=True)


def pair_kernel(info_ref, mine_ref, got_ref, grad_ref, tail_ref):
    rows = grad_ref.shape[1]
    half = grad_ref.shape[2]
    mine = [mine_ref[slot].astype(f32) for slot in range(2)]
    got = [got_ref[slot].astype(f32) for slot in range(2)]
    grad = mine[0][:rows] + got[1][:rows]
    other = mine[1][:rows] + got[0][:rows]
    grad_ref[0] = grad[:, :half]
    grad_ref[1] = grad[:, half:]
    tail_ref[...] = (mine[0][rows:] + mine[1][rows:]) + (got[0][rows:] + got[1][rows:])
    tail_ref[7:8, :] = jnp.broadcast_to(total_square(grad) + total_square(other), (1, 2 * half))


def square_kernel(
    info_ref, kept_ref, got_ref, local_ref, attend_ref, inner_ref, wide_ref, grad_ref, tail_ref
):
    grad = kept_ref[...].astype(f32) + got_ref[...].astype(f32)
    half = grad.shape[1] // 2
    grad_ref[0] = grad[:, :half]
    grad_ref[1] = grad[:, half:]
    tail_ref[...] = bias_rows(local_ref, attend_ref, inner_ref, wide_ref)
    tail_ref[7:8, :] = jnp.broadcast_to(total_square(grad), (1, tail_ref.shape[1]))


def update_kernel(
    info_ref, grad_ref, tail_ref, sums_ref, tops_ref, backs_ref, w_ref, w1_ref, w2_ref, v_ref,
    v1_ref, v2_ref,
    new_w_ref, new_w1_ref, new_w2_ref, new_v_ref, new_v1_ref, new_v2_ref, norm_ref,
):
    tail = tail_ref[...]
    tops = tops_ref[...]
    backs = backs_ref[...]
    mean, rstd = norm_terms(tops, 0, sums_ref[4:5, :])
    grad_v = jnp.concatenate(
        [
            tail[0:5],
            backs[1:2],
            backs[0:1],
            backs[2:3],
            backs[0:1],
            tail[5:7],
            backs[3:4],
            (tops[3:4] - mean * tops[2:3]) * rstd,
            tops[2:3],
        ],
        axis=0,
    )
    square = jnp.sum(jnp.sum(grad_v * grad_v, axis=0, keepdims=True), axis=1, keepdims=True)
    norm = jnp.sqrt(tail[7:8, 0:1] + square)
    norm_ref[...] = norm
    factor = jnp.minimum(1.0, clip_limit / (norm + 1e-06))
    new_v_ref[...], new_v1_ref[...], new_v2_ref[...] = adamw(
        v_ref[...], factor * grad_v, v1_ref[...], v2_ref[...], rate_vecs, 0.0
    )
    mats, span = w_ref.shape
    _, rows, half = grad_ref.shape
    for piece in range(span // half):
        cols = slice(piece * half, (piece + 1) * half)
        if rows == mats:
            grad = grad_ref[piece]
        else:
            grad = grad_ref[piece % 2, pl.ds(piece // 2, mats, rows // mats), :]
        new_w_ref[:, cols], new_w1_ref[:, cols], new_w2_ref[:, cols] = adamw(
            w_ref[:, cols], factor * grad, w1_ref[:, cols], w2_ref[:, cols], rate_mats, decay_mats
        )


def rows_spec(rows, width, offset=0):
    if offset:
        return pl.BlockSpec((rows, width), lambda step, info: (step + info[0], 0))
    return pl.BlockSpec((rows, width), lambda step, info: (step, 0))


def whole_spec(shape):
    zeros = (0,) * len(shape)
    return pl.BlockSpec(shape, lambda step, info: zeros)


def call(kernel, steps, info, inputs, outputs, scratch=(), room=10, cost=5):
    in_specs = []
    arrays = []
    for array, spec in inputs:
        arrays.append(array)
        in_specs.append(whole_spec(array.shape) if spec is None else spec)
    out_specs = []
    out_shapes = []
    for shape, dtype, spec, *far in outputs:
        out_specs.append(whole_spec(shape) if spec is None else spec)
        out_shapes.append(pltpu.HBM(shape, dtype) if far else jax.ShapeDtypeStruct(shape, dtype))
    return pl.pallas_call(
        kernel,
        grid_spec=pltpu.PrefetchScalarGridSpec(
            num_scalar_prefetch=1,
            grid=(steps,),
            in_specs=in_specs,
            out_specs=out_specs,
            scratch_shapes=list(scratch),
        ),
        out_shape=out_shapes,
        compiler_params=pltpu.CompilerParams(
            dimension_semantics=("arbitrary",), vmem_limit_bytes=room * 1024 * 1024
        ),
        name=kernel.__name__,
        cost_estimate=pl.CostEstimate(
            flops=cost * 1000000000, bytes_accessed=cost * 1000000, transcendentals=0
        ),
    )(info, *arrays)


def swap_with(values, step, total):
    return lax.ppermute(values, axis_names, [(place, place ^ step) for place in range(total)])


def steps_of(total):
    return [1 << power for power in range(total.bit_length() - 1)]


def beside(start, transfer, info, work):
    info = lax.optimization_barrier((info, start))[0]
    return lax.optimization_barrier((transfer, work(info)))


def sum_steps(total):
    return [step | 1 for step in steps_of(total)]


def sum_small(values, total, info=None, works=()):
    results = []
    works = list(works)
    for step in sum_steps(total):
        other = swap_with(values, step, total)
        if works and step > 1:
            other, done = beside(values, other, info, works.pop(0))
            results.append(done)
        values = values + other
    return (values, results) if results else values


def swap_chips(values, number, total, straight=0):
    orders = chip_orders(total)
    pairs = []
    for place in range(total):
        step = orders[odd_bits(place & ~straight)][number]
        pairs.append((place, place ^ (step if step & straight else step | 1)))
    return lax.ppermute(values, axis_names, pairs)


def in_rows(total, width):
    return width * width // total == 8 * width


def gather_matrices(shard, info, total, width, work):
    mats = shard.shape[0]
    if not in_rows(total, width):
        gathered = lax.all_gather(shard, axis_names, axis=1, tiled=True)
        return (gathered.reshape(mats, width, width), work(info))
    held = shard.reshape(1, mats * 8, width)
    for number in reversed(range(1, len(chip_orders(total)[0]))):
        held = jnp.concatenate([held, swap_chips(held, number, total)], axis=0)
    got = swap_chips(held, 0, total)
    other = swap_with(held, 1, total)

    def both(info):
        return (work(info), other)

    got, (done, other) = beside(held, got, info, both)
    far_other = swap_with(got, 1, total)
    matrices = call(
        assemble_kernel,
        1,
        info,
        [(held, None), (got, None), (other, None), (far_other, None)],
        [((mats, width, width), bf16, None)],
    )[0]
    return (matrices, done)


def scatter_plain(grads, total):
    place = lax.axis_index(axis_names)
    mats, width, _ = grads.shape
    bits = total.bit_length() - 1
    held = grads.reshape((mats,) + (2,) * bits + (width * width // total,))
    held = held.transpose(tuple(reversed(range(1, bits + 1))) + (0, bits + 1))
    for step in steps_of(total):
        mine = ((place & step) != 0).astype(jnp.int32)
        sent = lax.dynamic_index_in_dim(held, 1 - mine, 0, keepdims=False)
        kept = lax.dynamic_index_in_dim(held, mine, 0, keepdims=False)
        got = swap_with(sent, step, total)
        if step * 2 < total:
            held = low(kept.astype(f32) + got.astype(f32))
    return (kept, got)


def scatter_packed(kept, far_kept, sent, far_sent, total, info, works, biases):
    far_got = swap_with(far_sent, 1, total)
    got = swap_with(sent, 1, total)
    results = []
    rounds = len(chip_orders(total)[0])
    for number in range(rounds - 1):
        if number:
            half = kept.shape[0] // 2
            far_kept, far_got = kept[half:], got[half:]
            kept, got = kept[:half], got[:half]
        sent = low(far_kept.astype(f32) + far_got.astype(f32))
        kept = kept.astype(f32) + got.astype(f32)
        got = swap_chips(sent, number, total, total // 2)
        if number < len(works):
            got, done = beside(sent, got, info, works[number])
            results.append(done)
    mine = call(
        last_kernel,
        1,
        info,
        [(array, None) for array in (kept, got, *biases)],
        [((2, kept.shape[1] + 8, kept.shape[2]), bf16, None)],
    )[0]
    got = swap_chips(mine, rounds - 1, total, total // 2)
    grad_rows, tail = call(
        pair_kernel,
        1,
        info,
        [(mine, None), (got, None)],
        [((2, kept.shape[1], kept.shape[2] // 2), f32, None), ((8, kept.shape[2]), f32, None)],
    )
    for step in sum_steps(total)[:-1]:
        tail = tail + swap_with(tail, step, total)
    return (grad_rows, tail, results)


def adamw(params, gradient, moment_one, moment_two, rate, decay):
    first = beta_one * moment_one + (1.0 - beta_one) * gradient
    second = beta_two * moment_two + (1.0 - beta_two) * gradient * gradient
    first_hat = first / (1.0 - beta_one**STEP)
    second_hat = second / (1.0 - beta_two**STEP)
    updated = params - rate * (first_hat / (jnp.sqrt(second_hat) + adam_eps) + decay * params)
    return (updated, first, second)


def own_half(values, branch_index):
    half = values.shape[0] // 2
    return lax.dynamic_slice_in_dim(values, branch_index * half, half, 0)


def per_device(
    node_feats,
    edge_feats,
    cotangent,
    graph_ids,
    node_mask,
    edge_src,
    edge_dst,
    edge_mask,
    weights,
    weight_moment1,
    weight_moment2,
    vectors,
    vector_moment1,
    vector_moment2,
):
    total = lax.axis_size("rows") * lax.axis_size("branch")
    branch_index = lax.axis_index("branch")
    width = node_feats.shape[1]
    rows = node_feats.shape[0] // 2
    edges = edge_feats.shape[0] // 2
    blocks = rows // BLOCK
    group = math.gcd(blocks, GROUP)
    steps = blocks // group
    tall = group * BLOCK
    tall_edges = group * EB
    w_bf = low(weights)
    own_nodes = own_half(node_feats, branch_index)
    own_edges = own_half(edge_feats, branch_index)
    counts = jnp.sum(own_half(node_mask, branch_index).reshape(blocks, BLOCK), axis=1)
    info = jnp.concatenate(
        [(branch_index * steps)[None], counts, branch_index[None], lax.axis_index("rows")[None]]
    ).astype(jnp.int32)

    def by_step(values, slots):
        return own_half(values, branch_index).reshape(steps, group, slots)

    def step_spec(slots):
        return pl.BlockSpec((1, group, slots), lambda step, info: (step, 0, 0))

    edge_spec = rows_spec(tall_edges, width)
    node_spec = rows_spec(tall, width)
    def prep_work(info):
        return call(
            prep_kernel,
            steps,
            info,
            [
                (by_step(edge_src, EB), step_spec(EB)),
                (by_step(edge_dst, EB), step_spec(EB)),
                (by_step(edge_mask, EB), step_spec(EB)),
                (by_step(graph_ids, BLOCK), step_spec(BLOCK)),
            ],
            [
                ((edges, EB), bf16, edge_spec, True),
                ((edges, EB), bf16, edge_spec, True),
                ((rows, BLOCK), f32, rows_spec(tall, BLOCK)),
            ],
        )

    matrices, (hot, turned, bias) = gather_matrices(w_bf, info, total, width, prep_work)
    x_in = (own_nodes, node_spec)
    e_in = (own_edges, edge_spec)
    mats_in = (matrices, None)
    vec_in = (vectors, None)
    node_f32 = ((rows, width), f32, node_spec)
    node_bf = ((rows, width), bf16, node_spec)
    sums_out = ((8, width), f32, None)
    prob_spec = rows_spec(tall, HEADS * BLOCK)
    (
        local_out, gate_slope, recip, fall, opened, bend, b_source,
        global_out, queries, keyed, valued, attended, probs, sums_part,
    ) = call(
        forward_kernel,
        steps,
        info,
        [
            x_in,
            e_in,
            (bias, rows_spec(tall, BLOCK)),
            (hot, edge_spec),
            (turned, edge_spec),
            mats_in,
            vec_in,
        ],
        [
            node_f32,
            node_bf,
            node_bf,
            node_bf,
            ((edges, width), bf16, edge_spec),
            ((edges, width), bf16, edge_spec),
            ((edges, width), bf16, edge_spec),
            node_f32,
            node_bf,
            node_bf,
            node_bf,
            node_bf,
            ((rows, HEADS * BLOCK), bf16, prob_spec),
            sums_out,
        ],
        room=FRONT_ROOM,
    )
    sums = sum_small(sums_part, total)
    sums_in = (sums, None)
    cot_in = (cotangent, node_spec)
    wide_spec = rows_spec(tall, 2 * width)
    summed_low, hidden_low, hidden_slope, mixed, top_part = call(
        mix_kernel,
        steps,
        info,
        [(local_out, node_spec), (global_out, node_spec), cot_in, sums_in, mats_in, vec_in],
        [
            node_bf,
            ((rows, 2 * width), bf16, wide_spec),
            ((rows, 2 * width), bf16, wide_spec),
            node_f32,
            sums_out,
        ],
    )

    def hat_work(info):
        return call(
            hat_kernel,
            steps,
            info,
            [(local_out, node_spec), (global_out, node_spec), sums_in],
            [node_bf, node_bf],
        )

    tops, ((local_hat, global_hat),) = sum_small(top_part, total, info, [hat_work])
    d_mixed, d_hidden, d_summed, back_part = call(
        mix_back_kernel,
        steps,
        info,
        [
            (mixed, node_spec),
            (hidden_slope, wide_spec),
            cot_in,
            (local_hat, node_spec),
            (global_hat, node_spec),
            sums_in,
            (tops, None),
            mats_in,
            vec_in,
        ],
        [
            node_bf,
            ((rows, 2 * width), bf16, wide_spec),
            node_bf,
            sums_out,
        ],
    )

    def mat_out(tall_by, wide_by):
        return ((tall_by * width, wide_by * width), f32, None)

    def inner_work(info):
        return call(
            inner_grad_kernel,
            steps,
            info,
            [(summed_low, node_spec), (d_hidden, wide_spec)],
            [mat_out(1, 2), ((8, 2 * width), f32, None)],
        )

    def outer_work(info):
        return call(
            outer_grad_kernel,
            steps,
            info,
            [(hidden_low, wide_spec), (d_mixed, node_spec)],
            [mat_out(2, 1)],
        )[0]

    def layer_work(info):
        return call(
            layer_kernel,
            steps,
            info,
            [(mixed, node_spec), sums_in, (tops, None), vec_in],
            [node_bf],
        )[0]

    backs, ((inner_grads, inner_bias), outer_grads, layer_out) = sum_small(
        back_part, total, info, [inner_work, outer_work, layer_work]
    )
    backs_in = (backs, None)
    dsum_in = (d_summed, node_spec)
    dnode_spec = rows_spec(tall, 4 * width)
    dqkv_spec = rows_spec(tall, 3 * width)
    slots = total // 2
    packed = in_rows(total, width)
    grad_outs = [((MATS, width, width), bf16, None)]
    if packed:
        grad_outs = [((slots // 2, MATS * 8, width), bf16, None)] * 4
    d_node, d_edge, local_bias, d_qkv, d_low, attend_bias = call(
        back_kernel,
        steps,
        info,
        [
            dsum_in,
            (local_hat, node_spec),
            (gate_slope, node_spec),
            (recip, node_spec),
            (fall, node_spec),
            (opened, edge_spec),
            (bend, edge_spec),
            (b_source, edge_spec),
            (hot, edge_spec),
            (turned, edge_spec),
            (global_hat, node_spec),
            (queries, node_spec),
            (keyed, node_spec),
            (valued, node_spec),
            (probs, prob_spec),
            sums_in,
            backs_in,
            mats_in,
            vec_in,
        ],
        [
            ((rows, 4 * width), bf16, dnode_spec),
            ((edges, width), bf16, edge_spec),
            sums_out,
            ((rows, 3 * width), bf16, dqkv_spec),
            node_bf,
            sums_out,
        ],
        [pltpu.VMEM((tall, HEADS * BLOCK), bf16)],
        room=BACK_ROOM,
    )
    *grads, wide_bias = call(
        branch_grad_kernel,
        1,
        info,
        [
            (own_nodes, None),
            (own_edges, None),
            (attended, None),
            (d_node, None),
            (d_edge, None),
            (d_qkv, None),
            (d_low, None),
            (inner_grads, None),
            (outer_grads, None),
        ],
        grad_outs + [((8, 2 * width), f32, None)],
        [
            pltpu.VMEM((width, 4 * width), f32),
            pltpu.VMEM((width, 3 * width), f32),
            pltpu.VMEM((width, width), f32),
            pltpu.VMEM((width, width), f32),
        ],
    )

    def node_work(info):
        return call(
            node_grad_kernel,
            steps,
            info,
            [
                dsum_in,
                (local_hat, node_spec),
                (global_hat, node_spec),
                (d_node, dnode_spec),
                (d_qkv, dqkv_spec),
                sums_in,
                backs_in,
                mats_in,
                vec_in,
            ],
            [node_f32],
        )[0]

    def edge_work(info):
        return call(
            edge_grad_kernel,
            steps,
            info,
            [(d_edge, edge_spec), mats_in],
            [((edges, width), f32, edge_spec)],
        )[0]

    biases = (local_bias, attend_bias, inner_bias, wide_bias)
    if packed:
        grad_rows, tail, (node_grad, edge_grad) = scatter_packed(
            *grads, total, info, [node_work, edge_work], biases
        )
    else:
        grad_shard = scatter_plain(grads[0], total)
        node_grad, edge_grad = node_work(info), edge_work(info)
        grad_rows, tail_part = call(
            square_kernel,
            1,
            info,
            [(array, None) for array in (*grad_shard, *biases)],
            [
                ((2, grad_shard[0].shape[0], grad_shard[0].shape[1] // 2), f32, None),
                sums_out,
            ],
        )
        tail = sum_small(tail_part, total)
    like_mats = (weights.shape, f32, None)
    like_vecs = (vectors.shape, f32, None)
    new_weights, first_w, second_w, new_vectors, first_v, second_v, norm = call(
        update_kernel,
        1,
        info,
        [
            (array, None)
            for array in (
                grad_rows, tail, sums, tops, backs, weights, weight_moment1, weight_moment2,
                vectors, vector_moment1, vector_moment2,
            )
        ],
        [like_mats] * 3 + [like_vecs] * 3 + [((1, 1), f32, None)],
    )
    grad_norm = norm.reshape(())
    return (
        layer_out,
        node_grad,
        edge_grad,
        new_weights,
        first_w,
        second_w,
        new_vectors,
        first_v,
        second_v,
        grad_norm,
    )


def solution(mesh):
    in_specs = (
        P("rows", None),
        P("rows", None),
        P(("rows", "branch"), None),
        P("rows"),
        P("rows"),
        P("rows"),
        P("rows"),
        P("rows"),
        P(None, ("rows", "branch")),
        P(None, ("rows", "branch")),
        P(None, ("rows", "branch")),
        P(),
        P(),
        P(),
    )
    out_specs = (
        P(("rows", "branch"), None),
        P(("rows", "branch"), None),
        P(("rows", "branch"), None),
        P(None, ("rows", "branch")),
        P(None, ("rows", "branch")),
        P(None, ("rows", "branch")),
        P(),
        P(),
        P(),
        P(),
    )
    return jax.shard_map(
        per_device, mesh=mesh, in_specs=in_specs, out_specs=out_specs, check_vma=False
    )
```

```python
import functools
import math

import jax
import jax.numpy as jnp
from jax import lax
from jax.experimental import pallas as pl
from jax.experimental.pallas import tpu as pltpu
from jax.sharding import PartitionSpec as P

HEADS = 8
BLOCK = 128
EB = 256
MATS = 13
STEP = 7
GROUP = 8
BACK_ROOM = 12
FRONT_ROOM = 12

eps_norm = 1e-05
clip_limit = 1.0
beta_one = 0.9
beta_two = 0.999
rate_mats = 0.1
rate_vecs = 0.8
decay_mats = 0.01
adam_eps = 1e-08
hidden_floor = -1e30
axis_names = ("rows", "branch")
f32 = jnp.float32
bf16 = jnp.bfloat16


def mm(left, right):
    return jnp.dot(left, right, preferred_element_type=f32)


def mm_back(left, right):
    return lax.dot_general(left, right, (((1,), (1,)), ((), ())), preferred_element_type=f32)


def mm_rows(left, right):
    return lax.dot_general(left, right, (((0,), (0,)), ((), ())), preferred_element_type=f32)


def low(values):
    return values.astype(bf16)


def sig(values):
    return 0.5 * jnp.tanh(0.5 * values) + 0.5


def col_sum(values):
    return jnp.sum(values, axis=0, keepdims=True)


def live_of(info_ref, first_block, group, width):
    slot = lax.broadcasted_iota(jnp.int32, (BLOCK, width), 0)
    return jnp.concatenate(
        [
            jnp.where(slot < info_ref[1 + first_block + place], 1.0, 0.0)
            for place in range(group)
        ],
        axis=0,
    )


def nodes_of(place):
    return slice(place * BLOCK, (place + 1) * BLOCK)


def edges_of(place):
    return slice(place * EB, (place + 1) * EB)


def add_rows(out_ref, rows):
    @pl.when(pl.program_id(0) == 0)
    def _():
        out_ref[...] = jnp.zeros_like(out_ref)

    for place, row in enumerate(rows):
        out_ref[place : place + 1, :] += row


def norm_terms(sums, first, count_row):
    mean = sums[first : first + 1] / count_row
    rstd = lax.rsqrt(sums[first + 1 : first + 2] / count_row - mean * mean + eps_norm)
    return (mean, rstd)


def prep_kernel(info_ref, src_ref, dst_ref, mask_ref, id_ref, hot_ref, turned_ref, bias_ref):
    for place in range(GROUP):
        row = pl.ds(place, 1)
        node = lax.broadcasted_iota(jnp.int32, (BLOCK, EB), 0)
        live = mask_ref[0, row, :] != 0
        dst_rows = jnp.where((node == dst_ref[0, row, :]) & live, 1.0, 0.0)
        src_rows = jnp.where((node == src_ref[0, row, :]) & live, 1.0, 0.0)
        turned = jnp.concatenate([dst_rows, src_rows], axis=0)
        turned_ref[place * EB : (place + 1) * EB, :] = low(turned)
        hot_ref[place * EB : (place + 1) * EB, :] = low(turned.T)
        ids = jnp.broadcast_to(id_ref[0, row, :].astype(f32), (BLOCK, BLOCK))
        bias_ref[place * BLOCK : (place + 1) * BLOCK, :] = jnp.where(
            ids == ids.T, 0.0, hidden_floor
        )


def local_steps(
    info_ref, x_ref, e_ref, hot_ref, turned_ref, w_ref, vec_ref,
    out_ref, slope_ref, recip_ref, fall_ref, open_ref, bend_ref, bsrc_ref, stats,
):
    group = x_ref.shape[0] // BLOCK
    x = x_ref[...]
    a_part = mm(x, w_ref[0]) + vec_ref[0:1, :]
    b_part = low(mm(x, w_ref[1]))
    d_part = low(mm(x, w_ref[3]))
    e_part = low(mm(x, w_ref[4]))
    c_part = mm(e_ref[...], w_ref[2]) + vec_ref[1:2, :]
    gates = []
    picks = []
    for place in range(group):
        nodes = nodes_of(place)
        hot = hot_ref[edges_of(place), :]
        gates.append(mm(hot, jnp.concatenate([d_part[nodes], e_part[nodes]], axis=0)))
        picks.append(mm(hot[:, BLOCK:], b_part[nodes]))
    yield
    sums = []
    for place in range(group):
        edges = edges_of(place)
        opened = sig(c_part[edges] + gates[place])
        b_source = picks[place]
        opened_low = low(opened)
        open_ref[edges, :] = opened_low
        bend_ref[edges, :] = low(opened * (1.0 - opened))
        bsrc_ref[edges, :] = low(b_source)
        dst_turned = turned_ref[place * EB : place * EB + BLOCK, :]
        sums.append(
            mm(dst_turned, jnp.concatenate([low(opened * b_source), opened_low], axis=1))
        )
    yield
    both = jnp.concatenate(sums, axis=0)
    width = x.shape[1]
    recip = 1.0 / (both[:, width:] + 1.0)
    ratio = both[:, :width] * recip
    gated = a_part + ratio
    gated_sig = sig(gated)
    out = x.astype(f32) + gated * gated_sig
    slope_ref[...] = low(gated_sig * (1.0 + gated * (1.0 - gated_sig)))
    recip_ref[...] = low(recip)
    fall_ref[...] = low(ratio * recip)
    out_ref[...] = out
    live = live_of(info_ref, pl.program_id(0) * group, group, out.shape[1])
    kept = live * out
    stats[0:2] = [col_sum(kept), col_sum(kept * out)]


def head_masks(width):
    head = lax.broadcasted_iota(jnp.int32, (16, width), 1) // (width // HEADS)
    return [low(jnp.where(head == place, 1.0, 0.0))[:1] for place in range(HEADS)]


def head_stack(values, masks):
    return jnp.concatenate([values * mask for mask in masks], axis=0)


def tall_masks(width):
    head = lax.broadcasted_iota(jnp.int32, (width, BLOCK), 0) // (width // HEADS)
    return [low(jnp.where(head == place, 1.0, 0.0)) for place in range(HEADS)]


def side_stack(turned, masks):
    return jnp.concatenate([turned * mask for mask in masks], axis=1)


def turned_product(turned, weight, nodes, size):
    parts = []
    for head in range(0, HEADS, 2):
        both = mm(
            turned[head * size : (head + 2) * size],
            weight[nodes, head * BLOCK : (head + 2) * BLOCK],
        )
        parts += [both[:size, :BLOCK], both[size:, BLOCK:]]
    return low(jnp.concatenate(parts, axis=0)).T


def attend_steps(
    info_ref, x_ref, bias_ref, w_ref, vec_ref,
    out_ref, q_ref, k_ref, v_ref, att_ref, prob_ref, stats,
):
    group = x_ref.shape[0] // BLOCK
    x = x_ref[...]
    queries = low(mm(x, w_ref[5]) + vec_ref[2:3, :])
    keyed = low(mm(x, w_ref[6]))
    valued = low(mm(x, w_ref[7]) + vec_ref[3:4, :])
    q_ref[...] = queries
    k_ref[...] = keyed
    v_ref[...] = valued
    score_scale = (x.shape[1] // HEADS) ** (-0.5) * math.log2(math.e)
    tall = tall_masks(x.shape[1])
    queries_turned = queries.T
    valued_turned = valued.T
    size = x.shape[1] // HEADS
    raws = [
        mm(keyed[nodes_of(place)], side_stack(queries_turned[:, nodes_of(place)], tall))
        for place in range(group)
    ]
    yield
    for place in range(group):
        nodes = nodes_of(place)
        bias = bias_ref[nodes, :]
        for head in range(HEADS):
            cols = nodes_of(head)
            part = raws[place][:, cols] + bias
            part = jnp.exp2((part - jnp.max(part, axis=0, keepdims=True)) * score_scale)
            prob_ref[nodes, cols] = low(part * (1.0 / jnp.sum(part, axis=0, keepdims=True)))
    yield
    for place in range(group):
        nodes = nodes_of(place)
        att_ref[nodes, :] = turned_product(valued_turned[:, nodes], prob_ref, nodes, size)
    out = x.astype(f32) + mm(att_ref[...], w_ref[8]) + vec_ref[4:5, :]
    out_ref[...] = out
    live = live_of(info_ref, pl.program_id(0) * group, group, out.shape[1])
    kept = live * out
    stats[2:4] = [col_sum(kept), col_sum(kept * out)]


def forward_kernel(
    info_ref, x_ref, e_ref, bias_ref, hot_ref, turned_ref, w_ref, vec_ref,
    lout_ref, slope_ref, recip_ref, fall_ref, open_ref, bend_ref, bsrc_ref,
    gout_ref, q_ref, k_ref, v_ref, att_ref, prob_ref, sums_ref,
):
    stats = [None] * 4
    runs = [
        attend_steps(
            info_ref, x_ref, bias_ref, w_ref, vec_ref, gout_ref, q_ref, k_ref, v_ref, att_ref,
            prob_ref, stats,
        ),
        local_steps(
            info_ref, x_ref, e_ref, hot_ref, turned_ref, w_ref, vec_ref, lout_ref, slope_ref,
            recip_ref, fall_ref, open_ref, bend_ref, bsrc_ref, stats,
        ),
    ]
    while runs:
        runs = [run for run in runs if next(run, 1) is None]
    add_rows(sums_ref, stats)

    @pl.when(pl.program_id(0) == 0)
    def _():
        count = info_ref[1]
        for place in range(2, info_ref.shape[0] - 2):
            count = count + info_ref[place]
        sums_ref[4:5, :] = jnp.full((1, x_ref.shape[1]), count, jnp.int32).astype(f32)


def mix_kernel(
    info_ref, local_ref, global_ref, cot_ref, sums_ref, w_ref, vec_ref,
    low_ref, hlow_ref, slope_ref, mixed_ref, stat_ref,
):
    group = local_ref.shape[0] // BLOCK
    width = local_ref.shape[1]
    sums = sums_ref[...]
    count_row = sums[4:5]
    local_mean, local_rstd = norm_terms(sums, 0, count_row)
    global_mean, global_rstd = norm_terms(sums, 2, count_row)
    local_gain = vec_ref[5:6, :] * local_rstd
    global_gain = vec_ref[7:8, :] * global_rstd
    local_norm = local_ref[...] * local_gain + (vec_ref[6:7, :] - local_mean * local_gain)
    global_norm = global_ref[...] * global_gain + (vec_ref[8:9, :] - global_mean * global_gain)
    summed = low(local_norm).astype(f32) + low(global_norm).astype(f32)
    summed_low = low(summed)
    low_ref[...] = summed_low
    mixed = summed + vec_ref[11:12, :]
    for half in range(2):
        hidden = mm(summed_low, w_ref[9 + half]) + vec_ref[9 + half : 10 + half, :]
        sig_value = sig(hidden)
        hidden_low = low(hidden * sig_value)
        slope_ref[:, half * width : (half + 1) * width] = low(
            sig_value * (1.0 + hidden * (1.0 - sig_value))
        )
        hlow_ref[:, half * width : (half + 1) * width] = hidden_low
        mixed = mixed + mm(hidden_low, w_ref[11 + half])
    mixed_ref[...] = mixed
    live = live_of(info_ref, pl.program_id(0) * group, group, width)
    kept = live * mixed
    d_norm = live * cot_ref[...].astype(f32)
    add_rows(
        stat_ref, [col_sum(kept), col_sum(kept * mixed), col_sum(d_norm), col_sum(d_norm * mixed)]
    )


def hat_kernel(info_ref, local_ref, global_ref, sums_ref, lhat_ref, ghat_ref):
    sums = sums_ref[...]
    for value_ref, hat_ref, first in ((local_ref, lhat_ref, 0), (global_ref, ghat_ref, 2)):
        mean, rstd = norm_terms(sums, first, sums[4:5])
        hat_ref[...] = low((value_ref[...] - mean) * rstd)


def mix_back_kernel(
    info_ref, mixed_ref, slope_ref, cot_ref, lhat_ref, ghat_ref, sums_ref, tops_ref, w_ref,
    vec_ref,
    dmix_ref, dhid_ref, dsum_ref, stat_ref,
):
    group = mixed_ref.shape[0] // BLOCK
    width = mixed_ref.shape[1]
    sums = sums_ref[...]
    tops = tops_ref[...]
    count_row = sums[4:5]
    mean, rstd = norm_terms(tops, 0, count_row)
    live = live_of(info_ref, pl.program_id(0) * group, group, width)
    hat = (mixed_ref[...] - mean) * rstd
    d_norm = live * cot_ref[...].astype(f32)
    dz_sum = tops[2:3]
    dz_hat = (tops[3:4] - mean * dz_sum) * rstd
    d_mixed = (vec_ref[12:13, :] * rstd) * (
        d_norm - live * (dz_sum / count_row + hat * (dz_hat / count_row))
    )
    d_mixed_low = low(d_mixed)
    dmix_ref[...] = d_mixed_low
    d_summed = d_mixed
    for half in range(2):
        cols = slice(half * width, (half + 1) * width)
        d_hidden = low(mm_back(d_mixed_low, w_ref[11 + half]) * slope_ref[:, cols].astype(f32))
        dhid_ref[:, cols] = d_hidden
        d_summed = d_summed + mm_back(d_hidden, w_ref[9 + half])
    d_low = low(d_summed)
    dsum_ref[...] = d_low
    d_sum = d_low.astype(f32)
    add_rows(
        stat_ref,
        [
            col_sum(d_sum),
            col_sum(d_sum * lhat_ref[...].astype(f32)),
            col_sum(d_sum * ghat_ref[...].astype(f32)),
            col_sum(d_mixed),
        ],
    )


def accumulate(acc_ref, term):
    @pl.when(pl.program_id(0) == 0)
    def _():
        acc_ref[...] = jnp.zeros_like(acc_ref)

    acc_ref[...] += term


def layer_kernel(info_ref, mixed_ref, sums_ref, tops_ref, vec_ref, layer_ref):
    group = mixed_ref.shape[0] // BLOCK
    mean, rstd = norm_terms(tops_ref[...], 0, sums_ref[4:5, :])
    live = live_of(info_ref, pl.program_id(0) * group, group, mixed_ref.shape[1])
    hat = (mixed_ref[...] - mean) * rstd
    layer_ref[...] = low(live * (vec_ref[12:13, :] * hat + vec_ref[13:14, :]))


def ones_sum(ref, cols):
    return mm(jnp.ones((8, ref.shape[0]), bf16), ref[:, cols])


def inner_grad_kernel(info_ref, slow_ref, dhid_ref, out_ref, bias_ref):
    accumulate(out_ref, mm_rows(slow_ref[...], dhid_ref[...]))
    accumulate(bias_ref, ones_sum(dhid_ref, slice(None)))


def outer_grad_kernel(info_ref, hlow_ref, dmix_ref, out_ref):
    accumulate(out_ref, mm_rows(hlow_ref[...], dmix_ref[...]))


def norm_back(info_ref, dsum_ref, hat_ref, sums, backs, first, gain_row, hat_row):
    group = hat_ref.shape[0] // BLOCK
    count_row = sums[4:5]
    rstd = norm_terms(sums, first, count_row)[1]
    live = live_of(info_ref, pl.program_id(0) * group, group, hat_ref.shape[1])
    hat = hat_ref[...].astype(f32)
    return (gain_row * rstd) * (
        dsum_ref[...].astype(f32)
        - live * (backs[0:1] / count_row + hat * (backs[hat_row : hat_row + 1] / count_row))
    )


def local_back_steps(
    info_ref, dsum_ref, local_ref, slope_ref, recip_ref, fall_ref, open_ref, bend_ref, bsrc_ref,
    hot_ref, turned_ref, sums_ref, backs_ref, vec_ref,
    dnode_ref, dedge_ref, stat_ref,
):
    group = local_ref.shape[0] // BLOCK
    width = local_ref.shape[1]
    d_local = norm_back(
        info_ref, dsum_ref, local_ref, sums_ref[...], backs_ref[...], 0, vec_ref[5:6, :], 1
    )
    d_gated = d_local * slope_ref[...].astype(f32)
    dnode_ref[:, :width] = low(d_gated)
    d_num = low(d_gated * recip_ref[...].astype(f32))
    d_den = low(-d_gated * fall_ref[...].astype(f32))
    pre_row = jnp.zeros((1, width), f32)
    yield
    picks = [
        mm(
            hot_ref[edges_of(place), :BLOCK],
            jnp.concatenate([d_num[nodes_of(place)], d_den[nodes_of(place)]], axis=1),
        )
        for place in range(group)
    ]
    yield
    sources = []
    for place in range(group):
        edges = edges_of(place)
        d_message = picks[place][:, :width]
        d_open = d_message * bsrc_ref[edges, :].astype(f32) + picks[place][:, width:]
        sources.append(low(d_message * open_ref[edges, :].astype(f32)))
        d_pre = d_open * bend_ref[edges, :].astype(f32)
        pre_row = pre_row + col_sum(d_pre)
        dedge_ref[edges, :] = low(d_pre)
    yield
    for place in range(group):
        nodes = nodes_of(place)
        turned = turned_ref[edges_of(place), :]
        d_both = low(mm(turned, dedge_ref[edges_of(place), :]))
        dnode_ref[nodes, width : 2 * width] = low(mm(turned[BLOCK:], sources[place]))
        dnode_ref[nodes, 2 * width : 3 * width] = d_both[:BLOCK]
        dnode_ref[nodes, 3 * width :] = d_both[BLOCK:]
    add_rows(stat_ref, [col_sum(d_gated), pre_row])


def attend_back_steps(
    info_ref, dsum_ref, global_ref, q_ref, k_ref, v_ref, prob_ref, sums_ref,
    backs_ref, w_ref, vec_ref,
    dqkv_ref, dlow_ref, stat_ref, score_ref,
):
    group = global_ref.shape[0] // BLOCK
    width = global_ref.shape[1]
    score_scale = (width // HEADS) ** (-0.5)
    d_global = norm_back(
        info_ref, dsum_ref, global_ref, sums_ref[...], backs_ref[...], 2, vec_ref[7:8, :], 2
    )
    d_low = low(d_global)
    dlow_ref[...] = d_low
    d_att = low(mm_back(d_low, w_ref[8]))
    masks = head_masks(width)
    tall = tall_masks(width)
    turned_att = low(mm_back(w_ref[8], d_low))
    yield
    d_probs = [
        mm(v_ref[nodes_of(place), :], side_stack(turned_att[:, nodes_of(place)], tall))
        for place in range(group)
    ]
    yield
    for place in range(group):
        nodes = nodes_of(place)
        for head in range(HEADS):
            cols = nodes_of(head)
            prob = prob_ref[nodes, cols].astype(f32)
            part = d_probs[place][:, cols]
            inner = jnp.sum(prob * part, axis=0, keepdims=True)
            d_score = low(prob * ((part - inner) * score_scale))
            score_ref[nodes, cols] = d_score
    yield
    for place in range(group):
        nodes = nodes_of(place)
        dqkv_ref[nodes, :width] = turned_product(k_ref[nodes, :].T, score_ref, nodes, width // HEADS)
        dqkv_ref[nodes, width : 2 * width] = low(
            mm(score_ref[nodes, :], head_stack(q_ref[nodes, :], masks))
        )
        dqkv_ref[nodes, 2 * width :] = low(
            mm(prob_ref[nodes, :], head_stack(d_att[nodes], masks))
        )
    add_rows(
        stat_ref,
        [
            col_sum(d_global),
        ],
    )


def back_kernel(
    info_ref, dsum_ref, lhat_ref, slope_ref, recip_ref, fall_ref, open_ref, bend_ref, bsrc_ref,
    hot_ref, turned_ref, ghat_ref, q_ref, k_ref, v_ref, prob_ref, sums_ref, backs_ref, w_ref,
    vec_ref,
    dnode_ref, dedge_ref, lstat_ref, dqkv_ref, dlow_ref, gstat_ref, score_ref,
):
    runs = [
        attend_back_steps(
            info_ref, dsum_ref, ghat_ref, q_ref, k_ref, v_ref, prob_ref, sums_ref, backs_ref,
            w_ref, vec_ref, dqkv_ref, dlow_ref, gstat_ref, score_ref,
        ),
        local_back_steps(
            info_ref, dsum_ref, lhat_ref, slope_ref, recip_ref, fall_ref, open_ref, bend_ref,
            bsrc_ref, hot_ref, turned_ref, sums_ref, backs_ref, vec_ref, dnode_ref, dedge_ref,
            lstat_ref,
        ),
    ]
    while runs:
        runs = [run for run in runs if next(run, 1) is None]


def branch_grad_kernel(
    info_ref, x_ref, e_ref, att_ref, dnode_ref, dedge_ref, dqkv_ref, dlow_ref, igrad_ref, ograd_ref,
    *outs,
):
    outs, bias_ref, (node_ref, wide_ref, edge_ref, acc_ref) = outs[:-5], outs[-5], outs[-4:]
    width = x_ref.shape[1]
    for place in (0, 2):
        bias_ref[:, place // 2 * width : (place // 2 + 1) * width] = ones_sum(
            dqkv_ref, slice(place * width, (place + 1) * width)
        )
    x = x_ref[...]
    node_ref[...] = mm_rows(x, dnode_ref[...])
    wide_ref[...] = mm_rows(x, dqkv_ref[...])
    edge_ref[...] = mm_rows(e_ref[...], dedge_ref[...])
    acc_ref[...] = mm_rows(att_ref[...], dlow_ref[...])
    cols = [slice(place * width, (place + 1) * width) for place in range(4)]
    parts = [node_ref.at[:, cols[0]], node_ref.at[:, cols[1]], edge_ref]
    parts = parts + [node_ref.at[:, cols[2]], node_ref.at[:, cols[3]]]
    parts = parts + [wide_ref.at[:, cols[place]] for place in range(3)] + [acc_ref]
    parts = parts + [igrad_ref.at[:, cols[place]] for place in range(2)]
    parts = parts + [ograd_ref.at[cols[place], :] for place in range(2)]
    if len(outs) == 1:
        for place, part in enumerate(parts):
            outs[0][place] = low(part[...])
    else:
        pack(info_ref, parts, outs)


def reach(order, index):
    found = 0
    for place, step in enumerate(order):
        if index >> (len(order) - 1 - place) & 1:
            found ^= step >> 1
    return found


def odd_bits(number):
    return bin(number).count("1") & 1


def parity(chip, slots):
    bits = chip
    for place in range(1, slots.bit_length() - 1):
        bits = jnp.bitwise_xor(bits, lax.shift_right_logical(chip, jnp.int32(place)))
    return jnp.bitwise_and(bits, 1)


def chip_orders(total):
    chips = steps_of(total)[1:]
    return (chips, chips[1:-1] + chips[:1] + chips[-1:])


def pack(info_ref, parts, outs):
    half = outs[0].shape[0]
    slots = 2 * half
    orders = chip_orders(2 * slots)
    core = info_ref[info_ref.shape[0] - 2]
    chip = info_ref[info_ref.shape[0] - 1]
    even = parity(jnp.bitwise_and(chip, slots // 2 - 1), slots)
    for slot in range(slots):
        near = [reach(order, slot) for order in orders]
        for out_ref, owner in zip(outs[slot // half :: 2], (core, 1 - core)):
            step = jnp.where(owner == even, near[0], near[1])
            side = 1 - owner if odd_bits(slot >> 1) else owner
            row = pl.multiple_of(16 * jnp.bitwise_xor(chip, step) + 8 * side, 8)
            for first in range(0, len(parts), 2):
                pair = [part[pl.ds(row, 8), :] for part in parts[first : first + 2]]
                out_ref[slot % half, first * 8 : first * 8 + 8 * len(pair), :] = low(
                    jnp.concatenate(pair, axis=0)
                )


def assemble_kernel(info_ref, near_ref, far_ref, near_other_ref, far_other_ref, out_ref):
    half, tall, _ = near_ref.shape
    slots = 2 * half
    orders = chip_orders(2 * slots)
    core = info_ref[info_ref.shape[0] - 2]
    chip = info_ref[info_ref.shape[0] - 1]

    held = (near_ref, far_ref)
    others = (near_other_ref, far_other_ref)

    def fill(role, own):
        for far in range(slots):
            mine, other = [
                [slot for slot in range(slots) if reach(order, slot) == far][0]
                for order in (orders[role], orders[1 - role])
            ]
            row = pl.multiple_of(16 * jnp.bitwise_xor(chip, far), 16)
            for first in range(0, tall, 16):
                size = min(16, tall - first)
                part = slice(first, first + size)
                pair = [
                    held[mine // half][mine % half, part, :].astype(f32),
                    others[other // half][other % half, part, :].astype(f32),
                ]
                upper, lower = pair if own == odd_bits(far) else pair[::-1]
                for step in range(size // 8):
                    rows = slice(step * 8, step * 8 + 8)
                    out_ref[first // 8 + step, pl.ds(row, 16), :] = low(
                        jnp.concatenate([upper[rows], lower[rows]], axis=0)
                    )

    even = parity(chip, slots)
    for own in range(2):
        for role in range(2):

            @pl.when((core == own) & (jnp.bitwise_xor(even, own) == role))
            def _(own=own, role=role):
                fill(role, own)


def node_grad_kernel(
    info_ref, dsum_ref, lhat_ref, ghat_ref, dnode_ref, dqkv_ref, sums_ref, backs_ref, w_ref,
    vec_ref,
    node_ref,
):
    width = lhat_ref.shape[1]
    sums = sums_ref[...]
    backs = backs_ref[...]
    total = norm_back(info_ref, dsum_ref, lhat_ref, sums, backs, 0, vec_ref[5:6, :], 1)
    total = total + norm_back(info_ref, dsum_ref, ghat_ref, sums, backs, 2, vec_ref[7:8, :], 2)
    for place, mat in enumerate((0, 1, 3, 4)):
        total = total + mm_back(dnode_ref[:, place * width : (place + 1) * width], w_ref[mat])
    for place in range(3):
        total = total + mm_back(dqkv_ref[:, place * width : (place + 1) * width], w_ref[5 + place])
    node_ref[...] = total


def edge_grad_kernel(info_ref, dedge_ref, w_ref, edge_ref):
    edge_ref[...] = mm_back(dedge_ref[...], w_ref[2])


def bias_rows(local_ref, attend_ref, inner_ref, wide_ref):
    width = attend_ref.shape[1]
    return jnp.concatenate(
        [
            local_ref[0:2, :],
            wide_ref[0:1, :width],
            wide_ref[0:1, width:],
            attend_ref[0:1, :],
            inner_ref[0:1, :width],
            inner_ref[0:1, width:],
            jnp.zeros((1, width), f32),
        ],
        axis=0,
    )


def last_kernel(
    info_ref, kept_ref, got_ref, local_ref, attend_ref, inner_ref, wide_ref, out_ref
):
    biases = bias_rows(local_ref, attend_ref, inner_ref, wide_ref)
    upper = low(biases).astype(f32)
    for slot, extra in enumerate((upper, biases - upper)):
        total = kept_ref[slot].astype(f32) + got_ref[slot].astype(f32)
        out_ref[slot] = low(jnp.concatenate([total, extra], axis=0))


def total_square(values):
    return jnp.sum(jnp.sum(values * values, axis=0, keepdims=True), axis=1, keepdims=True)


def pair_kernel(info_ref, mine_ref, got_ref, grad_ref, tail_ref):
    rows = grad_ref.shape[1]
    half = grad_ref.shape[2]
    mine = [mine_ref[slot].astype(f32) for slot in range(2)]
    got = [got_ref[slot].astype(f32) for slot in range(2)]
    grad = mine[0][:rows] + got[1][:rows]
    other = mine[1][:rows] + got[0][:rows]
    grad_ref[0] = grad[:, :half]
    grad_ref[1] = grad[:, half:]
    tail_ref[...] = (mine[0][rows:] + mine[1][rows:]) + (got[0][rows:] + got[1][rows:])
    tail_ref[7:8, :] = jnp.broadcast_to(total_square(grad) + total_square(other), (1, 2 * half))


def square_kernel(
    info_ref, kept_ref, got_ref, local_ref, attend_ref, inner_ref, wide_ref, grad_ref, tail_ref
):
    grad = kept_ref[...].astype(f32) + got_ref[...].astype(f32)
    half = grad.shape[1] // 2
    grad_ref[0] = grad[:, :half]
    grad_ref[1] = grad[:, half:]
    tail_ref[...] = bias_rows(local_ref, attend_ref, inner_ref, wide_ref)
    tail_ref[7:8, :] = jnp.broadcast_to(total_square(grad), (1, tail_ref.shape[1]))


def update_kernel(
    info_ref, grad_ref, tail_ref, sums_ref, tops_ref, backs_ref, w_ref, w1_ref, w2_ref, v_ref,
    v1_ref, v2_ref,
    new_w_ref, new_w1_ref, new_w2_ref, new_v_ref, new_v1_ref, new_v2_ref, norm_ref,
):
    tail = tail_ref[...]
    tops = tops_ref[...]
    backs = backs_ref[...]
    mean, rstd = norm_terms(tops, 0, sums_ref[4:5, :])
    grad_v = jnp.concatenate(
        [
            tail[0:5],
            backs[1:2],
            backs[0:1],
            backs[2:3],
            backs[0:1],
            tail[5:7],
            backs[3:4],
            (tops[3:4] - mean * tops[2:3]) * rstd,
            tops[2:3],
        ],
        axis=0,
    )
    square = jnp.sum(jnp.sum(grad_v * grad_v, axis=0, keepdims=True), axis=1, keepdims=True)
    norm = jnp.sqrt(tail[7:8, 0:1] + square)
    norm_ref[...] = norm
    factor = jnp.minimum(1.0, clip_limit / (norm + 1e-06))
    new_v_ref[...], new_v1_ref[...], new_v2_ref[...] = adamw(
        v_ref[...], factor * grad_v, v1_ref[...], v2_ref[...], rate_vecs, 0.0
    )
    mats, span = w_ref.shape
    _, rows, half = grad_ref.shape
    for piece in range(span // half):
        cols = slice(piece * half, (piece + 1) * half)
        if rows == mats:
            grad = grad_ref[piece]
        else:
            grad = grad_ref[piece % 2, pl.ds(piece // 2, mats, rows // mats), :]
        new_w_ref[:, cols], new_w1_ref[:, cols], new_w2_ref[:, cols] = adamw(
            w_ref[:, cols], factor * grad, w1_ref[:, cols], w2_ref[:, cols], rate_mats, decay_mats
        )


def rows_spec(rows, width, offset=0):
    if offset:
        return pl.BlockSpec((rows, width), lambda step, info: (step + info[0], 0))
    return pl.BlockSpec((rows, width), lambda step, info: (step, 0))


def whole_spec(shape):
    zeros = (0,) * len(shape)
    return pl.BlockSpec(shape, lambda step, info: zeros)


def call(kernel, steps, info, inputs, outputs, scratch=(), room=10, cost=5):
    in_specs = []
    arrays = []
    for array, spec in inputs:
        arrays.append(array)
        in_specs.append(whole_spec(array.shape) if spec is None else spec)
    out_specs = []
    out_shapes = []
    for shape, dtype, spec, *far in outputs:
        out_specs.append(whole_spec(shape) if spec is None else spec)
        out_shapes.append(pltpu.HBM(shape, dtype) if far else jax.ShapeDtypeStruct(shape, dtype))
    return pl.pallas_call(
        kernel,
        grid_spec=pltpu.PrefetchScalarGridSpec(
            num_scalar_prefetch=1,
            grid=(steps,),
            in_specs=in_specs,
            out_specs=out_specs,
            scratch_shapes=list(scratch),
        ),
        out_shape=out_shapes,
        compiler_params=pltpu.CompilerParams(
            dimension_semantics=("arbitrary",), vmem_limit_bytes=room * 1024 * 1024
        ),
        name=kernel.__name__,
        cost_estimate=pl.CostEstimate(
            flops=cost * 1000000000, bytes_accessed=cost * 1000000, transcendentals=0
        ),
    )(info, *arrays)


def swap_with(values, step, total):
    return lax.ppermute(values, axis_names, [(place, place ^ step) for place in range(total)])


def steps_of(total):
    return [1 << power for power in range(total.bit_length() - 1)]


def beside(start, transfer, info, work):
    info = lax.optimization_barrier((info, start))[0]
    return lax.optimization_barrier((transfer, work(info)))


def sum_steps(total):
    return [step | 1 for step in steps_of(total)]


def sum_small(values, total, info=None, works=()):
    results = []
    works = list(works)
    for step in sum_steps(total):
        other = swap_with(values, step, total)
        if works and step > 1:
            other, done = beside(values, other, info, works.pop(0))
            results.append(done)
        values = values + other
    return (values, results) if results else values


def swap_chips(values, number, total, straight=0):
    orders = chip_orders(total)
    pairs = []
    for place in range(total):
        step = orders[odd_bits(place & ~straight)][number]
        pairs.append((place, place ^ (step if step & straight else step | 1)))
    return lax.ppermute(values, axis_names, pairs)


def in_rows(total, width):
    return width * width // total == 8 * width


def cast_kernel(info_ref, w_ref, out_ref, hold_ref):
    mats, span = w_ref.shape
    half = hold_ref.shape[2]
    for piece in range(span // half):
        hold_ref[piece % 2, pl.ds(piece // 2, mats, 8), :] = w_ref[
            :, piece * half : (piece + 1) * half
        ]
    out_ref[0] = low(jnp.concatenate([hold_ref[0], hold_ref[1]], axis=1))


def gather_matrices(shard, info, total, width, work):
    mats = shard.shape[0]
    if not in_rows(total, width):
        gathered = lax.all_gather(low(shard), axis_names, axis=1, tiled=True)
        return (gathered.reshape(mats, width, width), work(info))
    held = call(
        cast_kernel,
        1,
        jnp.zeros((1,), jnp.int32),
        [(shard, None)],
        [((1, mats * 8, width), bf16, None)],
        [pltpu.VMEM((2, mats * 8, width // 2), f32)],
    )[0]
    for number in reversed(range(1, len(chip_orders(total)[0]))):
        held = jnp.concatenate([held, swap_chips(held, number, total)], axis=0)
    got = swap_chips(held, 0, total)
    other = swap_with(held, 1, total)

    def both(info):
        return (work(info), other)

    got, (done, other) = beside(held, got, info, both)
    far_other = swap_with(got, 1, total)
    matrices = call(
        assemble_kernel,
        1,
        info,
        [(held, None), (got, None), (other, None), (far_other, None)],
        [((mats, width, width), bf16, None)],
    )[0]
    return (matrices, done)


def scatter_plain(grads, total):
    place = lax.axis_index(axis_names)
    mats, width, _ = grads.shape
    bits = total.bit_length() - 1
    held = grads.reshape((mats,) + (2,) * bits + (width * width // total,))
    held = held.transpose(tuple(reversed(range(1, bits + 1))) + (0, bits + 1))
    for step in steps_of(total):
        mine = ((place & step) != 0).astype(jnp.int32)
        sent = lax.dynamic_index_in_dim(held, 1 - mine, 0, keepdims=False)
        kept = lax.dynamic_index_in_dim(held, mine, 0, keepdims=False)
        got = swap_with(sent, step, total)
        if step * 2 < total:
            held = low(kept.astype(f32) + got.astype(f32))
    return (kept, got)


def scatter_packed(kept, far_kept, sent, far_sent, total, info, works, biases):
    far_got = swap_with(far_sent, 1, total)
    got = swap_with(sent, 1, total)
    results = []
    rounds = len(chip_orders(total)[0])
    for number in range(rounds - 1):
        if number:
            half = kept.shape[0] // 2
            far_kept, far_got = kept[half:], got[half:]
            kept, got = kept[:half], got[:half]
        sent = low(far_kept.astype(f32) + far_got.astype(f32))
        kept = kept.astype(f32) + got.astype(f32)
        got = swap_chips(sent, number, total, total // 2)
        if number < len(works):
            got, done = beside(sent, got, info, works[number])
            results.append(done)
    mine = call(
        last_kernel,
        1,
        info,
        [(array, None) for array in (kept, got, *biases)],
        [((2, kept.shape[1] + 8, kept.shape[2]), bf16, None)],
    )[0]
    got = swap_chips(mine, rounds - 1, total, total // 2)
    grad_rows, tail = call(
        pair_kernel,
        1,
        info,
        [(mine, None), (got, None)],
        [((2, kept.shape[1], kept.shape[2] // 2), f32, None), ((8, kept.shape[2]), f32, None)],
    )
    for step in sum_steps(total)[:-1]:
        tail = tail + swap_with(tail, step, total)
    return (grad_rows, tail, results)


def adamw(params, gradient, moment_one, moment_two, rate, decay):
    first = beta_one * moment_one + (1.0 - beta_one) * gradient
    second = beta_two * moment_two + (1.0 - beta_two) * gradient * gradient
    first_hat = first / (1.0 - beta_one**STEP)
    second_hat = second / (1.0 - beta_two**STEP)
    updated = params - rate * (first_hat / (jnp.sqrt(second_hat) + adam_eps) + decay * params)
    return (updated, first, second)


def own_half(values, branch_index):
    half = values.shape[0] // 2
    return lax.dynamic_slice_in_dim(values, branch_index * half, half, 0)


def per_device(
    node_feats,
    edge_feats,
    cotangent,
    graph_ids,
    node_mask,
    edge_src,
    edge_dst,
    edge_mask,
    weights,
    weight_moment1,
    weight_moment2,
    vectors,
    vector_moment1,
    vector_moment2,
):
    total = lax.axis_size("rows") * lax.axis_size("branch")
    branch_index = lax.axis_index("branch")
    width = node_feats.shape[1]
    rows = node_feats.shape[0] // 2
    edges = edge_feats.shape[0] // 2
    blocks = rows // BLOCK
    group = math.gcd(blocks, GROUP)
    steps = blocks // group
    tall = group * BLOCK
    tall_edges = group * EB
    own_nodes = own_half(node_feats, branch_index)
    own_edges = own_half(edge_feats, branch_index)
    counts = jnp.sum(own_half(node_mask, branch_index).reshape(blocks, BLOCK), axis=1)
    info = jnp.concatenate(
        [(branch_index * steps)[None], counts, branch_index[None], lax.axis_index("rows")[None]]
    ).astype(jnp.int32)

    def by_step(values, slots):
        return own_half(values, branch_index).reshape(steps, group, slots)

    def step_spec(slots):
        return pl.BlockSpec((1, group, slots), lambda step, info: (step, 0, 0))

    edge_spec = rows_spec(tall_edges, width)
    node_spec = rows_spec(tall, width)
    def prep_work(info):
        return call(
            prep_kernel,
            steps,
            info,
            [
                (by_step(edge_src, EB), step_spec(EB)),
                (by_step(edge_dst, EB), step_spec(EB)),
                (by_step(edge_mask, EB), step_spec(EB)),
                (by_step(graph_ids, BLOCK), step_spec(BLOCK)),
            ],
            [
                ((edges, EB), bf16, edge_spec, True),
                ((edges, EB), bf16, edge_spec, True),
                ((rows, BLOCK), f32, rows_spec(tall, BLOCK)),
            ],
        )

    matrices, (hot, turned, bias) = gather_matrices(weights, info, total, width, prep_work)
    x_in = (own_nodes, node_spec)
    e_in = (own_edges, edge_spec)
    mats_in = (matrices, None)
    vec_in = (vectors, None)
    node_f32 = ((rows, width), f32, node_spec)
    node_bf = ((rows, width), bf16, node_spec)
    sums_out = ((8, width), f32, None)
    prob_spec = rows_spec(tall, HEADS * BLOCK)
    (
        local_out, gate_slope, recip, fall, opened, bend, b_source,
        global_out, queries, keyed, valued, attended, probs, sums_part,
    ) = call(
        forward_kernel,
        steps,
        info,
        [
            x_in,
            e_in,
            (bias, rows_spec(tall, BLOCK)),
            (hot, edge_spec),
            (turned, edge_spec),
            mats_in,
            vec_in,
        ],
        [
            node_f32,
            node_bf,
            node_bf,
            node_bf,
            ((edges, width), bf16, edge_spec),
            ((edges, width), bf16, edge_spec),
            ((edges, width), bf16, edge_spec),
            node_f32,
            node_bf,
            node_bf,
            node_bf,
            node_bf,
            ((rows, HEADS * BLOCK), bf16, prob_spec),
            sums_out,
        ],
        room=FRONT_ROOM,
    )
    sums = sum_small(sums_part, total)
    sums_in = (sums, None)
    cot_in = (cotangent, node_spec)
    wide_spec = rows_spec(tall, 2 * width)
    summed_low, hidden_low, hidden_slope, mixed, top_part = call(
        mix_kernel,
        steps,
        info,
        [(local_out, node_spec), (global_out, node_spec), cot_in, sums_in, mats_in, vec_in],
        [
            node_bf,
            ((rows, 2 * width), bf16, wide_spec),
            ((rows, 2 * width), bf16, wide_spec),
            node_f32,
            sums_out,
        ],
    )

    def hat_work(info):
        return call(
            hat_kernel,
            steps,
            info,
            [(local_out, node_spec), (global_out, node_spec), sums_in],
            [node_bf, node_bf],
        )

    tops, ((local_hat, global_hat),) = sum_small(top_part, total, info, [hat_work])
    d_mixed, d_hidden, d_summed, back_part = call(
        mix_back_kernel,
        steps,
        info,
        [
            (mixed, node_spec),
            (hidden_slope, wide_spec),
            cot_in,
            (local_hat, node_spec),
            (global_hat, node_spec),
            sums_in,
            (tops, None),
            mats_in,
            vec_in,
        ],
        [
            node_bf,
            ((rows, 2 * width), bf16, wide_spec),
            node_bf,
            sums_out,
        ],
    )

    def mat_out(tall_by, wide_by):
        return ((tall_by * width, wide_by * width), f32, None)

    def inner_work(info):
        return call(
            inner_grad_kernel,
            steps,
            info,
            [(summed_low, node_spec), (d_hidden, wide_spec)],
            [mat_out(1, 2), ((8, 2 * width), f32, None)],
        )

    def outer_work(info):
        return call(
            outer_grad_kernel,
            steps,
            info,
            [(hidden_low, wide_spec), (d_mixed, node_spec)],
            [mat_out(2, 1)],
        )[0]

    def layer_work(info):
        return call(
            layer_kernel,
            steps,
            info,
            [(mixed, node_spec), sums_in, (tops, None), vec_in],
            [node_bf],
        )[0]

    backs, ((inner_grads, inner_bias), outer_grads, layer_out) = sum_small(
        back_part, total, info, [inner_work, outer_work, layer_work]
    )
    backs_in = (backs, None)
    dsum_in = (d_summed, node_spec)
    dnode_spec = rows_spec(tall, 4 * width)
    dqkv_spec = rows_spec(tall, 3 * width)
    slots = total // 2
    packed = in_rows(total, width)
    grad_outs = [((MATS, width, width), bf16, None)]
    if packed:
        grad_outs = [((slots // 2, MATS * 8, width), bf16, None)] * 4
    d_node, d_edge, local_bias, d_qkv, d_low, attend_bias = call(
        back_kernel,
        steps,
        info,
        [
            dsum_in,
            (local_hat, node_spec),
            (gate_slope, node_spec),
            (recip, node_spec),
            (fall, node_spec),
            (opened, edge_spec),
            (bend, edge_spec),
            (b_source, edge_spec),
            (hot, edge_spec),
            (turned, edge_spec),
            (global_hat, node_spec),
            (queries, node_spec),
            (keyed, node_spec),
            (valued, node_spec),
            (probs, prob_spec),
            sums_in,
            backs_in,
            mats_in,
            vec_in,
        ],
        [
            ((rows, 4 * width), bf16, dnode_spec),
            ((edges, width), bf16, edge_spec),
            sums_out,
            ((rows, 3 * width), bf16, dqkv_spec),
            node_bf,
            sums_out,
        ],
        [pltpu.VMEM((tall, HEADS * BLOCK), bf16)],
        room=BACK_ROOM,
    )
    *grads, wide_bias = call(
        branch_grad_kernel,
        1,
        info,
        [
            (own_nodes, None),
            (own_edges, None),
            (attended, None),
            (d_node, None),
            (d_edge, None),
            (d_qkv, None),
            (d_low, None),
            (inner_grads, None),
            (outer_grads, None),
        ],
        grad_outs + [((8, 2 * width), f32, None)],
        [
            pltpu.VMEM((width, 4 * width), f32),
            pltpu.VMEM((width, 3 * width), f32),
            pltpu.VMEM((width, width), f32),
            pltpu.VMEM((width, width), f32),
        ],
    )

    def node_work(info):
        return call(
            node_grad_kernel,
            steps,
            info,
            [
                dsum_in,
                (local_hat, node_spec),
                (global_hat, node_spec),
                (d_node, dnode_spec),
                (d_qkv, dqkv_spec),
                sums_in,
                backs_in,
                mats_in,
                vec_in,
            ],
            [node_f32],
        )[0]

    def edge_work(info):
        return call(
            edge_grad_kernel,
            steps,
            info,
            [(d_edge, edge_spec), mats_in],
            [((edges, width), f32, edge_spec)],
        )[0]

    biases = (local_bias, attend_bias, inner_bias, wide_bias)
    if packed:
        grad_rows, tail, (node_grad, edge_grad) = scatter_packed(
            *grads, total, info, [node_work, edge_work], biases
        )
    else:
        grad_shard = scatter_plain(grads[0], total)
        node_grad, edge_grad = node_work(info), edge_work(info)
        grad_rows, tail_part = call(
            square_kernel,
            1,
            info,
            [(array, None) for array in (*grad_shard, *biases)],
            [
                ((2, grad_shard[0].shape[0], grad_shard[0].shape[1] // 2), f32, None),
                sums_out,
            ],
        )
        tail = sum_small(tail_part, total)
    like_mats = (weights.shape, f32, None)
    like_vecs = (vectors.shape, f32, None)
    new_weights, first_w, second_w, new_vectors, first_v, second_v, norm = call(
        update_kernel,
        1,
        info,
        [
            (array, None)
            for array in (
                grad_rows, tail, sums, tops, backs, weights, weight_moment1, weight_moment2,
                vectors, vector_moment1, vector_moment2,
            )
        ],
        [like_mats] * 3 + [like_vecs] * 3 + [((1, 1), f32, None)],
    )
    grad_norm = norm.reshape(())
    return (
        layer_out,
        node_grad,
        edge_grad,
        new_weights,
        first_w,
        second_w,
        new_vectors,
        first_v,
        second_v,
        grad_norm,
    )


def solution(mesh):
    in_specs = (
        P("rows", None),
        P("rows", None),
        P(("rows", "branch"), None),
        P("rows"),
        P("rows"),
        P("rows"),
        P("rows"),
        P("rows"),
        P(None, ("rows", "branch")),
        P(None, ("rows", "branch")),
        P(None, ("rows", "branch")),
        P(),
        P(),
        P(),
    )
    out_specs = (
        P(("rows", "branch"), None),
        P(("rows", "branch"), None),
        P(("rows", "branch"), None),
        P(None, ("rows", "branch")),
        P(None, ("rows", "branch")),
        P(None, ("rows", "branch")),
        P(),
        P(),
        P(),
        P(),
    )
    return jax.shard_map(
        per_device, mesh=mesh, in_specs=in_specs, out_specs=out_specs, check_vma=False
    )
```
